128 devices in a mesh: section: 4 (over y), seq: 32 (over z, x, core).
Axes of the slice: x: 4, y: 4, z: 4, core: 2. Of those that a mesh axis runs over, the one named last changes fastest.
Arguments:
- stream: bfloat16 [4, 4096, 4096], P('section', 'seq'), may hold values from -4 to 4
- queries: bfloat16 [4, 4096, 4096], P('section', 'seq')
- span_kv: bfloat16 [4, 2, 4096, 512], P('section', None, 'seq')
- cache_kv: bfloat16 [4, 2, 4096, 512], P('section', None, 'seq'), may hold values from -6 to 6
- cache_len: int32 [32], replicated, may hold values from 48 to 80, as said below
- context_start: int32 [1], replicated, may hold values from 1 to 4096
- block_table: int32 [32, 32], replicated, may hold values from 0 to 1, as said below
Outputs:
- handed: bfloat16 [4, 4096, 4096], P('section', 'seq')
The draws below stay inside these ranges and needn't reach their ends.
Inputs may be any that keep to these rules, and one draw needn't show every extreme that they name: `cache_len`: some index holds exactly 80 live slots. `block_table`: the diagonal is 1 and every entry above it is 0.
All inputs are finite; a program needn't handle non-finite values.
Results may differ from the reference program's by a relative error of at most 0.006.
Values may be sent and summed in bfloat16 or wider, within the bound.
No kernel may reach another device: no remote copies, remote signals or barrier semaphores. Data moves between devices by JAX's collectives and lax.ppermute only.
A program may use at most 64 MiB of HBM per device.

```python
import math
import jax
import jax.numpy as jnp
from jax import lax

HEAD_DIM = 128
HEADS = 32
KV_HEADS = 4
TOK_DEV = 128
CACHE_DEV = 128
GROUP = 8
LIVE_MAX = 80
TOKENS = 4096
CACHE = 4096
N_SECTION = 4
N_SEQ = 32


def shaped_pairs(key):
    base = jax.random.normal(jax.random.fold_in(key, 11), (N_SECTION, 2, TOKENS, KV_HEADS * HEAD_DIM), jnp.float32)
    return base


def draw_span_kv(key, part):
    return shaped_pairs(key).astype(jnp.bfloat16)


def draw_queries(key, part):
    noise = 2.0 * jax.random.normal(jax.random.fold_in(key, 12), (N_SECTION, TOKENS, HEADS * HEAD_DIM), jnp.float32)
    return noise.astype(jnp.bfloat16)


def draw_cache_len(key, part):
    counts = jax.random.randint(jax.random.fold_in(key, 21), (N_SEQ,), 3 * LIVE_MAX // 5, LIVE_MAX + 1)
    fullest = jax.random.randint(jax.random.fold_in(key, 22), (), 0, N_SEQ)
    return jnp.where(jnp.arange(N_SEQ) == fullest, LIVE_MAX, counts).astype(jnp.int32)


def draw_block_table(key, part):
    coins = jax.random.randint(jax.random.fold_in(key, 31), (N_SEQ, N_SEQ), 0, 4)
    row_ids = jnp.arange(N_SEQ)[:, None]
    col_ids = jnp.arange(N_SEQ)[None, :]
    lower = jnp.where(coins > 0, 1, 0)
    return jnp.where(col_ids < row_ids, lower, jnp.where(col_ids == row_ids, 1, 0)).astype(jnp.int32)


def level_of(key, shape, shards, smallest, high):
    gain = 1.0
    for position, blocks in shards:
        draws = jax.random.uniform(jax.random.fold_in(jax.random.fold_in(key, 6), position), (blocks,), jnp.float32, smallest / len(shards), high / len(shards))
        gain = gain * jnp.repeat(jnp.exp(draws), shape[position] // blocks).reshape((-1,) + (1,) * (len(shape) - 1 - position))
    return gain


def bell_draw(own_key, extent, width, most, split=(), held_as=jnp.bfloat16):
    array = width * jax.random.normal(own_key, extent, jnp.float32)
    if split:
        array = array * level_of(own_key, extent, split, -0.22, 0.18)
    return jnp.clip(array, -most, most).astype(held_as)


def setup_inputs(seed: int = 0) -> dict:
    streams_of = jax.random.split(jax.random.key(seed), 8)
    return {
        "stream": bell_draw(streams_of[0], (N_SECTION, TOKENS, HEADS * HEAD_DIM), 0.5, 4.0, ((0, 4), (1, 32))),
        "queries": draw_queries(jax.random.fold_in(streams_of[7], 71), 0),
        "span_kv": draw_span_kv(jax.random.fold_in(streams_of[7], 71), 0),
        "cache_kv": bell_draw(streams_of[3], (N_SECTION, 2, CACHE, KV_HEADS * HEAD_DIM), 1.0, 6.0, ((0, 4), (2, 32))),
        "cache_len": draw_cache_len(jax.random.fold_in(streams_of[7], 71), 0),
        "context_start": jax.random.randint(streams_of[5], (1,), 1, CACHE + 1).astype(jnp.int32),
        "block_table": draw_block_table(jax.random.fold_in(streams_of[7], 71), 0),
    }


def reference(stream, queries, span_kv, cache_kv, cache_len, context_start, block_table):
    score_scale = 1.0 / math.sqrt(HEAD_DIM)
    positions = jnp.arange(CACHE, dtype=jnp.int32)
    owner = positions // CACHE_DEV
    slot_index = positions % CACHE_DEV
    cache_open = (slot_index < cache_len[owner]) & (positions >= CACHE - context_start[0])
    key_tokens = jnp.arange(TOKENS, dtype=jnp.int32)
    outputs = []
    for layer in range(N_SECTION):
        all_keys = jnp.concatenate([cache_kv[layer, 0], span_kv[layer, 0]], 0).astype(jnp.float32)
        all_keys = all_keys.reshape(CACHE + TOKENS, KV_HEADS, HEAD_DIM)
        all_values = jnp.concatenate([cache_kv[layer, 1], span_kv[layer, 1]], 0).astype(jnp.float32)
        all_values = all_values.reshape(CACHE + TOKENS, KV_HEADS, HEAD_DIM)
        layer_queries = queries[layer]

        def one_block(block):
            rows = lax.dynamic_slice_in_dim(layer_queries, block * TOK_DEV, TOK_DEV, 0).astype(jnp.float32)
            rows = rows.reshape(TOK_DEV, KV_HEADS, GROUP, HEAD_DIM)
            scores = jnp.einsum('tkgd,nkd->ktgn', rows, all_keys, precision=lax.Precision.HIGHEST) * score_scale
            query_pos = block * TOK_DEV + jnp.arange(TOK_DEV, dtype=jnp.int32)
            table_row = block_table[block]
            span_open = (key_tokens[None, :] <= query_pos[:, None]) & (table_row[key_tokens // TOK_DEV][None, :] == 1)
            allowed = jnp.concatenate([jnp.broadcast_to(cache_open[None, :], (TOK_DEV, CACHE)), span_open], 1)
            wide_mask = allowed[None, :, None, :]
            row_top = lax.optimization_barrier(jnp.max(jnp.where(wide_mask, scores, -jnp.inf), -1, keepdims=True))
            weights = jnp.where(wide_mask, jnp.exp(scores - row_top), 0.0)
            row_total = lax.optimization_barrier(jnp.sum(weights, -1))
            rounded = lax.optimization_barrier(weights.astype(jnp.bfloat16)).astype(jnp.float32)
            mixed = jnp.einsum('ktgn,nkd->ktgd', rounded, all_values, precision=lax.Precision.HIGHEST)
            mixed = mixed / row_total[..., None]
            return mixed.transpose(1, 0, 2, 3).reshape(TOK_DEV, HEADS * HEAD_DIM).astype(jnp.bfloat16)
        attn = lax.map(one_block, jnp.arange(N_SEQ, dtype=jnp.int32)).reshape(TOKENS, HEADS * HEAD_DIM)
        layer_out = (stream[layer].astype(jnp.float32) + attn.astype(jnp.float32)).astype(jnp.bfloat16)
        outputs.append(layer_out)
    return jnp.roll(jnp.stack(outputs), 1, axis=0)
```

```python
import functools
import math

import jax
import jax.numpy as jnp
from jax import lax
from jax.experimental import pallas as pl
from jax.experimental.pallas import tpu as pltpu
from jax.sharding import PartitionSpec as P

DIM = 128
GROUP = 8
TOK = 128
SLOTS = 128
LIVE = 80
SHARDS = 32
CACHE = SLOTS * SHARDS
ROWS = GROUP * TOK
PER = 4
SPAN_ROWS = PER * 2 * TOK
CACHE_ROWS = PER * 2 * LIVE
CHUNK = SPAN_ROWS + CACHE_ROWS
BLOCK = 128
TILE_BLOCKS = 2
OFFSETS = (0, -1, 1, 2)
TO_LOG2 = math.log2(math.e) / math.sqrt(DIM)
LEAST_TOTAL, MOST_TOTAL = 1e-12, 1e30
LEAST_MIXED, MOST_MIXED = 1e-20, 1e37
AXES = ("section", "seq")


def moved(value, rule):
    pairs = []
    for y in range(4):
        for z in range(4):
            for x in range(4):
                for c in range(2):
                    ty, tz, tx, tc = rule(y, z, x, c)
                    source = y * 32 + (z * 4 + x) * 2 + c
                    target = (ty % 4) * 32 + ((tz % 4) * 4 + tx % 4) * 2 + tc
                    pairs.append((source, target))
    return lax.ppermute(value, AXES, pairs)


def swapped(value):
    return moved(value, lambda y, z, x, c: (y, z, x, 1 - c))


def up(value):
    return moved(value, lambda y, z, x, c: (y + 1, z, x, c))


def up_swapped(value):
    return moved(value, lambda y, z, x, c: (y + 1, z, x, 1 - c))


def first_ring(value, k):
    return moved(value, lambda y, z, x, c: (y, z, x + k, c) if c == 0 else (y, z + k, x, c))


def second_ring(value, k):
    return moved(value, lambda y, z, x, c: (y, z + k, x, c) if c == 0 else (y, z, x + k, c))


def chip_of(place, row, col):
    z, x, c = place
    dz = jnp.where(c == 0, row, col)
    dx = jnp.where(c == 0, col, row)
    return ((z + dz + 4) % 4) * 4 + (x + dx + 4) % 4


def stage_kernel(rows_of, has_carry, last, *refs):
    refs = list(refs)
    place_ref, table_ref, len_ref, start_ref = refs[:4]
    refs = refs[4:]
    q_refs, refs = refs[:2], refs[2:]
    chunk_refs, refs = refs[: 2 * len(rows_of)], refs[2 * len(rows_of) :]
    carry_ref = None
    if has_carry:
        carry_ref, refs = refs[0], refs[1:]
    if last:
        own_ref, other_ref, bad_ref = refs[:3]
        refs = refs[3:]
        total_ref, refs = refs[0], refs[1:]
    else:
        total_ref, refs = refs[0], refs[1:]
    keys, values, queries, todo = refs
    count = len(rows_of)
    place = (place_ref[0], place_ref[1], place_ref[2])
    core = place[2]
    chip = place[0] * 4 + place[1]
    first_open = CACHE - start_ref[0]

    for n in range(count):
        base = n * CHUNK
        keys[base : base + CHUNK, :] = chunk_refs[2 * n][...]
        value_ref = chunk_refs[2 * n + 1]
        values[base : base + SPAN_ROWS, :DIM] = value_ref[:SPAN_ROWS, :]
        values[base : base + SPAN_ROWS, DIM:] = jnp.ones((SPAN_ROWS, DIM), jnp.bfloat16)
        for k in range(PER):
            there = chip_of(place, rows_of[n], OFFSETS[k])
            for e in range(2):
                shard = 2 * there + (core if e == 0 else 1 - core)
                low = first_open - shard * SLOTS
                slot = lax.broadcasted_iota(jnp.int32, (LIVE, DIM), 0)
                live = (slot >= low) & (slot < len_ref[shard])
                at = SPAN_ROWS + (2 * k + e) * LIVE
                piece = value_ref[at : at + LIVE, :].astype(jnp.float32)
                values[base + at : base + at + LIVE, :DIM] = jnp.where(live, piece, 0.0).astype(jnp.bfloat16)
                values[base + at : base + at + LIVE, DIM:] = jnp.where(live, 1.0, 0.0).astype(jnp.bfloat16)
    spare = count * CHUNK
    keys[spare : spare + BLOCK, :] = jnp.zeros((BLOCK, DIM), jnp.bfloat16)
    values[spare : spare + BLOCK, :] = jnp.zeros((BLOCK, 2 * DIM), jnp.bfloat16)

    worst_low = None
    for q in range(2):
        mine = 2 * chip + (core if q == 0 else 1 - core)
        for h in range(GROUP):
            queries[h * TOK : (h + 1) * TOK, :] = q_refs[q][:, h * DIM : (h + 1) * DIM]

        filled = jnp.int32(0)
        for n in range(count):
            for k in range(PER):
                there = chip_of(place, rows_of[n], OFFSETS[k])
                for e in range(2):
                    shard = 2 * there + (core if e == 0 else 1 - core)
                    wanted = (shard < mine) & (table_ref[mine, shard] == 1)
                    todo[filled] = n * CHUNK + (2 * k + e) * TOK
                    filled = filled + jnp.where(wanted, 1, 0)
            seen = []
            for k in range(PER):
                there = chip_of(place, rows_of[n], OFFSETS[k])
                for e in range(2):
                    shard = 2 * there + (core if e == 0 else 1 - core)
                    seen.append(shard * SLOTS + len_ref[shard] > first_open)
            for b in range(CACHE_ROWS // BLOCK):
                wanted = functools.reduce(
                    jnp.logical_or, seen[b * BLOCK // LIVE : ((b + 1) * BLOCK - 1) // LIVE + 1]
                )
                todo[filled] = n * CHUNK + SPAN_ROWS + b * BLOCK
                filled = filled + jnp.where(wanted, 1, 0)
        for b in range(TILE_BLOCKS - 1):
            todo[filled + b] = spare

        def weights_of(rows):
            scores = lax.dot_general(
                queries[...], rows, (((1,), (1,)), ((), ())), preferred_element_type=jnp.float32
            )
            return jnp.exp2(scores * TO_LOG2)

        def mix(weights, rows):
            return jnp.dot(weights.astype(jnp.bfloat16), rows, preferred_element_type=jnp.float32)

        if rows_of[0] == 0:
            at = q * TOK
            token = lax.broadcasted_iota(jnp.int32, (TOK, TOK), 0)
            key = lax.broadcasted_iota(jnp.int32, (TOK, TOK), 1)
            weights = weights_of(keys[at : at + TOK, :]).reshape(GROUP, TOK, TOK)
            weights = jnp.where((key <= token)[None], weights, 0.0).reshape(ROWS, TOK)
            part = mix(weights, values[at : at + TOK, :])
            if has_carry:
                part = part + carry_ref[q]
            total_ref[q] = part
        else:
            total_ref[q] = carry_ref[q]

        def tile(step, _):
            spots = [pl.multiple_of(todo[step * TILE_BLOCKS + b], BLOCK) for b in range(TILE_BLOCKS)]
            key_rows = jnp.concatenate([keys[pl.ds(s, BLOCK), :] for s in spots], 0)
            value_rows = jnp.concatenate([values[pl.ds(s, BLOCK), :] for s in spots], 0)
            total_ref[q] += mix(weights_of(key_rows), value_rows)
            return 0

        lax.fori_loop(0, (filled + TILE_BLOCKS - 1) // TILE_BLOCKS, tile, 0)

        if last:
            out_ref = own_ref if q == 0 else other_ref
            for h in range(GROUP):
                mixed = total_ref[q, h * TOK : (h + 1) * TOK, :DIM]
                total = total_ref[q, h * TOK : (h + 1) * TOK, DIM:]
                out_ref[:, h * DIM : (h + 1) * DIM] = (mixed / total).astype(jnp.bfloat16)
                if worst_low is None:
                    worst_low, worst_high, largest = total, total, jnp.abs(mixed)
                    strange = jnp.where((total > 0.0) & (jnp.abs(mixed) < MOST_MIXED), 0.0, 1.0)
                else:
                    worst_low = jnp.minimum(worst_low, total)
                    worst_high = jnp.maximum(worst_high, total)
                    largest = jnp.maximum(largest, jnp.abs(mixed))
                    good = (total > 0.0) & (jnp.abs(mixed) < MOST_MIXED)
                    strange = jnp.maximum(strange, jnp.where(good, 0.0, 1.0))
    if last:
        fine = (
            (jnp.max(strange) == 0.0)
            & (jnp.min(worst_low) >= LEAST_TOTAL)
            & (jnp.max(worst_high) <= MOST_TOTAL)
            & (jnp.max(largest) >= LEAST_MIXED)
        )
        bad_ref[0] = jnp.where(fine, 0, 1)


def stage(rows_of, last, scalars, queries, chunks, carry=None):
    smem = pl.BlockSpec(memory_space=pltpu.SMEM)
    vmem = pl.BlockSpec(memory_space=pltpu.VMEM)
    operands = list(scalars) + list(queries)
    for k, v in chunks:
        operands += [k, v]
    if carry is not None:
        operands.append(carry)
    specs = [smem] * 4 + [vmem] * (len(operands) - 4)
    count = len(rows_of)
    total = ((2, ROWS, 2 * DIM), jnp.float32)
    scratch = [
        pltpu.VMEM((count * CHUNK + BLOCK, DIM), jnp.bfloat16),
        pltpu.VMEM((count * CHUNK + BLOCK, 2 * DIM), jnp.bfloat16),
        pltpu.VMEM((ROWS, DIM), jnp.bfloat16),
        pltpu.SMEM((count * (PER * 2 + CACHE_ROWS // BLOCK) + TILE_BLOCKS,), jnp.int32),
    ]
    if last:
        out_shape = (
            jax.ShapeDtypeStruct((TOK, GROUP * DIM), jnp.bfloat16),
            jax.ShapeDtypeStruct((TOK, GROUP * DIM), jnp.bfloat16),
            jax.ShapeDtypeStruct((1,), jnp.int32),
        )
        out_specs = (vmem, vmem, smem)
        scratch = [pltpu.VMEM(*total)] + scratch
    else:
        out_shape = jax.ShapeDtypeStruct(*total)
        out_specs = vmem
    flops = count * 2 * ROWS * CHUNK * DIM * 6
    return pl.pallas_call(
        functools.partial(stage_kernel, tuple(rows_of), carry is not None, last),
        out_shape=out_shape,
        in_specs=specs,
        out_specs=out_specs,
        scratch_shapes=scratch,
        compiler_params=pltpu.CompilerParams(vmem_limit_bytes=40 * 1024 * 1024),
        cost_estimate=pl.CostEstimate(
            flops=flops, bytes_accessed=count * CHUNK * DIM * 4, transcendentals=count * 2 * ROWS * CHUNK
        ),
        name="stage_" + "_".join(str(r % 4) for r in rows_of),
    )(*operands)


def slow(scalars, queries, chunks):
    place, table, lengths, start = scalars
    spot = (place[0], place[1], place[2])
    core = spot[2]
    chip = spot[0] * 4 + spot[1]
    results = []
    for q in range(2):
        mine = 2 * chip + (core if q == 0 else 1 - core)
        token = mine * TOK + jnp.arange(TOK, dtype=jnp.int32)
        rows = queries[q].reshape(TOK, GROUP, DIM)
        top = jnp.full((GROUP, TOK), -jnp.inf, jnp.float32)
        total = jnp.zeros((GROUP, TOK), jnp.float32)
        mixed = jnp.zeros((GROUP, TOK, DIM), jnp.float32)
        for row in OFFSETS:
            k, v = chunks[row]
            shard = jnp.stack(
                [
                    2 * chip_of(spot, row, col) + (core if e == 0 else 1 - core)
                    for col in OFFSETS
                    for e in range(2)
                ]
            )
            key = (shard[:, None] * TOK + jnp.arange(TOK)[None]).reshape(-1)
            listed = jnp.repeat(table[mine][shard] == 1, TOK)
            span_open = (key[None] <= token[:, None]) & listed[None]
            slot = jnp.arange(LIVE)[None]
            live = (slot < lengths[shard][:, None]) & (shard[:, None] * SLOTS + slot >= CACHE - start[0])
            open_all = jnp.concatenate(
                [span_open, jnp.broadcast_to(live.reshape(1, -1), (TOK, CACHE_ROWS))], 1
            )[None]
            scores = jnp.einsum("tgd,nd->gtn", rows, k, preferred_element_type=jnp.float32)
            scores = jnp.where(open_all, scores * (1.0 / math.sqrt(DIM)), -jnp.inf)
            new_top = jnp.maximum(top, jnp.max(scores, -1))
            shift = jnp.where(new_top == -jnp.inf, 0.0, new_top)
            weights = jnp.where(open_all, jnp.exp(scores - shift[..., None]), 0.0)
            factor = jnp.exp(top - shift)
            total = total * factor + jnp.sum(weights, -1)
            mixed = mixed * factor[..., None] + jnp.einsum(
                "gtn,nd->gtd", weights.astype(jnp.bfloat16), v, preferred_element_type=jnp.float32
            )
            top = new_top
        out = (mixed / total[..., None]).astype(jnp.bfloat16)
        results.append(out.transpose(1, 0, 2).reshape(TOK, GROUP * DIM))
    return tuple(results)


def guarded(scalars, queries, chunks, own, other, bad):
    return lax.cond(
        bad[0] == 0, lambda: (own, other), lambda: slow(scalars, queries, chunks)
    )


def joined(units):
    spans = [u[:, : 2 * TOK] for u in units]
    caches = [u[:, 2 * TOK :] for u in units]
    return jnp.concatenate(spans + caches, 1)


def paired(own, other):
    return jnp.concatenate([own[:, :TOK], other[:, :TOK], own[:, TOK:], other[:, TOK:]], 1)


def gathered(unit):
    row = joined([unit] + [first_ring(unit, -k) for k in OFFSETS[1:]])
    before, after = second_ring(row, 1), second_ring(row, -1)
    far_k, far_v = second_ring(before[0], 1), second_ring(after[1], -1)
    return {
        0: (row[0], row[1]),
        -1: (before[0], before[1]),
        1: (after[0], after[1]),
        2: (far_k, far_v),
    }


def shards(stream, queries, span_kv, cache_kv, cache_len, context_start, block_table):
    seq = lax.axis_index("seq")
    core = seq % 2
    place = jnp.stack([seq // 8, (seq // 2) % 4, core]).astype(jnp.int32)
    scalars = (place, block_table, cache_len, context_start)

    def pair_of(head):
        span = lax.dynamic_slice_in_dim(span_kv[0], head * DIM, DIM, 2)
        cache = lax.dynamic_slice_in_dim(cache_kv[0, :, :LIVE], head * DIM, DIM, 2)
        return jnp.concatenate([span, cache], 1)

    def query_of(head):
        return lax.dynamic_slice_in_dim(queries[0], head * GROUP * DIM, GROUP * DIM, 1)

    near_unit = paired(pair_of(core), swapped(pair_of(1 - core)))
    late_unit = paired(up(pair_of(2 + core)), up_swapped(pair_of(3 - core)))
    near_q = (query_of(core), swapped(query_of(1 - core)))
    late_q = (up(query_of(2 + core)), up_swapped(query_of(3 - core)))
    half = GROUP * DIM * 2
    late_stream = up(stream[0, :, half:])

    near = gathered(near_unit)
    late = gathered(late_unit)

    own, other, bad = stage(OFFSETS, True, scalars, near_q, [near[r] for r in OFFSETS])
    own, other = guarded(scalars, near_q, near, own, other, bad)

    def added(own, other, base):
        received = swapped(other)
        both = jnp.where(
            core == 0, jnp.concatenate([own, received], 1), jnp.concatenate([received, own], 1)
        )
        return (base.astype(jnp.float32) + both.astype(jnp.float32)).astype(jnp.bfloat16)

    near_out = up(added(own, other, stream[0, :, :half]))

    carry = stage((0,), False, scalars, late_q, [late[0]])
    carry = stage((-1, 1), False, scalars, late_q, [late[-1], late[1]], carry)
    own, other, bad = stage((2,), True, scalars, late_q, [late[2]], carry)
    own, other = guarded(scalars, late_q, late, own, other, bad)
    late_out = added(own, other, late_stream)
    return jnp.concatenate([near_out, late_out], 1)[None]


def solution(mesh):
    return jax.shard_map(
        shards,
        mesh=mesh,
        in_specs=(
            P("section", "seq", None),
            P("section", "seq", None),
            P("section", None, "seq", None),
            P("section", None, "seq", None),
            P(),
            P(),
            P(),
        ),
        out_specs=P("section", "seq", None),
        check_vma=False,
    )
```

```python
import functools
import math

import jax
import jax.numpy as jnp
from jax import lax
from jax.experimental import pallas as pl
from jax.experimental.pallas import tpu as pltpu
from jax.sharding import PartitionSpec as P

DIM = 128
GROUP = 8
TOK = 128
SLOTS = 128
LIVE = 80
SHARDS = 32
CACHE = SLOTS * SHARDS
ROWS = GROUP * TOK
PER = 4
SPAN_ROWS = PER * 2 * TOK
CACHE_ROWS = PER * 2 * LIVE
CHUNK = SPAN_ROWS + CACHE_ROWS
BLOCK = 128
TILE_BLOCKS = 8
SUB = 256
OFFSETS = (0, -1, 1, 2)
TO_LOG2 = math.log2(math.e) / math.sqrt(DIM)
LEAST_TOTAL, MOST_TOTAL = 1e-12, 1e30
LEAST_MIXED, MOST_MIXED = 1e-20, 1e37
AXES = ("section", "seq")


def moved(value, rule):
    pairs = []
    for y in range(4):
        for z in range(4):
            for x in range(4):
                for c in range(2):
                    ty, tz, tx, tc = rule(y, z, x, c)
                    source = y * 32 + (z * 4 + x) * 2 + c
                    target = (ty % 4) * 32 + ((tz % 4) * 4 + tx % 4) * 2 + tc
                    pairs.append((source, target))
    return lax.ppermute(value, AXES, pairs)


def swapped(value):
    return moved(value, lambda y, z, x, c: (y, z, x, 1 - c))


def up(value):
    return moved(value, lambda y, z, x, c: (y + 1, z, x, c))


def up_swapped(value):
    return moved(value, lambda y, z, x, c: (y + 1, z, x, 1 - c))


def first_ring(value, k):
    return moved(value, lambda y, z, x, c: (y, z, x + k, c) if c == 0 else (y, z + k, x, c))


def second_ring(value, k):
    return moved(value, lambda y, z, x, c: (y, z + k, x, c) if c == 0 else (y, z, x + k, c))


def chip_of(place, row, col):
    z, x, c = place
    dz = jnp.where(c == 0, row, col)
    dx = jnp.where(c == 0, col, row)
    return ((z + dz + 4) % 4) * 4 + (x + dx + 4) % 4


def stage_kernel(rows_of, pieces, has_carry, last, idle, *refs):
    refs = list(refs)
    place_ref, table_ref, len_ref, start_ref = refs[:4]
    q_refs, refs = refs[4:6], refs[6:]
    chunk_refs = []
    for part in pieces:
        chunk_refs.append(refs[: len(part)])
        refs = refs[len(part) :]
    carry_ref = None
    if has_carry:
        carry_ref, refs = refs[0], refs[1:]
    all_refs = []
    if last:
        for part in last:
            all_refs.append(refs[: len(part)])
            refs = refs[len(part) :]
    refs = refs[idle:]
    if last:
        out_refs, refs = refs[:2], refs[2:]
    total_ref, keys, values, queries, todo = refs[:5]
    count = len(rows_of)
    place = (place_ref[0], place_ref[1], place_ref[2])
    core = place[2]
    chip = place[0] * 4 + place[1]
    first_open = CACHE - start_ref[0]

    def shard_at(row, k, e):
        return 2 * chip_of(place, row, OFFSETS[k]) + (core if e == 0 else 1 - core)

    for n in range(count):
        base = n * CHUNK
        values[base : base + SPAN_ROWS, DIM:] = jnp.ones((SPAN_ROWS, DIM), jnp.bfloat16)
        k = 0
        for ref, units in zip(chunk_refs[n], pieces[n]):
            for u in range(units):
                for e in range(2):
                    spot = base + (2 * k + e) * TOK
                    keys[spot : spot + TOK, :] = ref[u, e, 0, :TOK, :]
                    values[spot : spot + TOK, :DIM] = ref[u, e, 1, :TOK, :]
                    shard = shard_at(rows_of[n], k, e)
                    low = first_open - shard * SLOTS
                    slot = lax.broadcasted_iota(jnp.int32, (LIVE, DIM), 0)
                    live = (slot >= low) & (slot < len_ref[shard])
                    spot = base + SPAN_ROWS + (2 * k + e) * LIVE
                    keys[spot : spot + LIVE, :] = ref[u, e, 0, TOK:, :]
                    piece = ref[u, e, 1, TOK:, :].astype(jnp.float32)
                    values[spot : spot + LIVE, :DIM] = jnp.where(live, piece, 0.0).astype(jnp.bfloat16)
                    values[spot : spot + LIVE, DIM:] = jnp.where(live, 1.0, 0.0).astype(jnp.bfloat16)
                k += 1
    spare = count * CHUNK
    keys[spare : spare + BLOCK, :] = jnp.zeros((BLOCK, DIM), jnp.bfloat16)
    values[spare : spare + BLOCK, :] = jnp.zeros((BLOCK, 2 * DIM), jnp.bfloat16)

    for q in range(2):
        mine = 2 * chip + (core if q == 0 else 1 - core)
        for h in range(GROUP):
            queries[h * TOK : (h + 1) * TOK, :] = q_refs[q][:, h * DIM : (h + 1) * DIM]

        filled = jnp.int32(0)
        for n in range(count):
            seen = []
            for k in range(PER):
                for e in range(2):
                    shard = shard_at(rows_of[n], k, e)
                    wanted = (shard < mine) & (table_ref[mine, shard] == 1)
                    todo[filled] = n * CHUNK + (2 * k + e) * TOK
                    filled = filled + jnp.where(wanted, 1, 0)
                    seen.append(shard * SLOTS + len_ref[shard] > first_open)
            for b in range(CACHE_ROWS // BLOCK):
                wanted = functools.reduce(
                    jnp.logical_or, seen[b * BLOCK // LIVE : ((b + 1) * BLOCK - 1) // LIVE + 1]
                )
                todo[filled] = n * CHUNK + SPAN_ROWS + b * BLOCK
                filled = filled + jnp.where(wanted, 1, 0)
        for b in range(TILE_BLOCKS - 1):
            todo[filled + b] = spare

        def scores_of(first, rows):
            return lax.dot_general(
                queries[first : first + SUB, :], rows, (((1,), (1,)), ((), ())),
                preferred_element_type=jnp.float32,
            )

        def mix(weights, rows):
            return jnp.dot(weights.astype(jnp.bfloat16), rows, preferred_element_type=jnp.float32)

        if rows_of[0] == 0:
            at = q * TOK
            token = lax.broadcasted_iota(jnp.int32, (TOK, TOK), 0)
            key = lax.broadcasted_iota(jnp.int32, (TOK, TOK), 1)
            behind = (key <= token)[None]
            for first in range(0, ROWS, SUB):
                weights = jnp.exp2(scores_of(first, keys[at : at + TOK, :]) * TO_LOG2)
                weights = jnp.where(behind, weights.reshape(SUB // TOK, TOK, TOK), 0.0).reshape(SUB, TOK)
                part = mix(weights, values[at : at + TOK, :])
                if has_carry:
                    part = part + carry_ref[q, first : first + SUB, :]
                total_ref[q, first : first + SUB, :] = part
        else:
            total_ref[q] = carry_ref[q]

        def tile(blocks, begin):
            spots = [pl.multiple_of(todo[begin + b], BLOCK) for b in range(blocks)]
            key_rows = jnp.concatenate([keys[pl.ds(s, BLOCK), :] for s in spots], 0)
            value_rows = jnp.concatenate([values[pl.ds(s, BLOCK), :] for s in spots], 0)

            def finish(first, scores):
                weights = jnp.exp2(scores * TO_LOG2)
                total_ref[q, first : first + SUB, :] += mix(weights, value_rows)

            held = None
            for first in range(0, ROWS, SUB):
                scores = scores_of(first, key_rows)
                if held is not None:
                    finish(*held)
                held = (first, scores)
            finish(*held)

        whole = (filled + 3) // TILE_BLOCKS
        rest = filled - whole * TILE_BLOCKS

        def whole_tile(step, _):
            tile(TILE_BLOCKS, step * TILE_BLOCKS)
            return 0

        lax.fori_loop(0, whole, whole_tile, 0)

        @pl.when(rest > 2)
        def _():
            tile(4, whole * TILE_BLOCKS)

        @pl.when((rest > 0) & (rest <= 2))
        def _():
            tile(2, whole * TILE_BLOCKS)

        if last:
            held, top = refs[5:]

            def write_out():
                for h in range(GROUP):
                    mixed = total_ref[q, h * TOK : (h + 1) * TOK, :DIM]
                    total = total_ref[q, h * TOK : (h + 1) * TOK, DIM:]
                    out_refs[q][:, h * DIM : (h + 1) * DIM] = (mixed / total).astype(jnp.bfloat16)

            write_out()
            strange = jnp.zeros((TOK, DIM), jnp.float32)
            largest = jnp.zeros((TOK, DIM), jnp.float32)
            for h in range(GROUP):
                mixed = jnp.abs(total_ref[q, h * TOK : (h + 1) * TOK, :DIM])
                total = total_ref[q, h * TOK : (h + 1) * TOK, DIM:]
                good = (total >= LEAST_TOTAL) & (total <= MOST_TOTAL) & (mixed <= MOST_MIXED)
                strange = jnp.where(good, strange, 1.0)
                largest = jnp.maximum(largest, mixed)
            strange = jnp.where(jnp.max(largest) >= LEAST_MIXED, jnp.max(strange), 1.0)

            @pl.when(strange > 0.0)
            def _():
                careful(q, mine, place, first_open, table_ref, len_ref, last, all_refs,
                        queries, total_ref, held, top)
                write_out()


def careful(q, mine, place, first_open, table_ref, len_ref, parts, all_refs, queries, total_ref, held, top):
    core = place[2]
    total_ref[q] = jnp.zeros((ROWS, 2 * DIM), jnp.float32)
    top[...] = jnp.full((ROWS, DIM), -jnp.inf, jnp.float32)

    def add(keys, values, is_open):
        extent = keys.shape[0]

        def head(h, _):
            rows = pl.ds(pl.multiple_of(h * TOK, TOK), TOK)
            scores = lax.dot_general(
                queries[rows, :], keys, (((1,), (1,)), ((), ())), preferred_element_type=jnp.float32
            ) * (1.0 / math.sqrt(DIM))
            before = top[rows, :]
            highest = jnp.max(jnp.where(is_open, scores, -jnp.inf), -1, keepdims=True)
            after = jnp.maximum(before, highest)
            shift = jnp.where(after == -jnp.inf, 0.0, after)
            factor = jnp.exp(before - shift)
            weights = jnp.exp(jnp.minimum(scores - shift[:, :extent], 0.0))
            weights = jnp.where(is_open, weights, 0.0)
            mixed = jnp.dot(weights.astype(jnp.bfloat16), values, preferred_element_type=jnp.float32)
            total_ref[q, rows, :DIM] = total_ref[q, rows, :DIM] * factor + mixed
            total_ref[q, rows, DIM:] = total_ref[q, rows, DIM:] * factor + jnp.sum(weights, -1, keepdims=True)
            top[rows, :] = after
            return 0

        lax.fori_loop(0, GROUP, head, 0)

    for n, row in enumerate(OFFSETS):
        begin = 0
        for ref, units in zip(all_refs[n], parts[n]):

            def unit(u, _, ref=ref, row=row, begin=begin):
                pltpu.sync_copy(ref.at[u], held)
                k = begin + u
                there = chip_of(place, row, jnp.where(k < 2, -k, k - 1))

                def device(e, _):
                    shard = 2 * there + jnp.where(e == 0, core, 1 - core)
                    token = lax.broadcasted_iota(jnp.int32, (TOK, TOK), 0)
                    key = lax.broadcasted_iota(jnp.int32, (TOK, TOK), 1)
                    listed = table_ref[mine, shard] == 1
                    reach = jnp.where(shard < mine, TOK, jnp.where(shard == mine, 0, -2 * TOK))
                    reach = jnp.where(listed, reach, -2 * TOK)
                    add(held[e, 0, :TOK, :], held[e, 1, :TOK, :], key <= token + reach)
                    slot = lax.broadcasted_iota(jnp.int32, (TOK, LIVE), 1)
                    live = (slot >= first_open - shard * SLOTS) & (slot < len_ref[shard])
                    add(held[e, 0, TOK:, :], held[e, 1, TOK:, :], live)
                    return 0

                return lax.fori_loop(0, 2, device, 0)

            lax.fori_loop(0, units, unit, 0)
            begin += units


def stage(rows_of, last, scalars, queries, chunks, carry=None, after=()):
    smem = pl.BlockSpec(memory_space=pltpu.SMEM)
    vmem = pl.BlockSpec(memory_space=pltpu.VMEM)
    anywhere = pl.BlockSpec(memory_space=pl.ANY)
    operands = list(scalars) + list(queries)
    pieces = []
    for row in rows_of:
        operands += chunks[row]
        pieces.append(tuple(part.shape[0] for part in chunks[row]))
    if carry is not None:
        operands.append(carry)
    specs = [smem] * 4 + [vmem] * (len(operands) - 4)
    every = None
    if last:
        every = []
        for row in OFFSETS:
            operands += chunks[row]
            every.append(tuple(part.shape[0] for part in chunks[row]))
        every = tuple(every)
    operands += list(after)
    specs += [anywhere] * (len(operands) - len(specs))
    count = len(rows_of)
    total = ((2, ROWS, 2 * DIM), jnp.float32)
    scratch = [
        pltpu.VMEM((count * CHUNK + BLOCK, DIM), jnp.bfloat16),
        pltpu.VMEM((count * CHUNK + BLOCK, 2 * DIM), jnp.bfloat16),
        pltpu.VMEM((ROWS, DIM), jnp.bfloat16),
        pltpu.SMEM((count * (PER * 2 + CACHE_ROWS // BLOCK) + TILE_BLOCKS,), jnp.int32),
    ]
    if last:
        out_shape = (jax.ShapeDtypeStruct((TOK, GROUP * DIM), jnp.bfloat16),) * 2
        out_specs = (vmem, vmem)
        scratch = [pltpu.VMEM(*total)] + scratch + [
            pltpu.VMEM((2, 2, TOK + LIVE, DIM), jnp.bfloat16),
            pltpu.VMEM((ROWS, DIM), jnp.float32),
        ]
    else:
        out_shape = jax.ShapeDtypeStruct(*total)
        out_specs = vmem
    return pl.pallas_call(
        functools.partial(stage_kernel, tuple(rows_of), tuple(pieces), carry is not None, every, len(after)),
        out_shape=out_shape,
        in_specs=specs,
        out_specs=out_specs,
        scratch_shapes=scratch,
        compiler_params=pltpu.CompilerParams(vmem_limit_bytes=40 * 1024 * 1024),
        cost_estimate=pl.CostEstimate(
            flops=count * 2 * ROWS * CHUNK * DIM * 6,
            bytes_accessed=count * CHUNK * DIM * 4,
            transcendentals=count * 2 * ROWS * CHUNK,
        ),
        name="stage_" + "_".join(str(r % 4) for r in rows_of),
    )(*operands)


def pairs_kernel(place_ref, span_ref, cache_ref, *outs):
    core = place_ref[2]
    for out, head in zip(outs, (core, 1 - core, 2 + core, 3 - core)):
        columns = pl.ds(pl.multiple_of(head * DIM, DIM), DIM)
        for i in range(2):
            out[i, :TOK, :] = span_ref[i, :, columns]
            out[i, TOK:, :] = cache_ref[i, :LIVE, columns]


def queries_kernel(place_ref, queries_ref, stream_ref, *outs):
    core = place_ref[2]
    width = GROUP * DIM
    for out, head in zip(outs[:4], (core, 1 - core, 2 + core, 3 - core)):
        out[...] = queries_ref[:, pl.ds(pl.multiple_of(head * width, width), width)]
    outs[4][...] = stream_ref[:, 2 * width :]


def split(kernel, place, first, second, shapes, after=()):
    smem = pl.BlockSpec(memory_space=pltpu.SMEM)
    vmem = pl.BlockSpec(memory_space=pltpu.VMEM)
    anywhere = pl.BlockSpec(memory_space=pl.ANY)
    return pl.pallas_call(
        lambda place_ref, a, b, *rest: kernel(place_ref, a, b, *rest[len(after) :]),
        out_shape=tuple(jax.ShapeDtypeStruct(shape, jnp.bfloat16) for shape in shapes),
        in_specs=[smem, vmem, vmem] + [anywhere] * len(after),
        out_specs=(vmem,) * len(shapes),
        name=kernel.__name__,
    )(place, first, second, *after)


def spread(unit):
    return jnp.stack([unit] + [first_ring(unit, -k) for k in OFFSETS[1:]])


def shards(stream, queries, span_kv, cache_kv, cache_len, context_start, block_table):
    seq = lax.axis_index("seq")
    core = seq % 2
    place = jnp.stack([seq // 8, (seq // 2) % 4, core]).astype(jnp.int32)
    scalars = (place, block_table, cache_len, context_start)
    width = GROUP * DIM

    mine, theirs, late_same, late_cross = split(
        pairs_kernel, place, span_kv[0], cache_kv[0], [(2, TOK + LIVE, DIM)] * 4
    )
    near_unit = jnp.stack([mine, swapped(theirs)])
    late_unit = jnp.stack([up(late_same), up_swapped(late_cross)])
    q_mine, q_theirs, q_same, q_cross, stream_late = split(
        queries_kernel, place, queries[0], stream[0], [(TOK, width)] * 4 + [(TOK, 2 * width)]
    )
    near_q = (q_mine, swapped(q_theirs))
    late_q = (up(q_same), up_swapped(q_cross))
    late_stream = up(stream_late)

    near_row = spread(near_unit)
    near = {0: [near_row], -1: [second_ring(near_row, 1)], 1: [second_ring(near_row, -1)]}
    late_row = spread(late_unit)
    near_sum = stage((0,), False, scalars, near_q, near, after=[late_unit])
    near[2] = [second_ring(near[-1][0][:2], 1), second_ring(near[1][0][2:], -1)]
    late = {0: [late_row], -1: [second_ring(late_row, 1)], 1: [second_ring(late_row, -1)]}
    near_sum = stage((-1, 1), False, scalars, near_q, near, near_sum, after=[late_row])
    own, other = stage((2,), True, scalars, near_q, near, near_sum)

    def added(own, other, base):
        received = swapped(other)
        both = jnp.where(
            core == 0, jnp.concatenate([own, received], 1), jnp.concatenate([received, own], 1)
        )
        return (base.astype(jnp.float32) + both.astype(jnp.float32)).astype(jnp.bfloat16)

    late_sum = stage((0,), False, scalars, late_q, late, after=[own])
    near_done = added(own, other, stream[0, :, : 2 * width])
    near_out = up(near_done)
    late[2] = [second_ring(late[-1][0][:2], 1), second_ring(late[1][0][2:], -1)]
    late_sum = stage((-1, 1), False, scalars, late_q, late, late_sum, after=[near_done])
    own, other = stage((2,), True, scalars, late_q, late, late_sum, after=[near_out])
    late_out = added(own, other, late_stream)
    return jnp.concatenate([near_out, late_out], 1)[None]


def solution(mesh):
    return jax.shard_map(
        shards,
        mesh=mesh,
        in_specs=(
            P("section", "seq", None),
            P("section", "seq", None),
            P("section", None, "seq", None),
            P("section", None, "seq", None),
            P(),
            P(),
            P(),
        ),
        out_specs=P("section", "seq", None),
        check_vma=False,
    )
```

```python
import functools
import math

import jax
import jax.numpy as jnp
from jax import lax
from jax.experimental import pallas as pl
from jax.experimental.pallas import tpu as pltpu
from jax.sharding import PartitionSpec as P

DIM = 128
GROUP = 8
TOK = 128
SLOTS = 128
LIVE = 80
SHARDS = 32
CACHE = SLOTS * SHARDS
ROWS = GROUP * TOK
PER = 4
SPAN_ROWS = PER * 2 * TOK
CACHE_ROWS = PER * 2 * LIVE
PAIR = 2 * (TOK + LIVE)
CHUNK = SPAN_ROWS + CACHE_ROWS
BLOCK = 128
TILE_BLOCKS = 8
SUB = 256
OFFSETS = (0, -1, 1, 2)
TO_LOG2 = math.log2(math.e) / math.sqrt(DIM)
LEAST_TOTAL, MOST_TOTAL = 1e-12, 1e30
LEAST_MIXED, MOST_MIXED = 1e-20, 1e37
AXES = ("section", "seq")


def moved(value, rule):
    pairs = []
    for y in range(4):
        for z in range(4):
            for x in range(4):
                for c in range(2):
                    ty, tz, tx, tc = rule(y, z, x, c)
                    source = y * 32 + (z * 4 + x) * 2 + c
                    target = (ty % 4) * 32 + ((tz % 4) * 4 + tx % 4) * 2 + tc
                    pairs.append((source, target))
    return lax.ppermute(value, AXES, pairs)


def swapped(value):
    return moved(value, lambda y, z, x, c: (y, z, x, 1 - c))


def up(value):
    return moved(value, lambda y, z, x, c: (y + 1, z, x, c))


def up_swapped(value):
    return moved(value, lambda y, z, x, c: (y + 1, z, x, 1 - c))


def first_ring(value, k):
    return moved(value, lambda y, z, x, c: (y, z, x + k, c) if c == 0 else (y, z + k, x, c))


def second_ring(value, k):
    return moved(value, lambda y, z, x, c: (y, z + k, x, c) if c == 0 else (y, z, x + k, c))


def own_place():
    seq = lax.axis_index("seq")
    return seq >> 3, (seq >> 1) & 3, seq & 1


def chip_of(place, row, col):
    z, x, c = place
    dz = jnp.where(c == 0, row, col)
    dx = jnp.where(c == 0, col, row)
    return ((z + dz + 4) % 4) * 4 + (x + dx + 4) % 4


def stage_kernel(rows_of, pieces, has_carry, last, *refs):
    refs = list(refs)
    table_ref, len_ref, start_ref = refs[:3]
    q_refs, refs = refs[3:5], refs[5:]
    chunk_refs = []
    for part in pieces:
        chunk_refs.append(refs[: len(part)])
        refs = refs[len(part) :]
    carry_ref = None
    if has_carry:
        carry_ref, refs = refs[0], refs[1:]
    all_refs = []
    if last:
        for part in last:
            all_refs.append(refs[: len(part)])
            refs = refs[len(part) :]
    if last:
        out_refs, refs = refs[:2], refs[2:]
    total_ref, keys, values, todo = refs[:4]
    count = len(rows_of)
    place = own_place()
    core = place[2]
    chip = place[0] * 4 + place[1]
    first_open = CACHE - start_ref[0]

    def shard_at(row, k, e):
        return 2 * chip_of(place, row, OFFSETS[k]) + (core if e == 0 else 1 - core)

    for n in range(count):
        base = n * CHUNK
        values[base : base + SPAN_ROWS, DIM:] = jnp.ones((SPAN_ROWS, DIM), jnp.bfloat16)
        i = 0
        for ref, units in zip(chunk_refs[n], pieces[n]):
            for u in range(units):
                spot = base + i * TOK
                keys[spot : spot + TOK, :] = ref[u, 0, :TOK, :]
                values[spot : spot + TOK, :DIM] = ref[u, 1, :TOK, :]
                shard = shard_at(rows_of[n], i // 2, i % 2)
                low = first_open - shard * SLOTS
                slot = lax.broadcasted_iota(jnp.int32, (LIVE, DIM), 0)
                live = (slot >= low) & (slot < len_ref[shard])
                spot = base + SPAN_ROWS + i * LIVE
                keys[spot : spot + LIVE, :] = ref[u, 0, TOK:, :]
                piece = ref[u, 1, TOK:, :].astype(jnp.float32)
                values[spot : spot + LIVE, :DIM] = jnp.where(live, piece, 0.0).astype(jnp.bfloat16)
                values[spot : spot + LIVE, DIM:] = jnp.where(live, 1.0, 0.0).astype(jnp.bfloat16)
                i += 1
    spare = count * CHUNK
    keys[spare : spare + BLOCK, :] = jnp.zeros((BLOCK, DIM), jnp.bfloat16)
    values[spare : spare + BLOCK, :] = jnp.zeros((BLOCK, 2 * DIM), jnp.bfloat16)

    for q in range(2):
        mine = 2 * chip + (core if q == 0 else 1 - core)
        queries = q_refs[q].at[pl.ds(q_refs[q].shape[0] - ROWS, ROWS), :]

        filled = jnp.int32(0)
        for n in range(count):
            seen = []
            for k in range(PER):
                for e in range(2):
                    shard = shard_at(rows_of[n], k, e)
                    wanted = (shard < mine) & (table_ref[mine, shard] == 1)
                    todo[filled] = n * CHUNK + (2 * k + e) * TOK
                    filled = filled + jnp.where(wanted, 1, 0)
                    seen.append(shard * SLOTS + len_ref[shard] > first_open)
            for b in range(CACHE_ROWS // BLOCK):
                wanted = functools.reduce(
                    jnp.logical_or, seen[b * BLOCK // LIVE : ((b + 1) * BLOCK - 1) // LIVE + 1]
                )
                todo[filled] = n * CHUNK + SPAN_ROWS + b * BLOCK
                filled = filled + jnp.where(wanted, 1, 0)
        for b in range(TILE_BLOCKS - 1):
            todo[filled + b] = spare

        def scores_of(first, rows):
            return lax.dot_general(
                queries[first : first + SUB, :], rows, (((1,), (1,)), ((), ())),
                preferred_element_type=jnp.float32,
            )

        def mix(weights, rows):
            return jnp.dot(weights.astype(jnp.bfloat16), rows, preferred_element_type=jnp.float32)

        if rows_of[0] == 0:
            at = q * TOK
            token = lax.broadcasted_iota(jnp.int32, (TOK, TOK), 0)
            key = lax.broadcasted_iota(jnp.int32, (TOK, TOK), 1)
            behind = (key <= token)[None]
            for first in range(0, ROWS, SUB):
                weights = jnp.exp2(scores_of(first, keys[at : at + TOK, :]) * TO_LOG2)
                weights = jnp.where(behind, weights.reshape(SUB // TOK, TOK, TOK), 0.0).reshape(SUB, TOK)
                part = mix(weights, values[at : at + TOK, :])
                if has_carry:
                    part = part + carry_ref[q, first : first + SUB, :]
                total_ref[q, first : first + SUB, :] = part
        else:
            total_ref[q] = carry_ref[q]

        def tile(blocks, begin):
            spots = [pl.multiple_of(todo[begin + b], BLOCK) for b in range(blocks)]
            key_rows = jnp.concatenate([keys[pl.ds(s, BLOCK), :] for s in spots], 0)
            value_rows = jnp.concatenate([values[pl.ds(s, BLOCK), :] for s in spots], 0)

            def finish(first, scores):
                weights = jnp.exp2(scores * TO_LOG2)
                total_ref[q, first : first + SUB, :] += mix(weights, value_rows)

            held = None
            for first in range(0, ROWS, SUB):
                scores = scores_of(first, key_rows)
                if held is not None:
                    finish(*held)
                held = (first, scores)
            finish(*held)

        whole = (filled + 3) // TILE_BLOCKS
        rest = filled - whole * TILE_BLOCKS

        def whole_tile(step, _):
            tile(TILE_BLOCKS, step * TILE_BLOCKS)
            return 0

        lax.fori_loop(0, whole, whole_tile, 0)

        @pl.when(rest > 2)
        def _():
            tile(4, whole * TILE_BLOCKS)

        @pl.when((rest > 0) & (rest <= 2))
        def _():
            tile(2, whole * TILE_BLOCKS)

        if last:
            held, top = refs[4:]

            def write_out():
                for h in range(GROUP):
                    mixed = total_ref[q, h * TOK : (h + 1) * TOK, :DIM]
                    total = total_ref[q, h * TOK : (h + 1) * TOK, DIM:]
                    out_refs[q][:, h * DIM : (h + 1) * DIM] = (mixed / total).astype(jnp.bfloat16)

            write_out()
            strange = jnp.zeros((TOK, DIM), jnp.float32)
            largest = jnp.zeros((TOK, DIM), jnp.float32)
            for h in range(GROUP):
                mixed = jnp.abs(total_ref[q, h * TOK : (h + 1) * TOK, :DIM])
                total = total_ref[q, h * TOK : (h + 1) * TOK, DIM:]
                good = (total >= LEAST_TOTAL) & (total <= MOST_TOTAL) & (mixed <= MOST_MIXED)
                strange = jnp.where(good, strange, 1.0)
                largest = jnp.maximum(largest, mixed)
            strange = jnp.where(jnp.max(largest) >= LEAST_MIXED, jnp.max(strange), 1.0)

            @pl.when(strange > 0.0)
            def _():
                careful(q, mine, place, first_open, table_ref, len_ref, last, all_refs,
                        queries, total_ref, held, top)
                write_out()


def careful(q, mine, place, first_open, table_ref, len_ref, parts, all_refs, queries, total_ref, held, top):
    core = place[2]
    total_ref[q] = jnp.zeros((ROWS, 2 * DIM), jnp.float32)
    top[...] = jnp.full((ROWS, DIM), -jnp.inf, jnp.float32)

    def add(keys, values, is_open):
        extent = keys.shape[0]

        def head(h, _):
            rows = pl.ds(pl.multiple_of(h * TOK, TOK), TOK)
            scores = lax.dot_general(
                queries[rows, :], keys, (((1,), (1,)), ((), ())), preferred_element_type=jnp.float32
            ) * (1.0 / math.sqrt(DIM))
            before = top[rows, :]
            highest = jnp.max(jnp.where(is_open, scores, -jnp.inf), -1, keepdims=True)
            after = jnp.maximum(before, highest)
            shift = jnp.where(after == -jnp.inf, 0.0, after)
            factor = jnp.exp(before - shift)
            weights = jnp.exp(jnp.minimum(scores - shift[:, :extent], 0.0))
            weights = jnp.where(is_open, weights, 0.0)
            mixed = jnp.dot(weights.astype(jnp.bfloat16), values, preferred_element_type=jnp.float32)
            total_ref[q, rows, :DIM] = total_ref[q, rows, :DIM] * factor + mixed
            total_ref[q, rows, DIM:] = total_ref[q, rows, DIM:] * factor + jnp.sum(weights, -1, keepdims=True)
            top[rows, :] = after
            return 0

        lax.fori_loop(0, GROUP, head, 0)

    for n, row in enumerate(OFFSETS):
        begin = 0
        for ref, units in zip(all_refs[n], parts[n]):

            def unit(u, _, ref=ref, row=row, begin=begin):
                pltpu.sync_copy(ref.at[u], held)
                k, e = (begin + u) >> 1, (begin + u) & 1
                there = chip_of(place, row, jnp.where(k < 2, -k, k - 1))
                shard = 2 * there + jnp.where(e == 0, core, 1 - core)
                token = lax.broadcasted_iota(jnp.int32, (TOK, TOK), 0)
                key = lax.broadcasted_iota(jnp.int32, (TOK, TOK), 1)
                reach = jnp.where(shard < mine, TOK, jnp.where(shard == mine, 0, -2 * TOK))
                reach = jnp.where(table_ref[mine, shard] == 1, reach, -2 * TOK)
                add(held[0, :TOK, :], held[1, :TOK, :], key <= token + reach)
                slot = lax.broadcasted_iota(jnp.int32, (TOK, LIVE), 1)
                live = (slot >= first_open - shard * SLOTS) & (slot < len_ref[shard])
                add(held[0, TOK:, :], held[1, TOK:, :], live)
                return 0

            lax.fori_loop(0, units, unit, 0)
            begin += units


def stage(rows_of, last, scalars, queries, chunks, carry=None):
    smem = pl.BlockSpec(memory_space=pltpu.SMEM)
    vmem = pl.BlockSpec(memory_space=pltpu.VMEM)
    anywhere = pl.BlockSpec(memory_space=pl.ANY)
    operands = list(scalars) + list(queries)
    pieces = []
    for row in rows_of:
        operands += chunks[row]
        pieces.append(tuple(part.shape[0] for part in chunks[row]))
    if carry is not None:
        operands.append(carry)
    specs = [smem] * 3 + [vmem] * (len(operands) - 3)
    every = None
    if last:
        every = []
        for row in OFFSETS:
            operands += chunks[row]
            every.append(tuple(part.shape[0] for part in chunks[row]))
        every = tuple(every)
    specs += [anywhere] * (len(operands) - len(specs))
    count = len(rows_of)
    total = ((2, ROWS, 2 * DIM), jnp.float32)
    scratch = [
        pltpu.VMEM((count * CHUNK + BLOCK, DIM), jnp.bfloat16),
        pltpu.VMEM((count * CHUNK + BLOCK, 2 * DIM), jnp.bfloat16),
        pltpu.SMEM((count * (PER * 2 + CACHE_ROWS // BLOCK) + TILE_BLOCKS,), jnp.int32),
    ]
    if last:
        out_shape = (jax.ShapeDtypeStruct((TOK, GROUP * DIM), jnp.bfloat16),) * 2
        out_specs = (vmem, vmem)
        scratch = [pltpu.VMEM(*total)] + scratch + [
            pltpu.VMEM((2, TOK + LIVE, DIM), jnp.bfloat16),
            pltpu.VMEM((ROWS, DIM), jnp.float32),
        ]
    else:
        out_shape = jax.ShapeDtypeStruct(*total)
        out_specs = vmem
    return pl.pallas_call(
        functools.partial(stage_kernel, tuple(rows_of), tuple(pieces), carry is not None, every),
        out_shape=out_shape,
        in_specs=specs,
        out_specs=out_specs,
        scratch_shapes=scratch,
        compiler_params=pltpu.CompilerParams(vmem_limit_bytes=40 * 1024 * 1024),
        cost_estimate=pl.CostEstimate(
            flops=count * 2 * ROWS * CHUNK * DIM * 6,
            bytes_accessed=count * CHUNK * DIM * 4,
            transcendentals=count * 2 * ROWS * CHUNK,
        ),
        name="stage_" + "_".join(str(r % 4) for r in rows_of),
    )(*operands)


def ordered(value, *after):
    return lax.optimization_barrier((value, after))[0]


def split_kernel(span_ref, cache_ref, queries_ref, stream_ref, own_ref, own_q_ref, *rest):
    packs, stream_out, done = rest[:3], rest[3], rest[4]
    width = GROUP * DIM
    move = pltpu.make_async_copy(stream_ref.at[:, 2 * width :], stream_out, done)
    move.start()
    core = own_place()[2]

    def pairs_at(head, out, at):
        columns = pl.ds(pl.multiple_of(head * DIM, DIM), DIM)
        for i in range(2):
            begin = at + i * (TOK + LIVE)
            out[begin : begin + TOK, :] = span_ref[i, :, columns]
            out[begin + TOK : begin + TOK + LIVE, :] = cache_ref[i, :LIVE, columns]

    def queries_at(head, out, at):
        for h in range(GROUP):
            columns = pl.ds(pl.multiple_of(head * width + h * DIM, DIM), DIM)
            out[at + h * TOK : at + (h + 1) * TOK, :] = queries_ref[:, columns]

    pairs_at(core, own_ref, 0)
    queries_at(core, own_q_ref, 0)
    for out, head in zip(packs, (1 - core, 2 + core, 3 - core)):
        pairs_at(head, out, 0)
        queries_at(head, out, PAIR)
    move.wait()


def split(span, cache, queries, stream):
    vmem = pl.BlockSpec(memory_space=pltpu.VMEM)
    anywhere = pl.BlockSpec(memory_space=pl.ANY)
    shapes = [(PAIR, DIM), (ROWS, DIM)] + [(PAIR + ROWS, DIM)] * 3 + [(TOK, 2 * GROUP * DIM)]
    return pl.pallas_call(
        split_kernel,
        out_shape=tuple(jax.ShapeDtypeStruct(shape, jnp.bfloat16) for shape in shapes),
        in_specs=[vmem, vmem, vmem, anywhere],
        out_specs=(vmem,) * 5 + (anywhere,),
        scratch_shapes=[pltpu.SemaphoreType.DMA],
        cost_estimate=pl.CostEstimate(flops=0, bytes_accessed=8 * 1024 * 1024, transcendentals=0),
        name="split",
    )(span, cache, queries, stream)


def unit_of(first, second):
    return jnp.concatenate([first[:PAIR], second[:PAIR]]).reshape(2, 2, TOK + LIVE, DIM)


def shards(stream, queries, span_kv, cache_kv, cache_len, context_start, block_table):
    core = lax.axis_index("seq") % 2
    scalars = (block_table, cache_len, context_start)
    width = GROUP * DIM

    mine, q_mine, theirs, late_same, late_cross, stream_late = split(
        span_kv[0], cache_kv[0], queries[0], stream[0]
    )
    received = swapped(theirs)
    near_unit = unit_of(mine, received)
    near_q = (q_mine, received)
    late_parts = (up(late_same), up_swapped(late_cross))
    before, after = first_ring(near_unit, 1), first_ring(near_unit, -1)
    far = [first_ring(before[:1], 1), first_ring(after[1:], -1)]
    near_row = jnp.concatenate([near_unit, before, after] + far)
    near = {0: [near_row], -1: [second_ring(near_row, 1)], 1: [second_ring(near_row, -1)]}

    late_parts = ordered(late_parts, near_row)
    late_unit = unit_of(*late_parts)
    late_q = late_parts
    late_stream = up(stream_late)
    late_pieces = [first_ring(late_unit, -k) for k in OFFSETS[1:]]
    near_sum = stage((0,), False, scalars, ordered(near_q, late_unit), near)
    late_pieces = ordered(late_pieces, near_sum)
    near[-1] = ordered(near[-1], near_sum)
    near[2] = [second_ring(near[-1][0], 1)]
    late_row = jnp.concatenate([late_unit] + late_pieces)
    late = {0: [late_row], -1: [second_ring(late_row, 1)], 1: [second_ring(late_row, -1)]}
    near_sum = stage((-1, 1), False, scalars, ordered(near_q, late_row), near, near_sum)
    late[1] = ordered(late[1], near_sum)
    late[2] = [second_ring(late[1][0], -1)]
    own, other = stage((2,), True, scalars, ordered(near_q, late[1], late_stream), near, near_sum)

    def added(own, other, base):
        received = swapped(other)
        both = jnp.where(
            core == 0, jnp.concatenate([own, received], 1), jnp.concatenate([received, own], 1)
        )
        return (base.astype(jnp.float32) + both.astype(jnp.float32)).astype(jnp.bfloat16)

    near_done = added(own, other, stream[0, :, : 2 * width])
    near_out = up(near_done)
    late_sum = stage((0, -1, 1), False, scalars, ordered(late_q, near_done), late)
    late_sum, near_out = lax.optimization_barrier((late_sum, near_out))
    own, other = stage((2,), True, scalars, late_q, late, late_sum)
    late_out = added(own, other, late_stream)
    return jnp.concatenate([near_out, late_out], 1)[None]


def solution(mesh):
    return jax.shard_map(
        shards,
        mesh=mesh,
        in_specs=(
            P("section", "seq", None),
            P("section", "seq", None),
            P("section", None, "seq", None),
            P("section", None, "seq", None),
            P(),
            P(),
            P(),
        ),
        out_specs=P("section", "seq", None),
        check_vma=False,
    )
```

```python
import functools
import math

import jax
import jax.numpy as jnp
from jax import lax
from jax.experimental import pallas as pl
from jax.experimental.pallas import tpu as pltpu
from jax.sharding import PartitionSpec as P

DIM = 128
GROUP = 8
TOK = 128
SLOTS = 128
LIVE = 80
SHARDS = 32
CACHE = SLOTS * SHARDS
ROWS = GROUP * TOK
PER = 4
SPAN_ROWS = PER * 2 * TOK
CACHE_ROWS = PER * 2 * LIVE
PAIR = 2 * (TOK + LIVE)
CHUNK = SPAN_ROWS + CACHE_ROWS
BLOCK = 128
TILE_BLOCKS = 8
SUB = 256
OFFSETS = (0, -1, 1, 2)
TO_LOG2 = math.log2(math.e) / math.sqrt(DIM)
LEAST_TOTAL, MOST_TOTAL = 1e-12, 1e30
LEAST_MIXED, MOST_MIXED = 1e-20, 1e37
AXES = ("section", "seq")


def moved(value, rule):
    pairs = []
    for y in range(4):
        for z in range(4):
            for x in range(4):
                for c in range(2):
                    ty, tz, tx, tc = rule(y, z, x, c)
                    source = y * 32 + (z * 4 + x) * 2 + c
                    target = (ty % 4) * 32 + ((tz % 4) * 4 + tx % 4) * 2 + tc
                    pairs.append((source, target))
    return lax.ppermute(value, AXES, pairs)


def swapped(value):
    return moved(value, lambda y, z, x, c: (y, z, x, 1 - c))


def up(value):
    return moved(value, lambda y, z, x, c: (y + 1, z, x, c))


def up_swapped(value):
    return moved(value, lambda y, z, x, c: (y + 1, z, x, 1 - c))


def first_ring(value, k):
    return moved(value, lambda y, z, x, c: (y, z, x + k, c) if c == 0 else (y, z + k, x, c))


def second_ring(value, k):
    return moved(value, lambda y, z, x, c: (y, z + k, x, c) if c == 0 else (y, z, x + k, c))


def own_place():
    seq = lax.axis_index("seq")
    return seq >> 3, (seq >> 1) & 3, seq & 1


def chip_of(place, row, col):
    z, x, c = place
    dz = jnp.where(c == 0, row, col)
    dx = jnp.where(c == 0, col, row)
    return ((z + dz + 4) % 4) * 4 + (x + dx + 4) % 4


def stage_kernel(rows_of, pieces, has_carry, last, *refs):
    refs = list(refs)
    table_ref, len_ref, start_ref = refs[:3]
    q_refs, refs = refs[3:5], refs[5:]
    chunk_refs = []
    for part in pieces:
        chunk_refs.append(refs[: len(part)])
        refs = refs[len(part) :]
    carry_ref = None
    if has_carry:
        carry_ref, refs = refs[0], refs[1:]
    all_refs = []
    if last:
        for part in last:
            all_refs.append(refs[: len(part)])
            refs = refs[len(part) :]
    if last:
        out_refs, refs = refs[:2], refs[2:]
    total_ref, keys, values, todo = refs[:4]
    count = len(rows_of)
    place = own_place()
    core = place[2]
    chip = place[0] * 4 + place[1]
    first_open = CACHE - start_ref[0]

    def shard_at(row, k, e):
        return 2 * chip_of(place, row, OFFSETS[k]) + (core if e == 0 else 1 - core)

    for n in range(count):
        base = n * CHUNK
        values[base : base + SPAN_ROWS, DIM:] = jnp.ones((SPAN_ROWS, DIM), jnp.bfloat16)
        i = 0
        for ref, units in zip(chunk_refs[n], pieces[n]):
            for u in range(units):
                spot = base + i * TOK
                keys[spot : spot + TOK, :] = ref[u, 0, :TOK, :]
                values[spot : spot + TOK, :DIM] = ref[u, 1, :TOK, :]
                shard = shard_at(rows_of[n], i // 2, i % 2)
                low = first_open - shard * SLOTS
                slot = lax.broadcasted_iota(jnp.int32, (LIVE, DIM), 0)
                live = (slot >= low) & (slot < len_ref[shard])
                spot = base + SPAN_ROWS + i * LIVE
                keys[spot : spot + LIVE, :] = ref[u, 0, TOK:, :]
                piece = ref[u, 1, TOK:, :].astype(jnp.float32)
                values[spot : spot + LIVE, :DIM] = jnp.where(live, piece, 0.0).astype(jnp.bfloat16)
                values[spot : spot + LIVE, DIM:] = jnp.where(live, 1.0, 0.0).astype(jnp.bfloat16)
                i += 1
    spare = count * CHUNK
    keys[spare : spare + BLOCK, :] = jnp.zeros((BLOCK, DIM), jnp.bfloat16)
    values[spare : spare + BLOCK, :] = jnp.zeros((BLOCK, 2 * DIM), jnp.bfloat16)

    for q in range(2):
        mine = 2 * chip + (core if q == 0 else 1 - core)
        queries = q_refs[q].at[pl.ds(q_refs[q].shape[0] - ROWS, ROWS), :]

        filled = jnp.int32(0)
        for n in range(count):
            seen = []
            for k in range(PER):
                for e in range(2):
                    shard = shard_at(rows_of[n], k, e)
                    wanted = (shard < mine) & (table_ref[mine, shard] == 1)
                    todo[filled] = n * CHUNK + (2 * k + e) * TOK
                    filled = filled + jnp.where(wanted, 1, 0)
                    seen.append(shard * SLOTS + len_ref[shard] > first_open)
            for b in range(CACHE_ROWS // BLOCK):
                wanted = functools.reduce(
                    jnp.logical_or, seen[b * BLOCK // LIVE : ((b + 1) * BLOCK - 1) // LIVE + 1]
                )
                todo[filled] = n * CHUNK + SPAN_ROWS + b * BLOCK
                filled = filled + jnp.where(wanted, 1, 0)
        for b in range(TILE_BLOCKS - 1):
            todo[filled + b] = spare

        def scores_of(first, rows):
            return lax.dot_general(
                queries[first : first + SUB, :], rows, (((1,), (1,)), ((), ())),
                preferred_element_type=jnp.float32,
            )

        def mix(weights, rows):
            return jnp.dot(weights.astype(jnp.bfloat16), rows, preferred_element_type=jnp.float32)

        if rows_of[0] == 0:
            at = q * TOK
            token = lax.broadcasted_iota(jnp.int32, (TOK, TOK), 0)
            key = lax.broadcasted_iota(jnp.int32, (TOK, TOK), 1)
            behind = (key <= token)[None]
            for first in range(0, ROWS, SUB):
                weights = jnp.exp2(scores_of(first, keys[at : at + TOK, :]) * TO_LOG2)
                weights = jnp.where(behind, weights.reshape(SUB // TOK, TOK, TOK), 0.0).reshape(SUB, TOK)
                part = mix(weights, values[at : at + TOK, :])
                if has_carry:
                    part = part + carry_ref[q, first : first + SUB, :]
                total_ref[q, first : first + SUB, :] = part
        else:
            total_ref[q] = carry_ref[q]

        def tile(blocks, begin):
            spots = [pl.multiple_of(todo[begin + b], BLOCK) for b in range(blocks)]
            key_rows = jnp.concatenate([keys[pl.ds(s, BLOCK), :] for s in spots], 0)
            value_rows = jnp.concatenate([values[pl.ds(s, BLOCK), :] for s in spots], 0)

            def finish(first, scores):
                weights = jnp.exp2(scores * TO_LOG2)
                total_ref[q, first : first + SUB, :] += mix(weights, value_rows)

            held = None
            for first in range(0, ROWS, SUB):
                scores = scores_of(first, key_rows)
                if held is not None:
                    finish(*held)
                held = (first, scores)
            finish(*held)

        whole = (filled + 1) // TILE_BLOCKS
        rest = filled - whole * TILE_BLOCKS

        def whole_tile(step, _):
            tile(TILE_BLOCKS, step * TILE_BLOCKS)
            return 0

        lax.fori_loop(0, whole, whole_tile, 0)

        @pl.when(rest > 2)
        def _():
            tile(4, whole * TILE_BLOCKS)

        left = jnp.where(rest > 2, rest - 4, rest)

        @pl.when(left > 0)
        def _():
            tile(2, filled - left)

        if last:
            held, top = refs[4:]

            def write_out():
                for h in range(GROUP):
                    mixed = total_ref[q, h * TOK : (h + 1) * TOK, :DIM]
                    total = total_ref[q, h * TOK : (h + 1) * TOK, DIM:]
                    out_refs[q][:, h * DIM : (h + 1) * DIM] = (mixed / total).astype(jnp.bfloat16)

            write_out()
            strange = jnp.zeros((TOK, DIM), jnp.float32)
            largest = jnp.zeros((TOK, DIM), jnp.float32)
            for h in range(GROUP):
                mixed = jnp.abs(total_ref[q, h * TOK : (h + 1) * TOK, :DIM])
                total = total_ref[q, h * TOK : (h + 1) * TOK, DIM:]
                good = (total >= LEAST_TOTAL) & (total <= MOST_TOTAL) & (mixed <= MOST_MIXED)
                strange = jnp.where(good, strange, 1.0)
                largest = jnp.maximum(largest, mixed)
            strange = jnp.where(jnp.max(largest) >= LEAST_MIXED, jnp.max(strange), 1.0)

            @pl.when(strange > 0.0)
            def _():
                careful(q, mine, place, first_open, table_ref, len_ref, last, all_refs,
                        queries, total_ref, held, top)
                write_out()


def careful(q, mine, place, first_open, table_ref, len_ref, parts, all_refs, queries, total_ref, held, top):
    core = place[2]
    total_ref[q] = jnp.zeros((ROWS, 2 * DIM), jnp.float32)
    top[...] = jnp.full((ROWS, DIM), -jnp.inf, jnp.float32)

    def add(keys, values, is_open):
        extent = keys.shape[0]

        def head(h, _):
            rows = pl.ds(pl.multiple_of(h * TOK, TOK), TOK)
            scores = lax.dot_general(
                queries[rows, :], keys, (((1,), (1,)), ((), ())), preferred_element_type=jnp.float32
            ) * (1.0 / math.sqrt(DIM))
            before = top[rows, :]
            highest = jnp.max(jnp.where(is_open, scores, -jnp.inf), -1, keepdims=True)
            after = jnp.maximum(before, highest)
            shift = jnp.where(after == -jnp.inf, 0.0, after)
            factor = jnp.exp(before - shift)
            weights = jnp.exp(jnp.minimum(scores - shift[:, :extent], 0.0))
            weights = jnp.where(is_open, weights, 0.0)
            mixed = jnp.dot(weights.astype(jnp.bfloat16), values, preferred_element_type=jnp.float32)
            total_ref[q, rows, :DIM] = total_ref[q, rows, :DIM] * factor + mixed
            total_ref[q, rows, DIM:] = total_ref[q, rows, DIM:] * factor + jnp.sum(weights, -1, keepdims=True)
            top[rows, :] = after
            return 0

        lax.fori_loop(0, GROUP, head, 0)

    for n, row in enumerate(OFFSETS):
        begin = 0
        for ref, units in zip(all_refs[n], parts[n]):

            def unit(u, _, ref=ref, row=row, begin=begin):
                pltpu.sync_copy(ref.at[u], held)
                k, e = (begin + u) >> 1, (begin + u) & 1
                there = chip_of(place, row, jnp.where(k < 2, -k, k - 1))
                shard = 2 * there + jnp.where(e == 0, core, 1 - core)
                token = lax.broadcasted_iota(jnp.int32, (TOK, TOK), 0)
                key = lax.broadcasted_iota(jnp.int32, (TOK, TOK), 1)
                reach = jnp.where(shard < mine, TOK, jnp.where(shard == mine, 0, -2 * TOK))
                reach = jnp.where(table_ref[mine, shard] == 1, reach, -2 * TOK)
                add(held[0, :TOK, :], held[1, :TOK, :], key <= token + reach)
                slot = lax.broadcasted_iota(jnp.int32, (TOK, LIVE), 1)
                live = (slot >= first_open - shard * SLOTS) & (slot < len_ref[shard])
                add(held[0, TOK:, :], held[1, TOK:, :], live)
                return 0

            lax.fori_loop(0, units, unit, 0)
            begin += units


def stage(rows_of, last, scalars, queries, chunks, carry=None):
    smem = pl.BlockSpec(memory_space=pltpu.SMEM)
    vmem = pl.BlockSpec(memory_space=pltpu.VMEM)
    anywhere = pl.BlockSpec(memory_space=pl.ANY)
    operands = list(scalars) + list(queries)
    pieces = []
    for row in rows_of:
        operands += chunks[row]
        pieces.append(tuple(part.shape[0] for part in chunks[row]))
    if carry is not None:
        operands.append(carry)
    specs = [smem] * 3 + [vmem] * (len(operands) - 3)
    every = None
    if last:
        every = []
        for row in OFFSETS:
            operands += chunks[row]
            every.append(tuple(part.shape[0] for part in chunks[row]))
        every = tuple(every)
    specs += [anywhere] * (len(operands) - len(specs))
    count = len(rows_of)
    total = ((2, ROWS, 2 * DIM), jnp.float32)
    scratch = [
        pltpu.VMEM((count * CHUNK + BLOCK, DIM), jnp.bfloat16),
        pltpu.VMEM((count * CHUNK + BLOCK, 2 * DIM), jnp.bfloat16),
        pltpu.SMEM((count * (PER * 2 + CACHE_ROWS // BLOCK) + TILE_BLOCKS,), jnp.int32),
    ]
    if last:
        out_shape = (jax.ShapeDtypeStruct((TOK, GROUP * DIM), jnp.bfloat16),) * 2
        out_specs = (vmem, vmem)
        scratch = [pltpu.VMEM(*total)] + scratch + [
            pltpu.VMEM((2, TOK + LIVE, DIM), jnp.bfloat16),
            pltpu.VMEM((ROWS, DIM), jnp.float32),
        ]
    else:
        out_shape = jax.ShapeDtypeStruct(*total)
        out_specs = vmem
    return pl.pallas_call(
        functools.partial(stage_kernel, tuple(rows_of), tuple(pieces), carry is not None, every),
        out_shape=out_shape,
        in_specs=specs,
        out_specs=out_specs,
        scratch_shapes=scratch,
        compiler_params=pltpu.CompilerParams(vmem_limit_bytes=40 * 1024 * 1024),
        cost_estimate=pl.CostEstimate(
            flops=count * 2 * ROWS * CHUNK * DIM * 6,
            bytes_accessed=count * CHUNK * DIM * 4,
            transcendentals=count * 2 * ROWS * CHUNK,
        ),
        name="stage_" + "_".join(str(r % 4) for r in rows_of),
    )(*operands)


def ordered(value, *after):
    return lax.optimization_barrier((value, after))[0]


def split_kernel(span_ref, cache_ref, queries_ref, stream_ref, *outs):
    own, own_q, pack, same, cross, same_q, cross_q, late_stream = outs
    core = own_place()[2]
    width = GROUP * DIM

    def pairs_at(head, out):
        columns = pl.ds(pl.multiple_of(head * DIM, DIM), DIM)
        for i in range(2):
            begin = i * (TOK + LIVE)
            out[begin : begin + TOK, :] = span_ref[i, :, columns]
            out[begin + TOK : begin + TOK + LIVE, :] = cache_ref[i, :LIVE, columns]

    def queries_at(head, out, at):
        for h in range(GROUP):
            columns = pl.ds(pl.multiple_of(head * width + h * DIM, DIM), DIM)
            out[at + h * TOK : at + (h + 1) * TOK, :] = queries_ref[:, columns]

    pairs_at(core, own)
    queries_at(core, own_q, 0)
    pairs_at(1 - core, pack)
    queries_at(1 - core, pack, PAIR)
    pairs_at(2 + core, same)
    queries_at(2 + core, same_q, 0)
    late_stream[...] = stream_ref[:, 2 * width :]
    pairs_at(3 - core, cross)
    queries_at(3 - core, cross_q, 0)


def split(span, cache, queries, stream):
    vmem = pl.BlockSpec(memory_space=pltpu.VMEM)
    shapes = [(PAIR, DIM), (ROWS, DIM), (PAIR + ROWS, DIM)] + [(PAIR, DIM)] * 2
    shapes += [(ROWS, DIM)] * 2 + [(TOK, 2 * GROUP * DIM)]
    return pl.pallas_call(
        split_kernel,
        out_shape=tuple(jax.ShapeDtypeStruct(shape, jnp.bfloat16) for shape in shapes),
        in_specs=[vmem] * 4,
        out_specs=(vmem,) * len(shapes),
        cost_estimate=pl.CostEstimate(flops=0, bytes_accessed=8 * 1024 * 1024, transcendentals=0),
        name="split",
    )(span, cache, queries, stream)


def unit_of(first, second):
    return jnp.concatenate([first[:PAIR], second[:PAIR]]).reshape(2, 2, TOK + LIVE, DIM)


def shards(stream, queries, span_kv, cache_kv, cache_len, context_start, block_table):
    core = lax.axis_index("seq") % 2
    scalars = (block_table, cache_len, context_start)
    width = GROUP * DIM

    mine, q_mine, theirs, late_same, late_cross, q_same, q_cross, late_stream = split(
        span_kv[0], cache_kv[0], queries[0], stream[0]
    )
    received = swapped(theirs)
    near_unit = unit_of(mine, received)
    near_q = (q_mine, received)
    near_pieces = [first_ring(near_unit, -k) for k in OFFSETS[1:]]
    late_parts = (up(late_same), up_swapped(late_cross))
    near_pieces, late_parts = lax.optimization_barrier((near_pieces, late_parts))
    near_row = jnp.concatenate([near_unit] + near_pieces)
    near = {0: [near_row], -1: [second_ring(near_row, 1)], 1: [second_ring(near_row, -1)]}

    late_unit = unit_of(*ordered(late_parts, near_row))
    late_pieces = [first_ring(late_unit, -k) for k in OFFSETS[1:]]
    near_sum = stage((0,), False, scalars, ordered(near_q, late_unit), near)
    late_pieces = ordered(late_pieces, near_sum)
    late_row = jnp.concatenate([late_unit] + late_pieces)
    late = {0: [late_row], -1: [second_ring(late_row, 1)], 1: [second_ring(late_row, -1)]}
    near[-1] = ordered(near[-1], late_row)
    near[2] = [second_ring(near[-1][0], 1)]
    q_same, q_cross = ordered((q_same, q_cross), near_sum)
    late_q = (up(q_same), up_swapped(q_cross))
    near_sum = stage((-1, 1), False, scalars, ordered(near_q, late_row), near, near_sum)
    late[1] = ordered(late[1], near_sum)
    late[2] = [second_ring(late[1][0], -1)]
    own, other = stage((2,), True, scalars, ordered(near_q, late[1], late_q), near, near_sum)

    def added(own, other, base):
        received = swapped(other)
        both = jnp.where(
            core == 0, jnp.concatenate([own, received], 1), jnp.concatenate([received, own], 1)
        )
        return (base.astype(jnp.float32) + both.astype(jnp.float32)).astype(jnp.bfloat16)

    late_stream = up(ordered(late_stream, late_q))
    near_done = added(own, other, stream[0, :, : 2 * width])
    near_out = up(near_done)
    own, other = stage(OFFSETS, True, scalars, ordered(late_q, near_done, late[2]), late)
    other = ordered(other, near_out, late_stream)
    late_out = added(own, other, late_stream)
    return jnp.concatenate([near_out, late_out], 1)[None]


def solution(mesh):
    return jax.shard_map(
        shards,
        mesh=mesh,
        in_specs=(
            P("section", "seq", None),
            P("section", "seq", None),
            P("section", None, "seq", None),
            P("section", None, "seq", None),
            P(),
            P(),
            P(),
        ),
        out_specs=P("section", "seq", None),
        check_vma=False,
    )
```

```python
import functools
import math

import jax
import jax.numpy as jnp
from jax import lax
from jax.experimental import pallas as pl
from jax.experimental.pallas import tpu as pltpu
from jax.sharding import PartitionSpec as P

DIM = 128
GROUP = 8
TOK = 128
SLOTS = 128
LIVE = 80
SHARDS = 32
CACHE = SLOTS * SHARDS
ROWS = GROUP * TOK
PER = 4
SPAN_ROWS = PER * 2 * TOK
CACHE_ROWS = PER * 2 * LIVE
PAIR = 2 * (TOK + LIVE)
CHUNK = SPAN_ROWS + CACHE_ROWS
BLOCK = 128
TILE_BLOCKS = 8
SUB = 256
OFFSETS = (0, -1, 1, 2)
TO_LOG2 = math.log2(math.e) / math.sqrt(DIM)
LEAST_TOTAL, MOST_TOTAL = 1e-12, 1e30
LEAST_MIXED, MOST_MIXED = 1e-20, 1e37
AXES = ("section", "seq")


def moved(value, rule):
    pairs = []
    for y in range(4):
        for z in range(4):
            for x in range(4):
                for c in range(2):
                    ty, tz, tx, tc = rule(y, z, x, c)
                    source = y * 32 + (z * 4 + x) * 2 + c
                    target = (ty % 4) * 32 + ((tz % 4) * 4 + tx % 4) * 2 + tc
                    pairs.append((source, target))
    return lax.ppermute(value, AXES, pairs)


def swapped(value):
    return moved(value, lambda y, z, x, c: (y, z, x, 1 - c))


def up(value):
    return moved(value, lambda y, z, x, c: (y + 1, z, x, c))


def up_swapped(value):
    return moved(value, lambda y, z, x, c: (y + 1, z, x, 1 - c))


def first_ring(value, k):
    return moved(value, lambda y, z, x, c: (y, z, x + k, c) if c == 0 else (y, z + k, x, c))


def second_ring(value, k):
    return moved(value, lambda y, z, x, c: (y, z + k, x, c) if c == 0 else (y, z, x + k, c))


def own_place():
    seq = lax.axis_index("seq")
    return seq >> 3, (seq >> 1) & 3, seq & 1


def chip_of(place, row, col):
    z, x, c = place
    dz = jnp.where(c == 0, row, col)
    dx = jnp.where(c == 0, col, row)
    return ((z + dz + 4) % 4) * 4 + (x + dx + 4) % 4


def stage_kernel(rows_of, pieces, has_carry, last, *refs):
    refs = list(refs)
    table_ref, len_ref, start_ref = refs[:3]
    q_refs, refs = refs[3:5], refs[5:]
    chunk_refs = []
    for part in pieces:
        chunk_refs.append(refs[: len(part)])
        refs = refs[len(part) :]
    carry_ref = None
    if has_carry:
        carry_ref, refs = refs[0], refs[1:]
    all_refs = []
    if last:
        for part in last:
            all_refs.append(refs[: len(part)])
            refs = refs[len(part) :]
    if last:
        out_refs, refs = refs[:2], refs[2:]
    total_ref, keys, values, todo = refs[:4]
    count = len(rows_of)
    place = own_place()
    core = place[2]
    chip = place[0] * 4 + place[1]
    first_open = CACHE - start_ref[0]

    def shard_at(row, k, e):
        return 2 * chip_of(place, row, OFFSETS[k]) + (core if e == 0 else 1 - core)

    for n in range(count):
        base = n * CHUNK
        values[base : base + SPAN_ROWS, DIM:] = jnp.ones((SPAN_ROWS, DIM), jnp.bfloat16)
        i = 0
        for ref, units in zip(chunk_refs[n], pieces[n]):
            for u in range(units):
                spot = base + i * TOK
                keys[spot : spot + TOK, :] = ref[u, 0, :TOK, :]
                values[spot : spot + TOK, :DIM] = ref[u, 1, :TOK, :]
                shard = shard_at(rows_of[n], i // 2, i % 2)
                low = first_open - shard * SLOTS
                slot = lax.broadcasted_iota(jnp.int32, (LIVE, DIM), 0)
                live = (slot >= low) & (slot < len_ref[shard])
                spot = base + SPAN_ROWS + i * LIVE
                keys[spot : spot + LIVE, :] = ref[u, 0, TOK:, :]
                piece = ref[u, 1, TOK:, :].astype(jnp.float32)
                values[spot : spot + LIVE, :DIM] = jnp.where(live, piece, 0.0).astype(jnp.bfloat16)
                values[spot : spot + LIVE, DIM:] = jnp.where(live, 1.0, 0.0).astype(jnp.bfloat16)
                i += 1
    spare = count * CHUNK
    keys[spare : spare + BLOCK, :] = jnp.zeros((BLOCK, DIM), jnp.bfloat16)
    values[spare : spare + BLOCK, :] = jnp.zeros((BLOCK, 2 * DIM), jnp.bfloat16)

    for q in range(2):
        mine = 2 * chip + (core if q == 0 else 1 - core)
        queries = q_refs[q].at[pl.ds(q_refs[q].shape[0] - ROWS, ROWS), :]

        filled = jnp.int32(0)
        for n in range(count):
            seen = []
            for k in range(PER):
                for e in range(2):
                    shard = shard_at(rows_of[n], k, e)
                    wanted = (shard < mine) & (table_ref[mine, shard] == 1)
                    todo[filled] = n * CHUNK + (2 * k + e) * TOK
                    filled = filled + jnp.where(wanted, 1, 0)
                    seen.append(shard * SLOTS + len_ref[shard] > first_open)
            for b in range(CACHE_ROWS // BLOCK):
                wanted = functools.reduce(
                    jnp.logical_or, seen[b * BLOCK // LIVE : ((b + 1) * BLOCK - 1) // LIVE + 1]
                )
                todo[filled] = n * CHUNK + SPAN_ROWS + b * BLOCK
                filled = filled + jnp.where(wanted, 1, 0)
        for b in range(TILE_BLOCKS - 1):
            todo[filled + b] = spare

        def scores_of(first, rows):
            return lax.dot_general(
                queries[first : first + SUB, :], rows, (((1,), (1,)), ((), ())),
                preferred_element_type=jnp.float32,
            )

        def mix(weights, rows):
            return jnp.dot(weights.astype(jnp.bfloat16), rows, preferred_element_type=jnp.float32)

        if rows_of[0] == 0:
            at = q * TOK
            token = lax.broadcasted_iota(jnp.int32, (TOK, TOK), 0)
            key = lax.broadcasted_iota(jnp.int32, (TOK, TOK), 1)
            behind = (key <= token)[None]
            for first in range(0, ROWS, SUB):
                weights = jnp.exp2(scores_of(first, keys[at : at + TOK, :]) * TO_LOG2)
                weights = jnp.where(behind, weights.reshape(SUB // TOK, TOK, TOK), 0.0).reshape(SUB, TOK)
                part = mix(weights, values[at : at + TOK, :])
                if has_carry:
                    part = part + carry_ref[q, first : first + SUB, :]
                total_ref[q, first : first + SUB, :] = part
        else:
            total_ref[q] = carry_ref[q]

        def tile(blocks, begin):
            spots = [pl.multiple_of(todo[begin + b], BLOCK) for b in range(blocks)]
            key_rows = jnp.concatenate([keys[pl.ds(s, BLOCK), :] for s in spots], 0)
            value_rows = jnp.concatenate([values[pl.ds(s, BLOCK), :] for s in spots], 0)

            def finish(first, scores):
                weights = jnp.exp2(scores * TO_LOG2)
                total_ref[q, first : first + SUB, :] += mix(weights, value_rows)

            held = None
            for first in range(0, ROWS, SUB):
                scores = scores_of(first, key_rows)
                if held is not None:
                    finish(*held)
                held = (first, scores)
            finish(*held)

        whole = (filled + 1) // TILE_BLOCKS
        rest = filled - whole * TILE_BLOCKS

        def whole_tile(step, _):
            tile(TILE_BLOCKS, step * TILE_BLOCKS)
            return 0

        lax.fori_loop(0, whole, whole_tile, 0)

        @pl.when(rest > 2)
        def _():
            tile(4, whole * TILE_BLOCKS)

        left = jnp.where(rest > 2, rest - 4, rest)

        @pl.when(left > 0)
        def _():
            tile(2, filled - left)

        if last:
            held, top = refs[4:]

            def write_out():
                for h in range(GROUP):
                    mixed = total_ref[q, h * TOK : (h + 1) * TOK, :DIM]
                    total = total_ref[q, h * TOK : (h + 1) * TOK, DIM:]
                    out_refs[q][:, h * DIM : (h + 1) * DIM] = (mixed / total).astype(jnp.bfloat16)

            write_out()
            strange = jnp.zeros((TOK, DIM), jnp.float32)
            largest = jnp.zeros((TOK, DIM), jnp.float32)
            for h in range(GROUP):
                mixed = jnp.abs(total_ref[q, h * TOK : (h + 1) * TOK, :DIM])
                total = total_ref[q, h * TOK : (h + 1) * TOK, DIM:]
                good = (total >= LEAST_TOTAL) & (total <= MOST_TOTAL) & (mixed <= MOST_MIXED)
                strange = jnp.where(good, strange, 1.0)
                largest = jnp.maximum(largest, mixed)
            strange = jnp.where(jnp.max(largest) >= LEAST_MIXED, jnp.max(strange), 1.0)

            @pl.when(strange > 0.0)
            def _():
                careful(q, mine, place, first_open, table_ref, len_ref, last, all_refs,
                        queries, total_ref, held, top)
                write_out()


def careful(q, mine, place, first_open, table_ref, len_ref, parts, all_refs, queries, total_ref, held, top):
    core = place[2]
    total_ref[q] = jnp.zeros((ROWS, 2 * DIM), jnp.float32)
    top[...] = jnp.full((ROWS, DIM), -jnp.inf, jnp.float32)

    def add(keys, values, is_open):
        extent = keys.shape[0]

        def head(h, _):
            rows = pl.ds(pl.multiple_of(h * TOK, TOK), TOK)
            scores = lax.dot_general(
                queries[rows, :], keys, (((1,), (1,)), ((), ())), preferred_element_type=jnp.float32
            ) * (1.0 / math.sqrt(DIM))
            before = top[rows, :]
            highest = jnp.max(jnp.where(is_open, scores, -jnp.inf), -1, keepdims=True)
            after = jnp.maximum(before, highest)
            shift = jnp.where(after == -jnp.inf, 0.0, after)
            factor = jnp.exp(before - shift)
            weights = jnp.exp(jnp.minimum(scores - shift[:, :extent], 0.0))
            weights = jnp.where(is_open, weights, 0.0)
            mixed = jnp.dot(weights.astype(jnp.bfloat16), values, preferred_element_type=jnp.float32)
            total_ref[q, rows, :DIM] = total_ref[q, rows, :DIM] * factor + mixed
            total_ref[q, rows, DIM:] = total_ref[q, rows, DIM:] * factor + jnp.sum(weights, -1, keepdims=True)
            top[rows, :] = after
            return 0

        lax.fori_loop(0, GROUP, head, 0)

    for n, row in enumerate(OFFSETS):
        begin = 0
        for ref, units in zip(all_refs[n], parts[n]):

            def unit(u, _, ref=ref, row=row, begin=begin):
                pltpu.sync_copy(ref.at[u], held)
                k, e = (begin + u) >> 1, (begin + u) & 1
                there = chip_of(place, row, jnp.where(k < 2, -k, k - 1))
                shard = 2 * there + jnp.where(e == 0, core, 1 - core)
                token = lax.broadcasted_iota(jnp.int32, (TOK, TOK), 0)
                key = lax.broadcasted_iota(jnp.int32, (TOK, TOK), 1)
                reach = jnp.where(shard < mine, TOK, jnp.where(shard == mine, 0, -2 * TOK))
                reach = jnp.where(table_ref[mine, shard] == 1, reach, -2 * TOK)
                add(held[0, :TOK, :], held[1, :TOK, :], key <= token + reach)
                slot = lax.broadcasted_iota(jnp.int32, (TOK, LIVE), 1)
                live = (slot >= first_open - shard * SLOTS) & (slot < len_ref[shard])
                add(held[0, TOK:, :], held[1, TOK:, :], live)
                return 0

            lax.fori_loop(0, units, unit, 0)
            begin += units


def stage(rows_of, last, scalars, queries, chunks, carry=None):
    smem = pl.BlockSpec(memory_space=pltpu.SMEM)
    vmem = pl.BlockSpec(memory_space=pltpu.VMEM)
    anywhere = pl.BlockSpec(memory_space=pl.ANY)
    operands = list(scalars) + list(queries)
    pieces = []
    for row in rows_of:
        operands += chunks[row]
        pieces.append(tuple(part.shape[0] for part in chunks[row]))
    if carry is not None:
        operands.append(carry)
    specs = [smem] * 3 + [vmem] * (len(operands) - 3)
    every = None
    if last:
        every = []
        for row in OFFSETS:
            operands += chunks[row]
            every.append(tuple(part.shape[0] for part in chunks[row]))
        every = tuple(every)
    specs += [anywhere] * (len(operands) - len(specs))
    count = len(rows_of)
    total = ((2, ROWS, 2 * DIM), jnp.float32)
    scratch = [
        pltpu.VMEM((count * CHUNK + BLOCK, DIM), jnp.bfloat16),
        pltpu.VMEM((count * CHUNK + BLOCK, 2 * DIM), jnp.bfloat16),
        pltpu.SMEM((count * (PER * 2 + CACHE_ROWS // BLOCK) + TILE_BLOCKS,), jnp.int32),
    ]
    if last:
        out_shape = (jax.ShapeDtypeStruct((TOK, GROUP * DIM), jnp.bfloat16),) * 2
        out_specs = (vmem, vmem)
        scratch = [pltpu.VMEM(*total)] + scratch + [
            pltpu.VMEM((2, TOK + LIVE, DIM), jnp.bfloat16),
            pltpu.VMEM((ROWS, DIM), jnp.float32),
        ]
    else:
        out_shape = jax.ShapeDtypeStruct(*total)
        out_specs = vmem
    return pl.pallas_call(
        functools.partial(stage_kernel, tuple(rows_of), tuple(pieces), carry is not None, every),
        out_shape=out_shape,
        in_specs=specs,
        out_specs=out_specs,
        scratch_shapes=scratch,
        compiler_params=pltpu.CompilerParams(vmem_limit_bytes=40 * 1024 * 1024),
        cost_estimate=pl.CostEstimate(
            flops=count * 2 * ROWS * CHUNK * DIM * 6,
            bytes_accessed=count * CHUNK * DIM * 4,
            transcendentals=count * 2 * ROWS * CHUNK,
        ),
        name="stage_" + "_".join(str(r % 4) for r in rows_of),
    )(*operands)


def ordered(value, *after):
    return lax.optimization_barrier((value, after))[0]


def split_kernel(span_ref, cache_ref, queries_ref, stream_ref, *outs):
    own, own_q, pack, same, cross, same_q, cross_q, late_stream = outs
    core = own_place()[2]
    width = GROUP * DIM

    def pairs_at(head, out):
        columns = pl.ds(pl.multiple_of(head * DIM, DIM), DIM)
        for i in range(2):
            begin = i * (TOK + LIVE)
            out[begin : begin + TOK, :] = span_ref[i, :, columns]
            out[begin + TOK : begin + TOK + LIVE, :] = cache_ref[i, :LIVE, columns]

    def queries_at(head, out, at):
        for h in range(GROUP):
            columns = pl.ds(pl.multiple_of(head * width + h * DIM, DIM), DIM)
            out[at + h * TOK : at + (h + 1) * TOK, :] = queries_ref[:, columns]

    pairs_at(core, own)
    queries_at(core, own_q, 0)
    pairs_at(1 - core, pack)
    queries_at(1 - core, pack, PAIR)
    pairs_at(2 + core, same)
    queries_at(2 + core, same_q, 0)
    late_stream[...] = stream_ref[:, 2 * width :]
    pairs_at(3 - core, cross)
    queries_at(3 - core, cross_q, 0)


def split(span, cache, queries, stream):
    vmem = pl.BlockSpec(memory_space=pltpu.VMEM)
    shapes = [(PAIR, DIM), (ROWS, DIM), (PAIR + ROWS, DIM)] + [(PAIR, DIM)] * 2
    shapes += [(ROWS, DIM)] * 2 + [(TOK, 2 * GROUP * DIM)]
    return pl.pallas_call(
        split_kernel,
        out_shape=tuple(jax.ShapeDtypeStruct(shape, jnp.bfloat16) for shape in shapes),
        in_specs=[vmem] * 4,
        out_specs=(vmem,) * len(shapes),
        cost_estimate=pl.CostEstimate(flops=0, bytes_accessed=8 * 1024 * 1024, transcendentals=0),
        name="split",
    )(span, cache, queries, stream)


def unit_of(first, second):
    return jnp.concatenate([first[:PAIR], second[:PAIR]]).reshape(2, 2, TOK + LIVE, DIM)


def shards(stream, queries, span_kv, cache_kv, cache_len, context_start, block_table):
    core = lax.axis_index("seq") % 2
    scalars = (block_table, cache_len, context_start)
    width = GROUP * DIM

    mine, q_mine, theirs, late_same, late_cross, q_same, q_cross, late_stream = split(
        span_kv[0], cache_kv[0], queries[0], stream[0]
    )
    received = swapped(theirs)
    near_unit = unit_of(mine, received)
    near_q = (q_mine, received)
    near_pieces = [first_ring(near_unit, -k) for k in OFFSETS[1:]]
    late_parts = (up(late_same), up_swapped(late_cross))
    near_pieces, late_parts = lax.optimization_barrier((near_pieces, late_parts))
    near_row = jnp.concatenate([near_unit] + near_pieces)
    near = {0: [near_row], -1: [second_ring(near_row, 1)], 1: [second_ring(near_row, -1)]}

    q_same, q_cross = ordered((q_same, q_cross), near_row)
    late_q = (up(q_same), up_swapped(q_cross))
    near_sum = stage((0,), False, scalars, near_q, near)
    late_q = ordered(late_q, near_sum)
    late_unit = unit_of(*ordered(late_parts, near_sum))
    late_pieces = [first_ring(late_unit, -k) for k in OFFSETS[1:]]
    late_stream = up(ordered(late_stream, near_sum))
    near[-1] = ordered(near[-1], near_sum)
    near[2] = [second_ring(near[-1][0], 1)]
    near_sum = stage((-1, 1), False, scalars, ordered(near_q, late_unit, late_q), near, near_sum)
    late_pieces = ordered(late_pieces, near_sum)
    late_row = jnp.concatenate([late_unit] + late_pieces)
    late = {0: [late_row], -1: [second_ring(late_row, 1)], 1: [second_ring(late_row, -1)]}
    own, other = stage((2,), True, scalars, ordered(near_q, late_row, late_stream), near, near_sum)
    late[1] = ordered(late[1], own)
    late[2] = [second_ring(late[1][0], -1)]

    def added(own, other, base):
        received = swapped(other)
        both = jnp.where(
            core == 0, jnp.concatenate([own, received], 1), jnp.concatenate([received, own], 1)
        )
        return (base.astype(jnp.float32) + both.astype(jnp.float32)).astype(jnp.bfloat16)

    near_done = added(own, other, stream[0, :, : 2 * width])
    near_out = up(near_done)
    late_sum = stage((0, -1, 1), False, scalars, ordered(late_q, near_done), late)
    late_sum, near_out = lax.optimization_barrier((late_sum, near_out))
    own, other = stage((2,), True, scalars, late_q, late, late_sum)
    late_out = added(own, other, late_stream)
    return jnp.concatenate([near_out, late_out], 1)[None]


def solution(mesh):
    return jax.shard_map(
        shards,
        mesh=mesh,
        in_specs=(
            P("section", "seq", None),
            P("section", "seq", None),
            P("section", None, "seq", None),
            P("section", None, "seq", None),
            P(),
            P(),
            P(),
        ),
        out_specs=P("section", "seq", None),
        check_vma=False,
    )
```

```python
import functools
import math

import jax
import jax.numpy as jnp
from jax import lax
from jax.experimental import pallas as pl
from jax.experimental.pallas import tpu as pltpu
from jax.sharding import PartitionSpec as P

DIM = 128
GROUP = 8
TOK = 128
SLOTS = 128
LIVE = 80
SHARDS = 32
CACHE = SLOTS * SHARDS
ROWS = GROUP * TOK
PER = 4
SPAN_ROWS = PER * 2 * TOK
CACHE_ROWS = PER * 2 * LIVE
PAIR = 2 * (TOK + LIVE)
CHUNK = SPAN_ROWS + CACHE_ROWS
BLOCK = 128
TILE_BLOCKS = 8
SUB = 256
OFFSETS = (0, -1, 1, 2)
TO_LOG2 = math.log2(math.e) / math.sqrt(DIM)
LEAST_TOTAL, MOST_TOTAL = 1e-12, 1e30
LEAST_MIXED, MOST_MIXED = 1e-20, 1e37
AXES = ("section", "seq")


def moved(value, rule):
    pairs = []
    for y in range(4):
        for z in range(4):
            for x in range(4):
                for c in range(2):
                    ty, tz, tx, tc = rule(y, z, x, c)
                    source = y * 32 + (z * 4 + x) * 2 + c
                    target = (ty % 4) * 32 + ((tz % 4) * 4 + tx % 4) * 2 + tc
                    pairs.append((source, target))
    return lax.ppermute(value, AXES, pairs)


def swapped(value):
    return moved(value, lambda y, z, x, c: (y, z, x, 1 - c))


def up(value):
    return moved(value, lambda y, z, x, c: (y + 1, z, x, c))


def up_swapped(value):
    return moved(value, lambda y, z, x, c: (y + 1, z, x, 1 - c))


def first_ring(value, k):
    return moved(value, lambda y, z, x, c: (y, z, x + k, c) if c == 0 else (y, z + k, x, c))


def second_ring(value, k):
    return moved(value, lambda y, z, x, c: (y, z + k, x, c) if c == 0 else (y, z, x + k, c))


def own_place():
    seq = lax.axis_index("seq")
    return seq >> 3, (seq >> 1) & 3, seq & 1


def first_exchange(value):
    return moved(value, lambda y, z, x, c: (y, z, x ^ 1, c) if c == 0 else (y, z ^ 1, x, c))


def second_exchange(value):
    return moved(value, lambda y, z, x, c: (y, z, 3 - x, c) if c == 0 else (y, 3 - z, x, c))


def chip_of(place, row, col):
    z, x, c = place
    dz = jnp.where(c == 0, row, col)
    dx = jnp.where(c == 0, col, row)
    return ((z + dz + 4) % 4) * 4 + (x + dx + 4) % 4


def stage_kernel(rows_of, pieces, has_carry, last, paired, *refs):
    refs = list(refs)
    table_ref, len_ref, start_ref = refs[:3]
    q_refs, refs = refs[3:5], refs[5:]
    chunk_refs = []
    for part in pieces:
        chunk_refs.append(refs[: len(part)])
        refs = refs[len(part) :]
    carry_ref = None
    if has_carry:
        carry_ref, refs = refs[0], refs[1:]
    all_refs = []
    if last:
        for part in last:
            all_refs.append(refs[: len(part)])
            refs = refs[len(part) :]
    if last:
        out_refs, refs = refs[:2], refs[2:]
    total_ref, keys, values, todo = refs[:4]
    count = len(rows_of)
    place = own_place()
    core = place[2]
    chip = place[0] * 4 + place[1]
    first_open = CACHE - start_ref[0]

    sign = 1
    if paired:
        sign = 2 * (jnp.where(core == 0, place[1], place[0]) & 1) - 1

    def shard_at(row, k, e):
        step = OFFSETS[k] * sign if k in (1, 2) else OFFSETS[k]
        return 2 * chip_of(place, row, step) + (core if e == 0 else 1 - core)

    for n in range(count):
        base = n * CHUNK
        values[base : base + SPAN_ROWS, DIM:] = jnp.ones((SPAN_ROWS, DIM), jnp.bfloat16)
        i = 0
        for ref, units in zip(chunk_refs[n], pieces[n]):
            for u in range(units):
                spot = base + i * TOK
                keys[spot : spot + TOK, :] = ref[u, 0, :TOK, :]
                values[spot : spot + TOK, :DIM] = ref[u, 1, :TOK, :]
                shard = shard_at(rows_of[n], i // 2, i % 2)
                low = first_open - shard * SLOTS
                slot = lax.broadcasted_iota(jnp.int32, (LIVE, DIM), 0)
                live = (slot >= low) & (slot < len_ref[shard])
                spot = base + SPAN_ROWS + i * LIVE
                keys[spot : spot + LIVE, :] = ref[u, 0, TOK:, :]
                piece = ref[u, 1, TOK:, :].astype(jnp.float32)
                values[spot : spot + LIVE, :DIM] = jnp.where(live, piece, 0.0).astype(jnp.bfloat16)
                values[spot : spot + LIVE, DIM:] = jnp.where(live, 1.0, 0.0).astype(jnp.bfloat16)
                i += 1
    spare = count * CHUNK
    keys[spare : spare + BLOCK, :] = jnp.zeros((BLOCK, DIM), jnp.bfloat16)
    values[spare : spare + BLOCK, :] = jnp.zeros((BLOCK, 2 * DIM), jnp.bfloat16)

    for q in range(2):
        mine = 2 * chip + (core if q == 0 else 1 - core)
        queries = q_refs[q].at[pl.ds(q_refs[q].shape[0] - ROWS, ROWS), :]

        filled = jnp.int32(0)
        for n in range(count):
            seen = []
            for k in range(PER):
                for e in range(2):
                    shard = shard_at(rows_of[n], k, e)
                    wanted = (shard < mine) & (table_ref[mine, shard] == 1)
                    todo[filled] = n * CHUNK + (2 * k + e) * TOK
                    filled = filled + jnp.where(wanted, 1, 0)
                    seen.append(shard * SLOTS + len_ref[shard] > first_open)
            for b in range(CACHE_ROWS // BLOCK):
                wanted = functools.reduce(
                    jnp.logical_or, seen[b * BLOCK // LIVE : ((b + 1) * BLOCK - 1) // LIVE + 1]
                )
                todo[filled] = n * CHUNK + SPAN_ROWS + b * BLOCK
                filled = filled + jnp.where(wanted, 1, 0)
        for b in range(TILE_BLOCKS - 1):
            todo[filled + b] = spare

        def scores_of(first, rows):
            return lax.dot_general(
                queries[first : first + SUB, :], rows, (((1,), (1,)), ((), ())),
                preferred_element_type=jnp.float32,
            )

        def mix(weights, rows):
            return jnp.dot(weights.astype(jnp.bfloat16), rows, preferred_element_type=jnp.float32)

        if rows_of[0] == 0:
            at = q * TOK
            token = lax.broadcasted_iota(jnp.int32, (TOK, TOK), 0)
            key = lax.broadcasted_iota(jnp.int32, (TOK, TOK), 1)
            behind = (key <= token)[None]
            for first in range(0, ROWS, SUB):
                weights = jnp.exp2(scores_of(first, keys[at : at + TOK, :]) * TO_LOG2)
                weights = jnp.where(behind, weights.reshape(SUB // TOK, TOK, TOK), 0.0).reshape(SUB, TOK)
                part = mix(weights, values[at : at + TOK, :])
                if has_carry:
                    part = part + carry_ref[q, first : first + SUB, :]
                total_ref[q, first : first + SUB, :] = part
        else:
            total_ref[q] = carry_ref[q]

        def tile(blocks, begin):
            spots = [pl.multiple_of(todo[begin + b], BLOCK) for b in range(blocks)]
            key_rows = jnp.concatenate([keys[pl.ds(s, BLOCK), :] for s in spots], 0)
            value_rows = jnp.concatenate([values[pl.ds(s, BLOCK), :] for s in spots], 0)

            def finish(first, scores):
                weights = jnp.exp2(scores * TO_LOG2)
                total_ref[q, first : first + SUB, :] += mix(weights, value_rows)

            held = None
            for first in range(0, ROWS, SUB):
                scores = scores_of(first, key_rows)
                if held is not None:
                    finish(*held)
                held = (first, scores)
            finish(*held)

        whole = (filled + 1) // TILE_BLOCKS
        rest = filled - whole * TILE_BLOCKS

        def whole_tile(step, _):
            tile(TILE_BLOCKS, step * TILE_BLOCKS)
            return 0

        lax.fori_loop(0, whole, whole_tile, 0)

        @pl.when(rest > 2)
        def _():
            tile(4, whole * TILE_BLOCKS)

        left = jnp.where(rest > 2, rest - 4, rest)

        @pl.when(left > 0)
        def _():
            tile(2, filled - left)

        if last:
            held, top = refs[4:]

            def write_out():
                for h in range(GROUP):
                    mixed = total_ref[q, h * TOK : (h + 1) * TOK, :DIM]
                    total = total_ref[q, h * TOK : (h + 1) * TOK, DIM:]
                    out_refs[q][:, h * DIM : (h + 1) * DIM] = (mixed / total).astype(jnp.bfloat16)

            write_out()
            strange = jnp.zeros((TOK, DIM), jnp.float32)
            largest = jnp.zeros((TOK, DIM), jnp.float32)
            for h in range(GROUP):
                mixed = jnp.abs(total_ref[q, h * TOK : (h + 1) * TOK, :DIM])
                total = total_ref[q, h * TOK : (h + 1) * TOK, DIM:]
                good = (total >= LEAST_TOTAL) & (total <= MOST_TOTAL) & (mixed <= MOST_MIXED)
                strange = jnp.where(good, strange, 1.0)
                largest = jnp.maximum(largest, mixed)
            strange = jnp.where(jnp.max(largest) >= LEAST_MIXED, jnp.max(strange), 1.0)

            @pl.when(strange > 0.0)
            def _():
                careful(q, mine, place, sign, first_open, table_ref, len_ref, last, all_refs,
                        queries, total_ref, held, top)
                write_out()


def careful(q, mine, place, sign, first_open, table_ref, len_ref, parts, all_refs, queries, total_ref, held, top):
    core = place[2]
    total_ref[q] = jnp.zeros((ROWS, 2 * DIM), jnp.float32)
    top[...] = jnp.full((ROWS, DIM), -jnp.inf, jnp.float32)

    def add(keys, values, is_open):
        extent = keys.shape[0]

        def head(h, _):
            rows = pl.ds(pl.multiple_of(h * TOK, TOK), TOK)
            scores = lax.dot_general(
                queries[rows, :], keys, (((1,), (1,)), ((), ())), preferred_element_type=jnp.float32
            ) * (1.0 / math.sqrt(DIM))
            before = top[rows, :]
            highest = jnp.max(jnp.where(is_open, scores, -jnp.inf), -1, keepdims=True)
            after = jnp.maximum(before, highest)
            shift = jnp.where(after == -jnp.inf, 0.0, after)
            factor = jnp.exp(before - shift)
            weights = jnp.exp(jnp.minimum(scores - shift[:, :extent], 0.0))
            weights = jnp.where(is_open, weights, 0.0)
            mixed = jnp.dot(weights.astype(jnp.bfloat16), values, preferred_element_type=jnp.float32)
            total_ref[q, rows, :DIM] = total_ref[q, rows, :DIM] * factor + mixed
            total_ref[q, rows, DIM:] = total_ref[q, rows, DIM:] * factor + jnp.sum(weights, -1, keepdims=True)
            top[rows, :] = after
            return 0

        lax.fori_loop(0, GROUP, head, 0)

    for n, row in enumerate(OFFSETS):
        begin = 0
        for ref, units in zip(all_refs[n], parts[n]):

            def unit(u, _, ref=ref, row=row, begin=begin):
                pltpu.sync_copy(ref.at[u], held)
                k, e = (begin + u) >> 1, (begin + u) & 1
                there = chip_of(place, row, jnp.where(k == 3, 2, jnp.where(k < 2, -k, k - 1) * sign))
                shard = 2 * there + jnp.where(e == 0, core, 1 - core)
                token = lax.broadcasted_iota(jnp.int32, (TOK, TOK), 0)
                key = lax.broadcasted_iota(jnp.int32, (TOK, TOK), 1)
                reach = jnp.where(shard < mine, TOK, jnp.where(shard == mine, 0, -2 * TOK))
                reach = jnp.where(table_ref[mine, shard] == 1, reach, -2 * TOK)
                add(held[0, :TOK, :], held[1, :TOK, :], key <= token + reach)
                slot = lax.broadcasted_iota(jnp.int32, (TOK, LIVE), 1)
                live = (slot >= first_open - shard * SLOTS) & (slot < len_ref[shard])
                add(held[0, TOK:, :], held[1, TOK:, :], live)
                return 0

            lax.fori_loop(0, units, unit, 0)
            begin += units


def stage(rows_of, last, scalars, queries, chunks, carry=None, paired=False):
    smem = pl.BlockSpec(memory_space=pltpu.SMEM)
    vmem = pl.BlockSpec(memory_space=pltpu.VMEM)
    anywhere = pl.BlockSpec(memory_space=pl.ANY)
    operands = list(scalars) + list(queries)
    pieces = []
    for row in rows_of:
        operands += chunks[row]
        pieces.append(tuple(part.shape[0] for part in chunks[row]))
    if carry is not None:
        operands.append(carry)
    specs = [smem] * 3 + [vmem] * (len(operands) - 3)
    every = None
    if last:
        every = []
        for row in OFFSETS:
            operands += chunks[row]
            every.append(tuple(part.shape[0] for part in chunks[row]))
        every = tuple(every)
    specs += [anywhere] * (len(operands) - len(specs))
    count = len(rows_of)
    total = ((2, ROWS, 2 * DIM), jnp.float32)
    scratch = [
        pltpu.VMEM((count * CHUNK + BLOCK, DIM), jnp.bfloat16),
        pltpu.VMEM((count * CHUNK + BLOCK, 2 * DIM), jnp.bfloat16),
        pltpu.SMEM((count * (PER * 2 + CACHE_ROWS // BLOCK) + TILE_BLOCKS,), jnp.int32),
    ]
    if last:
        out_shape = (jax.ShapeDtypeStruct((TOK, GROUP * DIM), jnp.bfloat16),) * 2
        out_specs = (vmem, vmem)
        scratch = [pltpu.VMEM(*total)] + scratch + [
            pltpu.VMEM((2, TOK + LIVE, DIM), jnp.bfloat16),
            pltpu.VMEM((ROWS, DIM), jnp.float32),
        ]
    else:
        out_shape = jax.ShapeDtypeStruct(*total)
        out_specs = vmem
    return pl.pallas_call(
        functools.partial(stage_kernel, tuple(rows_of), tuple(pieces), carry is not None, every, paired),
        out_shape=out_shape,
        in_specs=specs,
        out_specs=out_specs,
        scratch_shapes=scratch,
        compiler_params=pltpu.CompilerParams(vmem_limit_bytes=40 * 1024 * 1024),
        cost_estimate=pl.CostEstimate(
            flops=count * 2 * ROWS * CHUNK * DIM * 6,
            bytes_accessed=count * CHUNK * DIM * 4,
            transcendentals=count * 2 * ROWS * CHUNK,
        ),
        name="stage_" + "_".join(str(r % 4) for r in rows_of),
    )(*operands)


def ordered(value, *after):
    return lax.optimization_barrier((value, after))[0]


def pairs_at(span_ref, cache_ref, head, out):
    columns = pl.ds(pl.multiple_of(head * DIM, DIM), DIM)
    for i in range(2):
        begin = i * (TOK + LIVE)
        out[begin : begin + TOK, :] = span_ref[i, :, columns]
        out[begin + TOK : begin + TOK + LIVE, :] = cache_ref[i, :LIVE, columns]


def queries_at(queries_ref, head, out, at):
    for h in range(GROUP):
        columns = pl.ds(pl.multiple_of((head * GROUP + h) * DIM, DIM), DIM)
        out[at + h * TOK : at + (h + 1) * TOK, :] = queries_ref[:, columns]


def near_kernel(span_ref, cache_ref, queries_ref, own, own_q, pack, same, cross):
    core = own_place()[2]
    for head, out in ((core, own), (1 - core, pack), (2 + core, same), (3 - core, cross)):
        pairs_at(span_ref, cache_ref, head, out)
    queries_at(queries_ref, core, own_q, 0)
    queries_at(queries_ref, 1 - core, pack, PAIR)


def late_kernel(queries_ref, stream_ref, same_q, cross_q, late_stream):
    core = own_place()[2]
    queries_at(queries_ref, core, same_q, 0)
    queries_at(queries_ref, 1 - core, cross_q, 0)
    late_stream[...] = stream_ref[...]


def cut(kernel, operands, specs, shapes):
    whole = lambda shape: pl.BlockSpec(shape, lambda i: (0,) * len(shape))
    return pl.pallas_call(
        kernel,
        grid=(1,),
        out_shape=tuple(jax.ShapeDtypeStruct(shape, jnp.bfloat16) for shape in shapes),
        in_specs=specs,
        out_specs=tuple(whole(shape) for shape in shapes),
        cost_estimate=pl.CostEstimate(flops=0, bytes_accessed=8 * 1024 * 1024, transcendentals=0),
        name=kernel.__name__,
    )(*operands)


def unit_of(first, second):
    return jnp.concatenate([first[:PAIR], second[:PAIR]]).reshape(2, 2, TOK + LIVE, DIM)


def shards(stream, queries, span_kv, cache_kv, cache_len, context_start, block_table):
    core = lax.axis_index("seq") % 2
    scalars = (block_table, cache_len, context_start)
    width = GROUP * DIM

    half = 2 * width
    left = pl.BlockSpec((TOK, half), lambda i: (0, 0))
    right = pl.BlockSpec((TOK, half), lambda i: (0, 1))
    mine, q_mine, theirs, late_same, late_cross = cut(
        near_kernel,
        (span_kv[0], cache_kv[0], queries[0]),
        [pl.BlockSpec((2, TOK, 4 * DIM), lambda i: (0, 0, 0))] * 2 + [left],
        [(PAIR, DIM), (ROWS, DIM), (PAIR + ROWS, DIM)] + [(PAIR, DIM)] * 2,
    )
    received = swapped(theirs)
    near_unit = unit_of(mine, received)
    near_q = (q_mine, received)
    late_queries, late_base = ordered((queries[0], stream[0]), near_unit)
    q_same, q_cross, late_stream = cut(
        late_kernel, (late_queries, late_base), [right, right], [(ROWS, DIM)] * 2 + [(TOK, half)]
    )
    near_pieces = [first_ring(near_unit, -k) for k in OFFSETS[1:]]
    late_parts = (up(late_same), up_swapped(late_cross))
    near_pieces, late_parts, (q_same, q_cross) = lax.optimization_barrier(
        (near_pieces, late_parts, (q_same, q_cross))
    )
    near_row = jnp.concatenate([near_unit] + near_pieces)
    near = {0: [near_row], -1: [second_ring(near_row, 1)], 1: [second_ring(near_row, -1)]}

    late_parts, q_same, q_cross = ordered((late_parts, q_same, q_cross), near_row)
    late_unit = unit_of(*late_parts)
    late_q = (up(q_same), up_swapped(q_cross))
    late_mate = first_exchange(late_unit)
    near_sum = stage((0,), False, scalars, ordered(near_q, late_unit), near)
    late_pair = jnp.concatenate([late_unit, ordered(late_mate, near_sum)])
    late_others = second_exchange(late_pair)
    late_stream = up(ordered(late_stream, near_sum))
    near[-1] = ordered(near[-1], near_sum)
    near[2] = [second_ring(near[-1][0], 1)]
    near_sum = stage((-1, 1), False, scalars, ordered(near_q, late_q, late_pair), near, near_sum)
    late_row = jnp.concatenate([late_pair, ordered(late_others, near_sum)])
    late = {0: [late_row], -1: [second_ring(late_row, 1)], 1: [second_ring(late_row, -1)]}
    own, other = stage((2,), True, scalars, ordered(near_q, late_row, late_stream), near, near_sum)
    late[1] = ordered(late[1], own)
    late[2] = [second_ring(late[1][0], -1)]

    def added(own, other, base):
        received = swapped(other)
        both = jnp.where(
            core == 0, jnp.concatenate([own, received], 1), jnp.concatenate([received, own], 1)
        )
        return (base.astype(jnp.float32) + both.astype(jnp.float32)).astype(jnp.bfloat16)

    near_done = added(own, other, stream[0, :, : 2 * width])
    near_out = up(near_done)
    late_sum = stage((0, -1, 1), False, scalars, ordered(late_q, near_done), late, paired=True)
    late_sum, near_out = lax.optimization_barrier((late_sum, near_out))
    own, other = stage((2,), True, scalars, late_q, late, late_sum, paired=True)
    late_out = added(own, other, late_stream)
    return jnp.concatenate([near_out, late_out], 1)[None]


def solution(mesh):
    return jax.shard_map(
        shards,
        mesh=mesh,
        in_specs=(
            P("section", "seq", None),
            P("section", "seq", None),
            P("section", None, "seq", None),
            P("section", None, "seq", None),
            P(),
            P(),
            P(),
        ),
        out_specs=P("section", "seq", None),
        check_vma=False,
    )
```

```python
import functools
import math

import jax
import jax.numpy as jnp
from jax import lax
from jax.experimental import pallas as pl
from jax.experimental.pallas import tpu as pltpu
from jax.sharding import PartitionSpec as P

DIM = 128
GROUP = 8
TOK = 128
SLOTS = 128
LIVE = 80
SHARDS = 32
CACHE = SLOTS * SHARDS
ROWS = GROUP * TOK
PER = 4
SPAN_ROWS = PER * 2 * TOK
CACHE_ROWS = PER * 2 * LIVE
PAIR = 2 * (TOK + LIVE)
CHUNK = SPAN_ROWS + CACHE_ROWS
BLOCK = 128
TILE_BLOCKS = 8
SUB = 256
OFFSETS = (0, -1, 1, 2)
TO_LOG2 = math.log2(math.e) / math.sqrt(DIM)
LEAST_TOTAL, MOST_TOTAL = 1e-12, 1e30
LEAST_MIXED, MOST_MIXED = 1e-20, 1e37
AXES = ("section", "seq")


def moved(value, rule):
    pairs = []
    for y in range(4):
        for z in range(4):
            for x in range(4):
                for c in range(2):
                    ty, tz, tx, tc = rule(y, z, x, c)
                    source = y * 32 + (z * 4 + x) * 2 + c
                    target = (ty % 4) * 32 + ((tz % 4) * 4 + tx % 4) * 2 + tc
                    pairs.append((source, target))
    return lax.ppermute(value, AXES, pairs)


def swapped(value):
    return moved(value, lambda y, z, x, c: (y, z, x, 1 - c))


def up(value):
    return moved(value, lambda y, z, x, c: (y + 1, z, x, c))


def up_swapped(value):
    return moved(value, lambda y, z, x, c: (y + 1, z, x, 1 - c))


def first_ring(value, k):
    return moved(value, lambda y, z, x, c: (y, z, x + k, c) if c == 0 else (y, z + k, x, c))


def second_ring(value, k):
    return moved(value, lambda y, z, x, c: (y, z + k, x, c) if c == 0 else (y, z, x + k, c))


def own_place():
    seq = lax.axis_index("seq")
    return seq >> 3, (seq >> 1) & 3, seq & 1


def first_exchange(value):
    return moved(value, lambda y, z, x, c: (y, z, x ^ 1, c) if c == 0 else (y, z ^ 1, x, c))


def second_exchange(value):
    return moved(value, lambda y, z, x, c: (y, z, 3 - x, c) if c == 0 else (y, 3 - z, x, c))


def chip_of(place, row, col):
    z, x, c = place
    dz = jnp.where(c == 0, row, col)
    dx = jnp.where(c == 0, col, row)
    return ((z + dz + 4) % 4) * 4 + (x + dx + 4) % 4


def stage_kernel(rows_of, pieces, has_carry, last, paired, *refs):
    refs = list(refs)
    table_ref, len_ref, start_ref = refs[:3]
    q_refs, refs = refs[3:5], refs[5:]
    chunk_refs = []
    for part in pieces:
        chunk_refs.append(refs[: len(part)])
        refs = refs[len(part) :]
    carry_ref = None
    if has_carry:
        carry_ref, refs = refs[0], refs[1:]
    all_refs = []
    if last:
        for part in last:
            all_refs.append(refs[: len(part)])
            refs = refs[len(part) :]
    if last:
        out_refs, refs = refs[:2], refs[2:]
    total_ref, keys, values, todo, asked, arrived = refs[:6]
    count = len(rows_of)
    place = own_place()
    core = place[2]
    chip = place[0] * 4 + place[1]
    first_open = CACHE - start_ref[0]

    sign = 1
    if paired:
        sign = 2 * (jnp.where(core == 0, place[1], place[0]) & 1) - 1

    def shard_at(row, k, e):
        step = OFFSETS[k] * sign if k in (1, 2) else OFFSETS[k]
        return 2 * chip_of(place, row, step) + (core if e == 0 else 1 - core)

    fetches = []
    for q in range(2):
        rows = pl.ds(q_refs[q].shape[0] - ROWS, ROWS)
        fetches.append(pltpu.make_async_copy(q_refs[q].at[rows, :], asked.at[q], arrived.at[q]))
        fetches[q].start()

    for n in range(count):
        base = n * CHUNK
        values[base : base + SPAN_ROWS, DIM:] = jnp.ones((SPAN_ROWS, DIM), jnp.bfloat16)
        i = 0
        for ref, units in zip(chunk_refs[n], pieces[n]):
            for u in range(units):
                spot = base + i * TOK
                keys[spot : spot + TOK, :] = ref[u, 0, :TOK, :]
                values[spot : spot + TOK, :DIM] = ref[u, 1, :TOK, :]
                shard = shard_at(rows_of[n], i // 2, i % 2)
                low = first_open - shard * SLOTS
                slot = lax.broadcasted_iota(jnp.int32, (LIVE, DIM), 0)
                live = (slot >= low) & (slot < len_ref[shard])
                spot = base + SPAN_ROWS + i * LIVE
                keys[spot : spot + LIVE, :] = ref[u, 0, TOK:, :]
                piece = ref[u, 1, TOK:, :].astype(jnp.float32)
                values[spot : spot + LIVE, :DIM] = jnp.where(live, piece, 0.0).astype(jnp.bfloat16)
                values[spot : spot + LIVE, DIM:] = jnp.where(live, 1.0, 0.0).astype(jnp.bfloat16)
                i += 1
    spare = count * CHUNK
    keys[spare : spare + BLOCK, :] = jnp.zeros((BLOCK, DIM), jnp.bfloat16)
    values[spare : spare + BLOCK, :] = jnp.zeros((BLOCK, 2 * DIM), jnp.bfloat16)

    for q in range(2):
        mine = 2 * chip + (core if q == 0 else 1 - core)
        queries = asked.at[q]
        fetches[q].wait()

        filled = jnp.int32(0)
        if rows_of[0] == 0:
            todo[0] = q * TOK
            filled = jnp.int32(1)
        for n in range(count):
            seen = []
            for k in range(PER):
                for e in range(2):
                    shard = shard_at(rows_of[n], k, e)
                    wanted = (shard < mine) & (table_ref[mine, shard] == 1)
                    todo[filled] = n * CHUNK + (2 * k + e) * TOK
                    filled = filled + jnp.where(wanted, 1, 0)
                    seen.append(shard * SLOTS + len_ref[shard] > first_open)
            for b in range(CACHE_ROWS // BLOCK):
                wanted = functools.reduce(
                    jnp.logical_or, seen[b * BLOCK // LIVE : ((b + 1) * BLOCK - 1) // LIVE + 1]
                )
                todo[filled] = n * CHUNK + SPAN_ROWS + b * BLOCK
                filled = filled + jnp.where(wanted, 1, 0)
        for b in range(TILE_BLOCKS - 1):
            todo[filled + b] = spare

        def scores_of(first, rows):
            return lax.dot_general(
                queries[first : first + SUB, :], rows, (((1,), (1,)), ((), ())),
                preferred_element_type=jnp.float32,
            )

        def mix(weights, rows):
            return jnp.dot(weights.astype(jnp.bfloat16), rows, preferred_element_type=jnp.float32)

        def tile(blocks, begin, opening=False):
            spots = [pl.multiple_of(todo[begin + b], BLOCK) for b in range(blocks)]
            key_rows = jnp.concatenate([keys[pl.ds(s, BLOCK), :] for s in spots], 0)
            value_rows = jnp.concatenate([values[pl.ds(s, BLOCK), :] for s in spots], 0)

            def finish(first, scores):
                weights = jnp.exp2(scores * TO_LOG2)
                if opening:
                    token = lax.broadcasted_iota(jnp.int32, (TOK, TOK), 0)
                    key = lax.broadcasted_iota(jnp.int32, (TOK, TOK), 1)
                    own = weights[:, :TOK].reshape(SUB // TOK, TOK, TOK)
                    own = jnp.where((key <= token)[None], own, 0.0).reshape(SUB, TOK)
                    weights = jnp.concatenate([own, weights[:, TOK:]], 1)
                    total_ref[q, first : first + SUB, :] = mix(weights, value_rows)
                else:
                    total_ref[q, first : first + SUB, :] += mix(weights, value_rows)

            held = None
            for first in range(0, ROWS, SUB):
                scores = scores_of(first, key_rows)
                if held is not None:
                    finish(*held)
                held = (first, scores)
            finish(*held)

        begin = 0
        if rows_of[0] == 0:
            tile(TILE_BLOCKS, 0, opening=True)
            begin = TILE_BLOCKS
            filled = jnp.maximum(filled - TILE_BLOCKS, 0)
        else:
            total_ref[q] = carry_ref[q]

        whole = (filled + 1) // TILE_BLOCKS
        rest = filled - whole * TILE_BLOCKS

        def whole_tile(step, _):
            tile(TILE_BLOCKS, begin + step * TILE_BLOCKS)
            return 0

        lax.fori_loop(0, whole, whole_tile, 0)

        @pl.when(rest > 2)
        def _():
            tile(4, begin + whole * TILE_BLOCKS)

        left = jnp.where(rest > 2, rest - 4, rest)

        @pl.when(left > 0)
        def _():
            tile(2, begin + filled - left)

    if last:
        held, top = refs[6:]
        strange = jnp.zeros((TOK, DIM), jnp.float32)

        def write_out(q):
            for h in range(GROUP):
                mixed = total_ref[q, h * TOK : (h + 1) * TOK, :DIM]
                total = total_ref[q, h * TOK : (h + 1) * TOK, DIM:]
                out_refs[q][:, h * DIM : (h + 1) * DIM] = (mixed / total).astype(jnp.bfloat16)

        largest = []
        for q in range(2):
            write_out(q)
            most = jnp.zeros((TOK, DIM), jnp.float32)
            for h in range(GROUP):
                mixed = jnp.abs(total_ref[q, h * TOK : (h + 1) * TOK, :DIM])
                total = total_ref[q, h * TOK : (h + 1) * TOK, DIM:]
                good = (total >= LEAST_TOTAL) & (total <= MOST_TOTAL) & (mixed <= MOST_MIXED)
                strange = jnp.where(good, strange, 1.0)
                most = jnp.maximum(most, mixed)
            largest.append(jnp.max(most))
        fine = (jnp.max(strange) == 0.0) & (largest[0] >= LEAST_MIXED) & (largest[1] >= LEAST_MIXED)

        @pl.when(jnp.logical_not(fine))
        def _():
            for q in range(2):
                mine = 2 * chip + (core if q == 0 else 1 - core)
                careful(q, mine, place, sign, first_open, table_ref, len_ref, last, all_refs,
                        asked.at[q], total_ref, held, top)
                write_out(q)


def careful(q, mine, place, sign, first_open, table_ref, len_ref, parts, all_refs, queries, total_ref, held, top):
    core = place[2]
    total_ref[q] = jnp.zeros((ROWS, 2 * DIM), jnp.float32)
    top[...] = jnp.full((ROWS, DIM), -jnp.inf, jnp.float32)

    def add(keys, values, is_open):
        extent = keys.shape[0]

        def head(h, _):
            rows = pl.ds(pl.multiple_of(h * TOK, TOK), TOK)
            scores = lax.dot_general(
                queries[rows, :], keys, (((1,), (1,)), ((), ())), preferred_element_type=jnp.float32
            ) * (1.0 / math.sqrt(DIM))
            before = top[rows, :]
            highest = jnp.max(jnp.where(is_open, scores, -jnp.inf), -1, keepdims=True)
            after = jnp.maximum(before, highest)
            shift = jnp.where(after == -jnp.inf, 0.0, after)
            factor = jnp.exp(before - shift)
            weights = jnp.exp(jnp.minimum(scores - shift[:, :extent], 0.0))
            weights = jnp.where(is_open, weights, 0.0)
            mixed = jnp.dot(weights.astype(jnp.bfloat16), values, preferred_element_type=jnp.float32)
            total_ref[q, rows, :DIM] = total_ref[q, rows, :DIM] * factor + mixed
            total_ref[q, rows, DIM:] = total_ref[q, rows, DIM:] * factor + jnp.sum(weights, -1, keepdims=True)
            top[rows, :] = after
            return 0

        lax.fori_loop(0, GROUP, head, 0)

    for n, row in enumerate(OFFSETS):
        begin = 0
        for ref, units in zip(all_refs[n], parts[n]):

            def unit(u, _, ref=ref, row=row, begin=begin):
                pltpu.sync_copy(ref.at[u], held)
                k, e = (begin + u) >> 1, (begin + u) & 1
                there = chip_of(place, row, jnp.where(k == 3, 2, jnp.where(k < 2, -k, k - 1) * sign))
                shard = 2 * there + jnp.where(e == 0, core, 1 - core)
                token = lax.broadcasted_iota(jnp.int32, (TOK, TOK), 0)
                key = lax.broadcasted_iota(jnp.int32, (TOK, TOK), 1)
                reach = jnp.where(shard < mine, TOK, jnp.where(shard == mine, 0, -2 * TOK))
                reach = jnp.where(table_ref[mine, shard] == 1, reach, -2 * TOK)
                add(held[0, :TOK, :], held[1, :TOK, :], key <= token + reach)
                slot = lax.broadcasted_iota(jnp.int32, (TOK, LIVE), 1)
                live = (slot >= first_open - shard * SLOTS) & (slot < len_ref[shard])
                add(held[0, TOK:, :], held[1, TOK:, :], live)
                return 0

            lax.fori_loop(0, units, unit, 0)
            begin += units


def stage(rows_of, last, scalars, queries, chunks, carry=None, paired=False):
    smem = pl.BlockSpec(memory_space=pltpu.SMEM)
    vmem = pl.BlockSpec(memory_space=pltpu.VMEM)
    anywhere = pl.BlockSpec(memory_space=pl.ANY)
    operands = list(scalars) + list(queries)
    pieces = []
    for row in rows_of:
        operands += chunks[row]
        pieces.append(tuple(part.shape[0] for part in chunks[row]))
    if carry is not None:
        operands.append(carry)
    specs = [smem] * 3 + [pl.BlockSpec(memory_space=pltpu.HBM)] * 2 + [vmem] * (len(operands) - 5)
    every = None
    if last:
        every = []
        for row in OFFSETS:
            operands += chunks[row]
            every.append(tuple(part.shape[0] for part in chunks[row]))
        every = tuple(every)
    specs += [anywhere] * (len(operands) - len(specs))
    count = len(rows_of)
    total = ((2, ROWS, 2 * DIM), jnp.float32)
    scratch = [
        pltpu.VMEM((count * CHUNK + BLOCK, DIM), jnp.bfloat16),
        pltpu.VMEM((count * CHUNK + BLOCK, 2 * DIM), jnp.bfloat16),
        pltpu.SMEM((count * (PER * 2 + CACHE_ROWS // BLOCK) + TILE_BLOCKS + 1,), jnp.int32),
        pltpu.VMEM((2, ROWS, DIM), jnp.bfloat16),
        pltpu.SemaphoreType.DMA((2,)),
    ]
    if last:
        out_shape = (jax.ShapeDtypeStruct((TOK, GROUP * DIM), jnp.bfloat16),) * 2
        out_specs = (vmem, vmem)
        scratch = [pltpu.VMEM(*total)] + scratch + [
            pltpu.VMEM((2, TOK + LIVE, DIM), jnp.bfloat16),
            pltpu.VMEM((ROWS, DIM), jnp.float32),
        ]
    else:
        out_shape = jax.ShapeDtypeStruct(*total)
        out_specs = vmem
    return pl.pallas_call(
        functools.partial(stage_kernel, tuple(rows_of), tuple(pieces), carry is not None, every, paired),
        out_shape=out_shape,
        in_specs=specs,
        out_specs=out_specs,
        scratch_shapes=scratch,
        compiler_params=pltpu.CompilerParams(vmem_limit_bytes=40 * 1024 * 1024),
        cost_estimate=pl.CostEstimate(
            flops=count * 2 * ROWS * CHUNK * DIM * 6,
            bytes_accessed=count * CHUNK * DIM * 4,
            transcendentals=count * 2 * ROWS * CHUNK,
        ),
        name="stage_" + "_".join(str(r % 4) for r in rows_of),
    )(*operands)


def ordered(value, *after):
    return lax.optimization_barrier((value, after))[0]


def pairs_at(span_ref, cache_ref, head, out):
    columns = pl.ds(pl.multiple_of(head * DIM, DIM), DIM)
    for i in range(2):
        begin = i * (TOK + LIVE)
        out[begin : begin + TOK, :] = span_ref[i, :, columns]
        out[begin + TOK : begin + TOK + LIVE, :] = cache_ref[i, :LIVE, columns]


def queries_at(queries_ref, head, out, at):
    for h in range(GROUP):
        columns = pl.ds(pl.multiple_of((head * GROUP + h) * DIM, DIM), DIM)
        out[at + h * TOK : at + (h + 1) * TOK, :] = queries_ref[:, columns]


def near_kernel(span_ref, cache_ref, queries_ref, own, own_q, pack, same, cross):
    core = own_place()[2]
    for head, out in ((core, own), (1 - core, pack), (2 + core, same), (3 - core, cross)):
        pairs_at(span_ref, cache_ref, head, out)
    queries_at(queries_ref, core, own_q, 0)
    queries_at(queries_ref, 1 - core, pack, PAIR)


def late_kernel(queries_ref, stream_ref, same_q, cross_q, late_stream):
    core = own_place()[2]
    queries_at(queries_ref, core, same_q, 0)
    queries_at(queries_ref, 1 - core, cross_q, 0)
    late_stream[...] = stream_ref[...]


def cut(kernel, operands, specs, shapes):
    whole = lambda shape: pl.BlockSpec(shape, lambda i: (0,) * len(shape))
    return pl.pallas_call(
        kernel,
        grid=(1,),
        out_shape=tuple(jax.ShapeDtypeStruct(shape, jnp.bfloat16) for shape in shapes),
        in_specs=specs,
        out_specs=tuple(whole(shape) for shape in shapes),
        cost_estimate=pl.CostEstimate(flops=0, bytes_accessed=8 * 1024 * 1024, transcendentals=0),
        name=kernel.__name__,
    )(*operands)


def unit_of(first, second):
    return jnp.concatenate([first[:PAIR], second[:PAIR]]).reshape(2, 2, TOK + LIVE, DIM)


def shards(stream, queries, span_kv, cache_kv, cache_len, context_start, block_table):
    core = lax.axis_index("seq") % 2
    scalars = (block_table, cache_len, context_start)
    width = GROUP * DIM

    half = 2 * width
    left = pl.BlockSpec((TOK, half), lambda i: (0, 0))
    right = pl.BlockSpec((TOK, half), lambda i: (0, 1))
    mine, q_mine, theirs, late_same, late_cross = cut(
        near_kernel,
        (span_kv[0], cache_kv[0], queries[0]),
        [pl.BlockSpec((2, TOK, 4 * DIM), lambda i: (0, 0, 0))] * 2 + [left],
        [(PAIR, DIM), (ROWS, DIM), (PAIR + ROWS, DIM)] + [(PAIR, DIM)] * 2,
    )
    received = swapped(theirs)
    near_unit = unit_of(mine, received)
    near_q = (q_mine, received)
    late_queries, late_base = ordered((queries[0], stream[0]), near_unit)
    q_same, q_cross, late_stream = cut(
        late_kernel, (late_queries, late_base), [right, right], [(ROWS, DIM)] * 2 + [(TOK, half)]
    )
    near_pieces = [first_ring(near_unit, -k) for k in OFFSETS[1:]]
    late_parts = (up(late_same), up_swapped(late_cross))
    near_pieces, late_parts, (q_same, q_cross) = lax.optimization_barrier(
        (near_pieces, late_parts, (q_same, q_cross))
    )
    near_row = jnp.concatenate([near_unit] + near_pieces)
    near = {0: [near_row], -1: [second_ring(near_row, 1)], 1: [second_ring(near_row, -1)]}

    late_parts, q_same = ordered((late_parts, q_same), near_row)
    late_unit = unit_of(*late_parts)
    q_same = up(q_same)
    late_mate = first_exchange(late_unit)
    near_sum = stage((0,), False, scalars, ordered(near_q, late_unit), near)
    late_pair = jnp.concatenate([late_unit, ordered(late_mate, near_sum)])
    late_others = second_exchange(late_pair)
    q_cross, late_stream = ordered((q_cross, late_stream), near_sum)
    q_cross, late_stream = up_swapped(q_cross), up(late_stream)
    late_q = (q_same, q_cross)
    near[-1] = ordered(near[-1], near_sum)
    near[2] = [second_ring(near[-1][0], 1)]
    near_sum = stage((-1, 1), False, scalars, ordered(near_q, late_pair, q_same), near, near_sum)
    late_row = jnp.concatenate([late_pair, ordered(late_others, near_sum)])
    late = {0: [late_row], -1: [second_ring(late_row, 1)], 1: [second_ring(late_row, -1)]}
    own, other = stage((2,), True, scalars, ordered(near_q, late_row, late_stream, q_cross), near, near_sum)
    late[1] = ordered(late[1], own)
    late[2] = [second_ring(late[1][0], -1)]

    def added(own, other, base):
        received = swapped(other)
        both = jnp.where(
            core == 0, jnp.concatenate([own, received], 1), jnp.concatenate([received, own], 1)
        )
        return (base.astype(jnp.float32) + both.astype(jnp.float32)).astype(jnp.bfloat16)

    near_done = added(own, other, stream[0, :, : 2 * width])
    near_out = up(near_done)
    late_sum = stage((0, -1, 1), False, scalars, ordered(late_q, near_done), late, paired=True)
    late_sum, near_out = lax.optimization_barrier((late_sum, near_out))
    own, other = stage((2,), True, scalars, late_q, late, late_sum, paired=True)
    late_out = added(own, other, late_stream)
    return jnp.concatenate([near_out, late_out], 1)[None]


def solution(mesh):
    return jax.shard_map(
        shards,
        mesh=mesh,
        in_specs=(
            P("section", "seq", None),
            P("section", "seq", None),
            P("section", None, "seq", None),
            P("section", None, "seq", None),
            P(),
            P(),
            P(),
        ),
        out_specs=P("section", "seq", None),
        check_vma=False,
    )
```

```python
import functools
import math

import jax
import jax.numpy as jnp
from jax import lax
from jax.experimental import pallas as pl
from jax.experimental.pallas import tpu as pltpu
from jax.sharding import PartitionSpec as P

DIM = 128
GROUP = 8
TOK = 128
SLOTS = 128
LIVE = 80
SHARDS = 32
CACHE = SLOTS * SHARDS
ROWS = GROUP * TOK
PER = 4
SPAN_ROWS = PER * 2 * TOK
CACHE_ROWS = PER * 2 * LIVE
PAIR = 2 * (TOK + LIVE)
CHUNK = SPAN_ROWS + CACHE_ROWS
BLOCK = 128
TILE_BLOCKS = 8
SUB = 256
OFFSETS = (0, -1, 1, 2)
TO_LOG2 = math.log2(math.e) / math.sqrt(DIM)
LEAST_TOTAL, MOST_TOTAL = 1e-12, 1e30
LEAST_MIXED, MOST_MIXED = 1e-20, 1e37
AXES = ("section", "seq")


def moved(value, rule):
    pairs = []
    for y in range(4):
        for z in range(4):
            for x in range(4):
                for c in range(2):
                    ty, tz, tx, tc = rule(y, z, x, c)
                    source = y * 32 + (z * 4 + x) * 2 + c
                    target = (ty % 4) * 32 + ((tz % 4) * 4 + tx % 4) * 2 + tc
                    pairs.append((source, target))
    return lax.ppermute(value, AXES, pairs)


def swapped(value):
    return moved(value, lambda y, z, x, c: (y, z, x, 1 - c))


def up(value):
    return moved(value, lambda y, z, x, c: (y + 1, z, x, c))


def up_swapped(value):
    return moved(value, lambda y, z, x, c: (y + 1, z, x, 1 - c))


def first_ring(value, k):
    return moved(value, lambda y, z, x, c: (y, z, x + k, c) if c == 0 else (y, z + k, x, c))


def second_ring(value, k):
    return moved(value, lambda y, z, x, c: (y, z + k, x, c) if c == 0 else (y, z, x + k, c))


def own_place():
    seq = lax.axis_index("seq")
    return seq >> 3, (seq >> 1) & 3, seq & 1


def first_exchange(value):
    return moved(value, lambda y, z, x, c: (y, z, x ^ 1, c) if c == 0 else (y, z ^ 1, x, c))


def second_exchange(value):
    return moved(value, lambda y, z, x, c: (y, z, 3 - x, c) if c == 0 else (y, 3 - z, x, c))


def chip_of(place, row, col):
    z, x, c = place
    dz = jnp.where(c == 0, row, col)
    dx = jnp.where(c == 0, col, row)
    return ((z + dz + 4) % 4) * 4 + (x + dx + 4) % 4


def stage_kernel(rows_of, pieces, has_carry, last, paired, *refs):
    refs = list(refs)
    table_ref, len_ref, start_ref = refs[:3]
    q_refs, refs = refs[3:5], refs[5:]
    chunk_refs = []
    for part in pieces:
        chunk_refs.append(refs[: len(part)])
        refs = refs[len(part) :]
    carry_ref = None
    if has_carry:
        carry_ref, refs = refs[0], refs[1:]
    all_refs = []
    if last:
        for part in last:
            all_refs.append(refs[: len(part)])
            refs = refs[len(part) :]
    if last:
        out_refs, refs = refs[:2], refs[2:]
    total_ref, keys, values, todo, asked, arrived = refs[:6]
    count = len(rows_of)
    place = own_place()
    core = place[2]
    chip = place[0] * 4 + place[1]
    first_open = CACHE - start_ref[0]

    sign = 1
    if paired:
        sign = 2 * (jnp.where(core == 0, place[1], place[0]) & 1) - 1

    def shard_at(row, k, e):
        step = OFFSETS[k] * sign if k in (1, 2) else OFFSETS[k]
        return 2 * chip_of(place, row, step) + (core if e == 0 else 1 - core)

    fetches = []
    for q in range(2):
        rows = pl.ds(q_refs[q].shape[0] - ROWS, ROWS)
        fetches.append(pltpu.make_async_copy(q_refs[q].at[rows, :], asked.at[q], arrived.at[q]))
        fetches[q].start()

    for n in range(count):
        base = n * CHUNK
        values[base : base + SPAN_ROWS, DIM:] = jnp.ones((SPAN_ROWS, DIM), jnp.bfloat16)
        i = 0
        for ref, units in zip(chunk_refs[n], pieces[n]):
            for u in range(units):
                spot = base + i * TOK
                keys[spot : spot + TOK, :] = ref[u, 0, :TOK, :]
                values[spot : spot + TOK, :DIM] = ref[u, 1, :TOK, :]
                shard = shard_at(rows_of[n], i // 2, i % 2)
                low = first_open - shard * SLOTS
                slot = lax.broadcasted_iota(jnp.int32, (LIVE, DIM), 0)
                live = (slot >= low) & (slot < len_ref[shard])
                spot = base + SPAN_ROWS + i * LIVE
                keys[spot : spot + LIVE, :] = ref[u, 0, TOK:, :]
                piece = ref[u, 1, TOK:, :].astype(jnp.float32)
                values[spot : spot + LIVE, :DIM] = jnp.where(live, piece, 0.0).astype(jnp.bfloat16)
                values[spot : spot + LIVE, DIM:] = jnp.where(live, 1.0, 0.0).astype(jnp.bfloat16)
                i += 1
    spare = count * CHUNK
    keys[spare : spare + BLOCK, :] = jnp.zeros((BLOCK, DIM), jnp.bfloat16)
    values[spare : spare + BLOCK, :] = jnp.zeros((BLOCK, 2 * DIM), jnp.bfloat16)

    for q in range(2):
        mine = 2 * chip + (core if q == 0 else 1 - core)
        queries = asked.at[q]
        fetches[q].wait()

        filled = jnp.int32(0)
        if rows_of[0] == 0:
            todo[0] = q * TOK
            filled = jnp.int32(1)
        for n in range(count):
            seen = []
            for k in range(PER):
                for e in range(2):
                    shard = shard_at(rows_of[n], k, e)
                    wanted = (shard < mine) & (table_ref[mine, shard] == 1)
                    todo[filled] = n * CHUNK + (2 * k + e) * TOK
                    filled = filled + jnp.where(wanted, 1, 0)
                    seen.append(shard * SLOTS + len_ref[shard] > first_open)
            for b in range(CACHE_ROWS // BLOCK):
                wanted = functools.reduce(
                    jnp.logical_or, seen[b * BLOCK // LIVE : ((b + 1) * BLOCK - 1) // LIVE + 1]
                )
                todo[filled] = n * CHUNK + SPAN_ROWS + b * BLOCK
                filled = filled + jnp.where(wanted, 1, 0)
        for b in range(TILE_BLOCKS - 1):
            todo[filled + b] = spare

        def scores_of(first, rows):
            return lax.dot_general(
                queries[first : first + SUB, :], rows, (((1,), (1,)), ((), ())),
                preferred_element_type=jnp.float32,
            )

        def mix(weights, rows):
            return jnp.dot(weights.astype(jnp.bfloat16), rows, preferred_element_type=jnp.float32)

        def tile(blocks, begin, opening=False):
            spots = [pl.multiple_of(todo[begin + b], BLOCK) for b in range(blocks)]
            key_rows = jnp.concatenate([keys[pl.ds(s, BLOCK), :] for s in spots], 0)
            value_rows = jnp.concatenate([values[pl.ds(s, BLOCK), :] for s in spots], 0)

            def finish(first, scores):
                weights = jnp.exp2(scores * TO_LOG2)
                if opening:
                    token = lax.broadcasted_iota(jnp.int32, (TOK, TOK), 0)
                    key = lax.broadcasted_iota(jnp.int32, (TOK, TOK), 1)
                    own = weights[:, :TOK].reshape(SUB // TOK, TOK, TOK)
                    own = jnp.where((key <= token)[None], own, 0.0).reshape(SUB, TOK)
                    weights = jnp.concatenate([own, weights[:, TOK:]], 1)
                    total_ref[q, first : first + SUB, :] = mix(weights, value_rows)
                else:
                    total_ref[q, first : first + SUB, :] += mix(weights, value_rows)

            held = None
            for first in range(0, ROWS, SUB):
                scores = scores_of(first, key_rows)
                if held is not None:
                    finish(*held)
                held = (first, scores)
            finish(*held)

        begin = 0
        if rows_of[0] == 0:
            tile(TILE_BLOCKS, 0, opening=True)
            begin = TILE_BLOCKS
            filled = jnp.maximum(filled - TILE_BLOCKS, 0)
        else:
            total_ref[q] = carry_ref[q]

        whole = (filled + 1) // TILE_BLOCKS
        rest = filled - whole * TILE_BLOCKS

        def whole_tile(step, _):
            tile(TILE_BLOCKS, begin + step * TILE_BLOCKS)
            return 0

        lax.fori_loop(0, whole, whole_tile, 0)

        @pl.when(rest > 2)
        def _():
            tile(4, begin + whole * TILE_BLOCKS)

        left = jnp.where(rest > 2, rest - 4, rest)

        @pl.when(left > 0)
        def _():
            tile(2, begin + filled - left)

    if last:
        held, top = refs[6:]
        strange = jnp.zeros((TOK, DIM), jnp.float32)

        def write_out(q):
            for h in range(GROUP):
                mixed = total_ref[q, h * TOK : (h + 1) * TOK, :DIM]
                total = total_ref[q, h * TOK : (h + 1) * TOK, DIM:]
                out_refs[q][:, h * DIM : (h + 1) * DIM] = (mixed / total).astype(jnp.bfloat16)

        largest = []
        for q in range(2):
            write_out(q)
            most = jnp.zeros((TOK, DIM), jnp.float32)
            for h in range(GROUP):
                mixed = jnp.abs(total_ref[q, h * TOK : (h + 1) * TOK, :DIM])
                total = total_ref[q, h * TOK : (h + 1) * TOK, DIM:]
                good = (total >= LEAST_TOTAL) & (total <= MOST_TOTAL) & (mixed <= MOST_MIXED)
                strange = jnp.where(good, strange, 1.0)
                most = jnp.maximum(most, mixed)
            largest.append(jnp.max(most))
        fine = (jnp.max(strange) == 0.0) & (largest[0] >= LEAST_MIXED) & (largest[1] >= LEAST_MIXED)

        @pl.when(jnp.logical_not(fine))
        def _():
            for q in range(2):
                mine = 2 * chip + (core if q == 0 else 1 - core)
                careful(q, mine, place, sign, first_open, table_ref, len_ref, last, all_refs,
                        asked.at[q], total_ref, held, top)
                write_out(q)


def careful(q, mine, place, sign, first_open, table_ref, len_ref, parts, all_refs, queries, total_ref, held, top):
    core = place[2]
    total_ref[q] = jnp.zeros((ROWS, 2 * DIM), jnp.float32)
    top[...] = jnp.full((ROWS, DIM), -jnp.inf, jnp.float32)

    def add(keys, values, is_open):
        extent = keys.shape[0]

        def head(h, _):
            rows = pl.ds(pl.multiple_of(h * TOK, TOK), TOK)
            scores = lax.dot_general(
                queries[rows, :], keys, (((1,), (1,)), ((), ())), preferred_element_type=jnp.float32
            ) * (1.0 / math.sqrt(DIM))
            before = top[rows, :]
            highest = jnp.max(jnp.where(is_open, scores, -jnp.inf), -1, keepdims=True)
            after = jnp.maximum(before, highest)
            shift = jnp.where(after == -jnp.inf, 0.0, after)
            factor = jnp.exp(before - shift)
            weights = jnp.exp(jnp.minimum(scores - shift[:, :extent], 0.0))
            weights = jnp.where(is_open, weights, 0.0)
            mixed = jnp.dot(weights.astype(jnp.bfloat16), values, preferred_element_type=jnp.float32)
            total_ref[q, rows, :DIM] = total_ref[q, rows, :DIM] * factor + mixed
            total_ref[q, rows, DIM:] = total_ref[q, rows, DIM:] * factor + jnp.sum(weights, -1, keepdims=True)
            top[rows, :] = after
            return 0

        lax.fori_loop(0, GROUP, head, 0)

    for n, row in enumerate(OFFSETS):
        begin = 0
        for ref, units in zip(all_refs[n], parts[n]):

            def unit(u, _, ref=ref, row=row, begin=begin):
                pltpu.sync_copy(ref.at[u], held)
                k, e = (begin + u) >> 1, (begin + u) & 1
                there = chip_of(place, row, jnp.where(k == 3, 2, jnp.where(k < 2, -k, k - 1) * sign))
                shard = 2 * there + jnp.where(e == 0, core, 1 - core)
                token = lax.broadcasted_iota(jnp.int32, (TOK, TOK), 0)
                key = lax.broadcasted_iota(jnp.int32, (TOK, TOK), 1)
                reach = jnp.where(shard < mine, TOK, jnp.where(shard == mine, 0, -2 * TOK))
                reach = jnp.where(table_ref[mine, shard] == 1, reach, -2 * TOK)
                add(held[0, :TOK, :], held[1, :TOK, :], key <= token + reach)
                slot = lax.broadcasted_iota(jnp.int32, (TOK, LIVE), 1)
                live = (slot >= first_open - shard * SLOTS) & (slot < len_ref[shard])
                add(held[0, TOK:, :], held[1, TOK:, :], live)
                return 0

            lax.fori_loop(0, units, unit, 0)
            begin += units


def stage(rows_of, last, scalars, queries, chunks, carry=None, paired=False):
    smem = pl.BlockSpec(memory_space=pltpu.SMEM)
    vmem = pl.BlockSpec(memory_space=pltpu.VMEM)
    anywhere = pl.BlockSpec(memory_space=pl.ANY)
    operands = list(scalars) + list(queries)
    pieces = []
    for row in rows_of:
        operands += chunks[row]
        pieces.append(tuple(part.shape[0] for part in chunks[row]))
    if carry is not None:
        operands.append(carry)
    specs = [smem] * 3 + [pl.BlockSpec(memory_space=pltpu.HBM)] * 2 + [vmem] * (len(operands) - 5)
    every = None
    if last:
        every = []
        for row in OFFSETS:
            operands += chunks[row]
            every.append(tuple(part.shape[0] for part in chunks[row]))
        every = tuple(every)
    specs += [anywhere] * (len(operands) - len(specs))
    count = len(rows_of)
    total = ((2, ROWS, 2 * DIM), jnp.float32)
    scratch = [
        pltpu.VMEM((count * CHUNK + BLOCK, DIM), jnp.bfloat16),
        pltpu.VMEM((count * CHUNK + BLOCK, 2 * DIM), jnp.bfloat16),
        pltpu.SMEM((count * (PER * 2 + CACHE_ROWS // BLOCK) + TILE_BLOCKS + 1,), jnp.int32),
        pltpu.VMEM((2, ROWS, DIM), jnp.bfloat16),
        pltpu.SemaphoreType.DMA((2,)),
    ]
    if last:
        out_shape = (jax.ShapeDtypeStruct((TOK, GROUP * DIM), jnp.bfloat16),) * 2
        out_specs = (vmem, vmem)
        scratch = [pltpu.VMEM(*total)] + scratch + [
            pltpu.VMEM((2, TOK + LIVE, DIM), jnp.bfloat16),
            pltpu.VMEM((ROWS, DIM), jnp.float32),
        ]
    else:
        out_shape = jax.ShapeDtypeStruct(*total)
        out_specs = vmem
    return pl.pallas_call(
        functools.partial(stage_kernel, tuple(rows_of), tuple(pieces), carry is not None, every, paired),
        out_shape=out_shape,
        in_specs=specs,
        out_specs=out_specs,
        scratch_shapes=scratch,
        compiler_params=pltpu.CompilerParams(vmem_limit_bytes=24 * 1024 * 1024),
        cost_estimate=pl.CostEstimate(
            flops=count * 2 * ROWS * CHUNK * DIM * 6,
            bytes_accessed=count * CHUNK * DIM * 4,
            transcendentals=count * 2 * ROWS * CHUNK,
        ),
        name="stage_" + "_".join(str(r % 4) for r in rows_of),
    )(*operands)


def ordered(value, *after):
    return lax.optimization_barrier((value, after))[0]


def pairs_at(span_ref, cache_ref, head, out):
    columns = pl.ds(pl.multiple_of(head * DIM, DIM), DIM)
    for i in range(2):
        begin = i * (TOK + LIVE)
        out[begin : begin + TOK, :] = span_ref[i, :, columns]
        out[begin + TOK : begin + TOK + LIVE, :] = cache_ref[i, :LIVE, columns]


def queries_at(queries_ref, head, out, at):
    for h in range(GROUP):
        columns = pl.ds(pl.multiple_of((head * GROUP + h) * DIM, DIM), DIM)
        out[at + h * TOK : at + (h + 1) * TOK, :] = queries_ref[:, columns]


def near_kernel(span_ref, cache_ref, queries_ref, own, own_q, pack, same, cross):
    core = own_place()[2]
    for head, out in ((core, own), (1 - core, pack), (2 + core, same), (3 - core, cross)):
        pairs_at(span_ref, cache_ref, head, out)
    queries_at(queries_ref, core, own_q, 0)
    queries_at(queries_ref, 1 - core, pack, PAIR)


def late_kernel(queries_ref, stream_ref, same_q, cross_q, late_stream):
    core = own_place()[2]
    queries_at(queries_ref, core, same_q, 0)
    queries_at(queries_ref, 1 - core, cross_q, 0)
    late_stream[...] = stream_ref[...]


def cut(kernel, operands, specs, shapes):
    whole = lambda shape: pl.BlockSpec(shape, lambda i: (0,) * len(shape))
    return pl.pallas_call(
        kernel,
        grid=(1,),
        out_shape=tuple(jax.ShapeDtypeStruct(shape, jnp.bfloat16) for shape in shapes),
        in_specs=specs,
        out_specs=tuple(whole(shape) for shape in shapes),
        cost_estimate=pl.CostEstimate(flops=0, bytes_accessed=8 * 1024 * 1024, transcendentals=0),
        name=kernel.__name__,
    )(*operands)


def unit_of(first, second):
    return jnp.concatenate([first[:PAIR], second[:PAIR]]).reshape(2, 2, TOK + LIVE, DIM)


def shards(stream, queries, span_kv, cache_kv, cache_len, context_start, block_table):
    core = lax.axis_index("seq") % 2
    scalars = (block_table, cache_len, context_start)
    width = GROUP * DIM

    half = 2 * width
    left = pl.BlockSpec((TOK, half), lambda i: (0, 0))
    right = pl.BlockSpec((TOK, half), lambda i: (0, 1))
    mine, q_mine, theirs, late_same, late_cross = cut(
        near_kernel,
        (span_kv[0], cache_kv[0], queries[0]),
        [pl.BlockSpec((2, TOK, 4 * DIM), lambda i: (0, 0, 0))] * 2 + [left],
        [(PAIR, DIM), (ROWS, DIM), (PAIR + ROWS, DIM)] + [(PAIR, DIM)] * 2,
    )
    received = swapped(theirs)
    near_unit = unit_of(mine, received)
    near_q = (q_mine, received)
    late_queries, late_base = ordered((queries[0], stream[0]), near_unit)
    q_same, q_cross, late_stream = cut(
        late_kernel, (late_queries, late_base), [right, right], [(ROWS, DIM)] * 2 + [(TOK, half)]
    )
    near_pieces = [first_ring(near_unit, -k) for k in OFFSETS[1:]]
    late_parts = (up(late_same), up_swapped(late_cross))
    near_pieces, late_parts, (q_same, q_cross) = lax.optimization_barrier(
        (near_pieces, late_parts, (q_same, q_cross))
    )
    near_row = jnp.concatenate([near_unit] + near_pieces)
    near = {0: [near_row], -1: [second_ring(near_row, 1)], 1: [second_ring(near_row, -1)]}

    late_parts, q_same = ordered((late_parts, q_same), near_row)
    late_unit = unit_of(*late_parts)
    q_same = up(q_same)
    late_mate = first_exchange(late_unit)
    near_sum = stage((0,), False, scalars, ordered(near_q, late_unit), near)
    late_pair = jnp.concatenate([late_unit, ordered(late_mate, near_sum)])
    late_others = second_exchange(late_pair)
    q_cross = up_swapped(ordered(q_cross, near_sum))
    late_stream = up(ordered(late_stream, near_sum, q_same))
    late_q = (q_same, q_cross)
    near[-1] = ordered(near[-1], near_sum)
    near[2] = [second_ring(near[-1][0], 1)]
    near_sum = stage((-1, 1), False, scalars, ordered(near_q, late_pair, q_same), near, near_sum)
    late_row = jnp.concatenate([late_pair, ordered(late_others, near_sum, q_cross)])
    late = {0: [late_row], -1: [second_ring(late_row, 1)], 1: [second_ring(late_row, -1)]}
    own, other = stage((2,), True, scalars, ordered(near_q, late_row, late_stream, q_cross), near, near_sum)
    late[1] = ordered(late[1], own)
    late[2] = [second_ring(late[1][0], -1)]

    def added(own, other, base):
        received = swapped(other)
        both = jnp.where(
            core == 0, jnp.concatenate([own, received], 1), jnp.concatenate([received, own], 1)
        )
        return (base.astype(jnp.float32) + both.astype(jnp.float32)).astype(jnp.bfloat16)

    near_done = added(own, other, stream[0, :, : 2 * width])
    near_out = up(near_done)
    late_sum = stage((0, -1, 1), False, ordered(scalars, near_done), late_q, late, paired=True)
    late_sum, near_out = lax.optimization_barrier((late_sum, near_out))
    own, other = stage((2,), True, scalars, late_q, late, late_sum, paired=True)
    late_out = added(own, other, late_stream)
    return jnp.concatenate([near_out, late_out], 1)[None]


def solution(mesh):
    return jax.shard_map(
        shards,
        mesh=mesh,
        in_specs=(
            P("section", "seq", None),
            P("section", "seq", None),
            P("section", None, "seq", None),
            P("section", None, "seq", None),
            P(),
            P(),
            P(),
        ),
        out_specs=P("section", "seq", None),
        check_vma=False,
    )
```

```python
import functools
import math

import jax
import jax.numpy as jnp
from jax import lax
from jax.experimental import pallas as pl
from jax.experimental.pallas import tpu as pltpu
from jax.sharding import PartitionSpec as P

DIM = 128
GROUP = 8
TOK = 128
SLOTS = 128
LIVE = 80
SHARDS = 32
CACHE = SLOTS * SHARDS
ROWS = GROUP * TOK
PER = 4
SPAN_ROWS = PER * 2 * TOK
CACHE_ROWS = PER * 2 * LIVE
PAIR = 2 * (TOK + LIVE)
CHUNK = SPAN_ROWS + CACHE_ROWS
BLOCK = 128
TILE_BLOCKS = 8
SUB = 256
OFFSETS = (0, -1, 1, 2)
TO_LOG2 = math.log2(math.e) / math.sqrt(DIM)
LEAST_TOTAL, MOST_TOTAL = 1e-12, 1e30
LEAST_MIXED, MOST_MIXED = 1e-20, 1e37
AXES = ("section", "seq")


def moved(value, rule):
    pairs = []
    for y in range(4):
        for z in range(4):
            for x in range(4):
                for c in range(2):
                    ty, tz, tx, tc = rule(y, z, x, c)
                    source = y * 32 + (z * 4 + x) * 2 + c
                    target = (ty % 4) * 32 + ((tz % 4) * 4 + tx % 4) * 2 + tc
                    pairs.append((source, target))
    return lax.ppermute(value, AXES, pairs)


def swapped(value):
    return moved(value, lambda y, z, x, c: (y, z, x, 1 - c))


def up(value):
    return moved(value, lambda y, z, x, c: (y + 1, z, x, c))


def up_swapped(value):
    return moved(value, lambda y, z, x, c: (y + 1, z, x, 1 - c))


def first_ring(value, k):
    return moved(value, lambda y, z, x, c: (y, z, x + k, c) if c == 0 else (y, z + k, x, c))


def second_ring(value, k):
    return moved(value, lambda y, z, x, c: (y, z + k, x, c) if c == 0 else (y, z, x + k, c))


def own_place():
    seq = lax.axis_index("seq")
    return seq >> 3, (seq >> 1) & 3, seq & 1


def first_exchange(value):
    return moved(value, lambda y, z, x, c: (y, z, x ^ 1, c) if c == 0 else (y, z ^ 1, x, c))


def second_exchange(value):
    return moved(value, lambda y, z, x, c: (y, z, 3 - x, c) if c == 0 else (y, 3 - z, x, c))


def chip_of(place, row, col):
    z, x, c = place
    dz = jnp.where(c == 0, row, col)
    dx = jnp.where(c == 0, col, row)
    return ((z + dz + 4) % 4) * 4 + (x + dx + 4) % 4


def stage_kernel(rows_of, pieces, has_carry, last, paired, *refs):
    refs = list(refs)
    table_ref, len_ref, start_ref = refs[:3]
    q_refs, refs = refs[3:5], refs[5:]
    chunk_refs = []
    for part in pieces:
        chunk_refs.append(refs[: len(part)])
        refs = refs[len(part) :]
    carry_ref = None
    if has_carry:
        carry_ref, refs = refs[0], refs[1:]
    all_refs = []
    if last:
        for part in last:
            all_refs.append(refs[: len(part)])
            refs = refs[len(part) :]
    if last:
        out_refs, refs = refs[:2], refs[2:]
    total_ref, keys, values, todo, asked, arrived = refs[:6]
    count = len(rows_of)
    place = own_place()
    core = place[2]
    chip = place[0] * 4 + place[1]
    first_open = CACHE - start_ref[0]

    sign = 1
    if paired:
        sign = 2 * (jnp.where(core == 0, place[1], place[0]) & 1) - 1

    def shard_at(row, k, e):
        step = OFFSETS[k] * sign if k in (1, 2) else OFFSETS[k]
        return 2 * chip_of(place, row, step) + (core if e == 0 else 1 - core)

    fetches = []
    for q in range(2):
        rows = pl.ds(q_refs[q].shape[0] - ROWS, ROWS)
        fetches.append(pltpu.make_async_copy(q_refs[q].at[rows, :], asked.at[q], arrived.at[q]))
        fetches[q].start()

    for n in range(count):
        base = n * CHUNK
        values[base : base + SPAN_ROWS, DIM:] = jnp.ones((SPAN_ROWS, DIM), jnp.bfloat16)
        i = 0
        for ref, units in zip(chunk_refs[n], pieces[n]):
            for u in range(units):
                spot = base + i * TOK
                keys[spot : spot + TOK, :] = ref[u, 0, :TOK, :]
                values[spot : spot + TOK, :DIM] = ref[u, 1, :TOK, :]
                shard = shard_at(rows_of[n], i // 2, i % 2)
                low = first_open - shard * SLOTS
                slot = lax.broadcasted_iota(jnp.int32, (LIVE, DIM), 0)
                live = (slot >= low) & (slot < len_ref[shard])
                spot = base + SPAN_ROWS + i * LIVE
                keys[spot : spot + LIVE, :] = ref[u, 0, TOK:, :]
                piece = ref[u, 1, TOK:, :].astype(jnp.float32)
                values[spot : spot + LIVE, :DIM] = jnp.where(live, piece, 0.0).astype(jnp.bfloat16)
                values[spot : spot + LIVE, DIM:] = jnp.where(live, 1.0, 0.0).astype(jnp.bfloat16)
                i += 1
    spare = count * CHUNK
    keys[spare : spare + BLOCK, :] = jnp.zeros((BLOCK, DIM), jnp.bfloat16)
    values[spare : spare + BLOCK, :] = jnp.zeros((BLOCK, 2 * DIM), jnp.bfloat16)

    for q in range(2):
        mine = 2 * chip + (core if q == 0 else 1 - core)
        queries = asked.at[q]
        fetches[q].wait()

        filled = jnp.int32(0)
        if rows_of[0] == 0:
            todo[0] = q * TOK
            filled = jnp.int32(1)
        for n in range(count):
            seen = []
            for k in range(PER):
                for e in range(2):
                    shard = shard_at(rows_of[n], k, e)
                    wanted = (shard < mine) & (table_ref[mine, shard] == 1)
                    todo[filled] = n * CHUNK + (2 * k + e) * TOK
                    filled = filled + jnp.where(wanted, 1, 0)
                    seen.append(shard * SLOTS + len_ref[shard] > first_open)
            for b in range(CACHE_ROWS // BLOCK):
                wanted = functools.reduce(
                    jnp.logical_or, seen[b * BLOCK // LIVE : ((b + 1) * BLOCK - 1) // LIVE + 1]
                )
                todo[filled] = n * CHUNK + SPAN_ROWS + b * BLOCK
                filled = filled + jnp.where(wanted, 1, 0)
        for b in range(TILE_BLOCKS - 1):
            todo[filled + b] = spare

        def scores_of(first, rows):
            return lax.dot_general(
                queries[first : first + SUB, :], rows, (((1,), (1,)), ((), ())),
                preferred_element_type=jnp.float32,
            )

        def mix(weights, rows):
            return jnp.dot(weights.astype(jnp.bfloat16), rows, preferred_element_type=jnp.float32)

        def tile(blocks, begin, opening=False):
            spots = [pl.multiple_of(todo[begin + b], BLOCK) for b in range(blocks)]
            key_rows = jnp.concatenate([keys[pl.ds(s, BLOCK), :] for s in spots], 0)
            value_rows = jnp.concatenate([values[pl.ds(s, BLOCK), :] for s in spots], 0)

            def finish(first, scores):
                weights = jnp.exp2(scores * TO_LOG2)
                if opening:
                    token = lax.broadcasted_iota(jnp.int32, (TOK, TOK), 0)
                    key = lax.broadcasted_iota(jnp.int32, (TOK, TOK), 1)
                    own = weights[:, :TOK].reshape(SUB // TOK, TOK, TOK)
                    own = jnp.where((key <= token)[None], own, 0.0).reshape(SUB, TOK)
                    weights = jnp.concatenate([own, weights[:, TOK:]], 1)
                    total_ref[q, first : first + SUB, :] = mix(weights, value_rows)
                else:
                    total_ref[q, first : first + SUB, :] += mix(weights, value_rows)

            held = None
            for first in range(0, ROWS, SUB):
                scores = scores_of(first, key_rows)
                if held is not None:
                    finish(*held)
                held = (first, scores)
            finish(*held)

        begin = 0
        if rows_of[0] == 0:
            tile(TILE_BLOCKS, 0, opening=True)
            begin = TILE_BLOCKS
            filled = jnp.maximum(filled - TILE_BLOCKS, 0)
        else:
            total_ref[q] = carry_ref[q]

        whole = (filled + 1) // TILE_BLOCKS
        rest = filled - whole * TILE_BLOCKS

        def whole_tile(step, _):
            tile(TILE_BLOCKS, begin + step * TILE_BLOCKS)
            return 0

        lax.fori_loop(0, whole, whole_tile, 0)

        @pl.when(rest > 2)
        def _():
            tile(4, begin + whole * TILE_BLOCKS)

        left = jnp.where(rest > 2, rest - 4, rest)

        @pl.when(left > 0)
        def _():
            tile(2, begin + filled - left)

    if last:
        held, top = refs[6:]
        strange = jnp.zeros((TOK, DIM), jnp.float32)

        def write_out(q):
            for h in range(GROUP):
                mixed = total_ref[q, h * TOK : (h + 1) * TOK, :DIM]
                total = total_ref[q, h * TOK : (h + 1) * TOK, DIM:]
                out_refs[q][:, h * DIM : (h + 1) * DIM] = (mixed / total).astype(jnp.bfloat16)

        largest = []
        for q in range(2):
            write_out(q)
            most = jnp.zeros((TOK, DIM), jnp.float32)
            for h in range(GROUP):
                mixed = jnp.abs(total_ref[q, h * TOK : (h + 1) * TOK, :DIM])
                total = total_ref[q, h * TOK : (h + 1) * TOK, DIM:]
                good = (total >= LEAST_TOTAL) & (total <= MOST_TOTAL) & (mixed <= MOST_MIXED)
                strange = jnp.where(good, strange, 1.0)
                most = jnp.maximum(most, mixed)
            largest.append(jnp.max(most))
        fine = (jnp.max(strange) == 0.0) & (largest[0] >= LEAST_MIXED) & (largest[1] >= LEAST_MIXED)

        @pl.when(jnp.logical_not(fine))
        def _():
            for q in range(2):
                mine = 2 * chip + (core if q == 0 else 1 - core)
                careful(q, mine, place, sign, first_open, table_ref, len_ref, last, all_refs,
                        asked.at[q], total_ref, held, top)
                write_out(q)


def careful(q, mine, place, sign, first_open, table_ref, len_ref, parts, all_refs, queries, total_ref, held, top):
    core = place[2]
    total_ref[q] = jnp.zeros((ROWS, 2 * DIM), jnp.float32)
    top[...] = jnp.full((ROWS, DIM), -jnp.inf, jnp.float32)

    def add(keys, values, is_open):
        extent = keys.shape[0]

        def head(h, _):
            rows = pl.ds(pl.multiple_of(h * TOK, TOK), TOK)
            scores = lax.dot_general(
                queries[rows, :], keys, (((1,), (1,)), ((), ())), preferred_element_type=jnp.float32
            ) * (1.0 / math.sqrt(DIM))
            before = top[rows, :]
            highest = jnp.max(jnp.where(is_open, scores, -jnp.inf), -1, keepdims=True)
            after = jnp.maximum(before, highest)
            shift = jnp.where(after == -jnp.inf, 0.0, after)
            factor = jnp.exp(before - shift)
            weights = jnp.exp(jnp.minimum(scores - shift[:, :extent], 0.0))
            weights = jnp.where(is_open, weights, 0.0)
            mixed = jnp.dot(weights.astype(jnp.bfloat16), values, preferred_element_type=jnp.float32)
            total_ref[q, rows, :DIM] = total_ref[q, rows, :DIM] * factor + mixed
            total_ref[q, rows, DIM:] = total_ref[q, rows, DIM:] * factor + jnp.sum(weights, -1, keepdims=True)
            top[rows, :] = after
            return 0

        lax.fori_loop(0, GROUP, head, 0)

    for n, row in enumerate(OFFSETS):
        begin = 0
        for ref, units in zip(all_refs[n], parts[n]):

            def unit(u, _, ref=ref, row=row, begin=begin):
                pltpu.sync_copy(ref.at[u], held)
                k, e = (begin + u) >> 1, (begin + u) & 1
                there = chip_of(place, row, jnp.where(k == 3, 2, jnp.where(k < 2, -k, k - 1) * sign))
                shard = 2 * there + jnp.where(e == 0, core, 1 - core)
                token = lax.broadcasted_iota(jnp.int32, (TOK, TOK), 0)
                key = lax.broadcasted_iota(jnp.int32, (TOK, TOK), 1)
                reach = jnp.where(shard < mine, TOK, jnp.where(shard == mine, 0, -2 * TOK))
                reach = jnp.where(table_ref[mine, shard] == 1, reach, -2 * TOK)
                add(held[0, :TOK, :], held[1, :TOK, :], key <= token + reach)
                slot = lax.broadcasted_iota(jnp.int32, (TOK, LIVE), 1)
                live = (slot >= first_open - shard * SLOTS) & (slot < len_ref[shard])
                add(held[0, TOK:, :], held[1, TOK:, :], live)
                return 0

            lax.fori_loop(0, units, unit, 0)
            begin += units


def stage(rows_of, last, scalars, queries, chunks, carry=None, paired=False):
    smem = pl.BlockSpec(memory_space=pltpu.SMEM)
    vmem = pl.BlockSpec(memory_space=pltpu.VMEM)
    anywhere = pl.BlockSpec(memory_space=pl.ANY)
    operands = list(scalars) + list(queries)
    pieces = []
    for row in rows_of:
        operands += chunks[row]
        pieces.append(tuple(part.shape[0] for part in chunks[row]))
    if carry is not None:
        operands.append(carry)
    specs = [smem] * 3 + [pl.BlockSpec(memory_space=pltpu.HBM)] * 2 + [vmem] * (len(operands) - 5)
    every = None
    if last:
        every = []
        for row in OFFSETS:
            operands += chunks[row]
            every.append(tuple(part.shape[0] for part in chunks[row]))
        every = tuple(every)
    specs += [anywhere] * (len(operands) - len(specs))
    count = len(rows_of)
    total = ((2, ROWS, 2 * DIM), jnp.float32)
    scratch = [
        pltpu.VMEM((count * CHUNK + BLOCK, DIM), jnp.bfloat16),
        pltpu.VMEM((count * CHUNK + BLOCK, 2 * DIM), jnp.bfloat16),
        pltpu.SMEM((count * (PER * 2 + CACHE_ROWS // BLOCK) + TILE_BLOCKS + 1,), jnp.int32),
        pltpu.VMEM((2, ROWS, DIM), jnp.bfloat16),
        pltpu.SemaphoreType.DMA((2,)),
    ]
    if last:
        out_shape = (jax.ShapeDtypeStruct((TOK, GROUP * DIM), jnp.bfloat16),) * 2
        out_specs = (vmem, vmem)
        scratch = [pltpu.VMEM(*total)] + scratch + [
            pltpu.VMEM((2, TOK + LIVE, DIM), jnp.bfloat16),
            pltpu.VMEM((ROWS, DIM), jnp.float32),
        ]
    else:
        out_shape = jax.ShapeDtypeStruct(*total)
        out_specs = vmem
    return pl.pallas_call(
        functools.partial(stage_kernel, tuple(rows_of), tuple(pieces), carry is not None, every, paired),
        out_shape=out_shape,
        in_specs=specs,
        out_specs=out_specs,
        scratch_shapes=scratch,
        compiler_params=pltpu.CompilerParams(vmem_limit_bytes=24 * 1024 * 1024),
        cost_estimate=pl.CostEstimate(
            flops=count * 2 * ROWS * CHUNK * DIM * 6,
            bytes_accessed=count * CHUNK * DIM * 4,
            transcendentals=count * 2 * ROWS * CHUNK,
        ),
        name="stage_" + "_".join(str(r % 4) for r in rows_of),
    )(*operands)


def ordered(value, *after):
    return lax.optimization_barrier((value, after))[0]


def pairs_at(span_ref, cache_ref, head, out):
    columns = pl.ds(pl.multiple_of(head * DIM, DIM), DIM)
    for i in range(2):
        begin = i * (TOK + LIVE)
        out[begin : begin + TOK, :] = span_ref[i, :, columns]
        out[begin + TOK : begin + TOK + LIVE, :] = cache_ref[i, :LIVE, columns]


def queries_at(queries_ref, head, out, at):
    for h in range(GROUP):
        columns = pl.ds(pl.multiple_of((head * GROUP + h) * DIM, DIM), DIM)
        out[at + h * TOK : at + (h + 1) * TOK, :] = queries_ref[:, columns]


def near_kernel(span_ref, cache_ref, queries_ref, own, own_q, pack, same, cross):
    core = own_place()[2]
    for head, out in ((core, own), (1 - core, pack), (2 + core, same), (3 - core, cross)):
        pairs_at(span_ref, cache_ref, head, out)
    queries_at(queries_ref, core, own_q, 0)
    queries_at(queries_ref, 1 - core, pack, PAIR)


def late_kernel(queries_ref, stream_ref, same_q, cross_q, late_stream):
    core = own_place()[2]
    queries_at(queries_ref, core, same_q, 0)
    queries_at(queries_ref, 1 - core, cross_q, 0)
    late_stream[...] = stream_ref[...]


def cut(kernel, operands, specs, shapes):
    whole = lambda shape: pl.BlockSpec(shape, lambda i: (0,) * len(shape))
    return pl.pallas_call(
        kernel,
        grid=(1,),
        out_shape=tuple(jax.ShapeDtypeStruct(shape, jnp.bfloat16) for shape in shapes),
        in_specs=specs,
        out_specs=tuple(whole(shape) for shape in shapes),
        cost_estimate=pl.CostEstimate(flops=0, bytes_accessed=8 * 1024 * 1024, transcendentals=0),
        name=kernel.__name__,
    )(*operands)


def unit_of(first, second):
    return jnp.concatenate([first[:PAIR], second[:PAIR]]).reshape(2, 2, TOK + LIVE, DIM)


def shards(stream, queries, span_kv, cache_kv, cache_len, context_start, block_table):
    core = lax.axis_index("seq") % 2
    scalars = (block_table, cache_len, context_start)
    width = GROUP * DIM

    half = 2 * width
    left = pl.BlockSpec((TOK, half), lambda i: (0, 0))
    right = pl.BlockSpec((TOK, half), lambda i: (0, 1))
    mine, q_mine, theirs, late_same, late_cross = cut(
        near_kernel,
        (span_kv[0], cache_kv[0], queries[0]),
        [pl.BlockSpec((2, TOK, 4 * DIM), lambda i: (0, 0, 0))] * 2 + [left],
        [(PAIR, DIM), (ROWS, DIM), (PAIR + ROWS, DIM)] + [(PAIR, DIM)] * 2,
    )
    received = swapped(theirs)
    near_unit = unit_of(mine, received)
    near_q = (q_mine, received)
    late_queries, late_base = ordered((queries[0], stream[0]), near_unit)
    q_same, q_cross, late_stream = cut(
        late_kernel, (late_queries, late_base), [right, right], [(ROWS, DIM)] * 2 + [(TOK, half)]
    )
    near_pieces = [first_ring(near_unit, -k) for k in OFFSETS[1:]]
    late_parts = (up(late_same), up_swapped(late_cross))
    near_pieces, late_parts, (q_same, q_cross) = lax.optimization_barrier(
        (near_pieces, late_parts, (q_same, q_cross))
    )
    near_row = jnp.concatenate([near_unit] + near_pieces)
    near = {0: [near_row], -1: [second_ring(near_row, 1)], 1: [second_ring(near_row, -1)]}

    late_parts, q_same = ordered((late_parts, q_same), near_row)
    late_unit = unit_of(*late_parts)
    q_same = up(q_same)
    late_mate = first_exchange(late_unit)
    near_sum = stage((0,), False, scalars, ordered(near_q, late_unit), near)
    late_pair = jnp.concatenate([late_unit, ordered(late_mate, near_sum, q_same)])
    late_others = second_exchange(late_pair)
    q_cross = up_swapped(ordered(q_cross, near_sum))
    late_stream = up(ordered(late_stream, near_sum, q_same))
    late_q = (q_same, q_cross)
    near[-1] = ordered(near[-1], near_sum)
    near[2] = [second_ring(near[-1][0], 1)]
    near[1] = ordered(near[1], near_sum)
    late_row = jnp.concatenate([late_pair, ordered(late_others, near[1])])
    late = {0: [late_row], -1: [second_ring(late_row, 1)], 1: [second_ring(late_row, -1)]}
    near_sum = stage((-1, 1), False, scalars, ordered(near_q, late_row), near, near_sum)
    late[1] = ordered(late[1], near_sum)
    late[2] = [second_ring(late[1][0], -1)]
    own, other = stage((2,), True, scalars, ordered(near_q, late[1], late_stream, q_cross), near, near_sum)

    def added(own, other, base):
        received = swapped(other)
        both = jnp.where(
            core == 0, jnp.concatenate([own, received], 1), jnp.concatenate([received, own], 1)
        )
        return (base.astype(jnp.float32) + both.astype(jnp.float32)).astype(jnp.bfloat16)

    near_done = added(own, other, stream[0, :, : 2 * width])
    near_out = up(near_done)
    own, other = stage(OFFSETS, True, scalars, ordered(late_q, near_done, late[2]), late, paired=True)
    other = ordered(other, near_out)
    late_out = added(own, other, late_stream)
    return jnp.concatenate([near_out, late_out], 1)[None]


def solution(mesh):
    return jax.shard_map(
        shards,
        mesh=mesh,
        in_specs=(
            P("section", "seq", None),
            P("section", "seq", None),
            P("section", None, "seq", None),
            P("section", None, "seq", None),
            P(),
            P(),
            P(),
        ),
        out_specs=P("section", "seq", None),
        check_vma=False,
    )
```

```python
import functools
import math

import jax
import jax.numpy as jnp
from jax import lax
from jax.experimental import pallas as pl
from jax.experimental.pallas import tpu as pltpu
from jax.sharding import PartitionSpec as P

DIM = 128
GROUP = 8
TOK = 128
SLOTS = 128
LIVE = 80
SHARDS = 32
CACHE = SLOTS * SHARDS
ROWS = GROUP * TOK
PER = 4
SPAN_ROWS = PER * 2 * TOK
CACHE_ROWS = PER * 2 * LIVE
PAIR = 2 * (TOK + LIVE)
CHUNK = SPAN_ROWS + CACHE_ROWS
BLOCK = 128
TILE_BLOCKS = 8
SUB = 256
OFFSETS = (0, -1, 1, 2)
TO_LOG2 = math.log2(math.e) / math.sqrt(DIM)
LEAST_TOTAL, MOST_TOTAL = 1e-12, 1e30
LEAST_MIXED, MOST_MIXED = 1e-20, 1e37
AXES = ("section", "seq")


def moved(value, rule):
    pairs = []
    for y in range(4):
        for z in range(4):
            for x in range(4):
                for c in range(2):
                    ty, tz, tx, tc = rule(y, z, x, c)
                    source = y * 32 + (z * 4 + x) * 2 + c
                    target = (ty % 4) * 32 + ((tz % 4) * 4 + tx % 4) * 2 + tc
                    pairs.append((source, target))
    return lax.ppermute(value, AXES, pairs)


def swapped(value):
    return moved(value, lambda y, z, x, c: (y, z, x, 1 - c))


def up(value):
    return moved(value, lambda y, z, x, c: (y + 1, z, x, c))


def up_swapped(value):
    return moved(value, lambda y, z, x, c: (y + 1, z, x, 1 - c))


def first_ring(value, k):
    return moved(value, lambda y, z, x, c: (y, z, x + k, c) if c == 0 else (y, z + k, x, c))


def second_ring(value, k):
    return moved(value, lambda y, z, x, c: (y, z + k, x, c) if c == 0 else (y, z, x + k, c))


def own_place():
    seq = lax.axis_index("seq")
    return seq >> 3, (seq >> 1) & 3, seq & 1


def first_exchange(value):
    return moved(value, lambda y, z, x, c: (y, z, x ^ 1, c) if c == 0 else (y, z ^ 1, x, c))


def second_exchange(value):
    return moved(value, lambda y, z, x, c: (y, z, 3 - x, c) if c == 0 else (y, 3 - z, x, c))


def chip_of(place, row, col):
    z, x, c = place
    dz = jnp.where(c == 0, row, col)
    dx = jnp.where(c == 0, col, row)
    return ((z + dz + 4) % 4) * 4 + (x + dx + 4) % 4


def stage_kernel(rows_of, pieces, has_carry, last, paired, *refs):
    refs = list(refs)
    table_ref, len_ref, start_ref = refs[:3]
    q_refs, refs = refs[3:5], refs[5:]
    chunk_refs = []
    for part in pieces:
        chunk_refs.append(refs[: len(part)])
        refs = refs[len(part) :]
    carry_ref = None
    if has_carry:
        carry_ref, refs = refs[0], refs[1:]
    all_refs = []
    if last:
        for part in last:
            all_refs.append(refs[: len(part)])
            refs = refs[len(part) :]
    if last:
        out_refs, refs = refs[:2], refs[2:]
    total_ref, keys, values, todo, asked, arrived = refs[:6]
    count = len(rows_of)
    place = own_place()
    core = place[2]
    chip = place[0] * 4 + place[1]
    first_open = CACHE - start_ref[0]

    sign = 1
    if paired:
        sign = 2 * (jnp.where(core == 0, place[1], place[0]) & 1) - 1

    def shard_at(row, k, e):
        step = OFFSETS[k] * sign if k in (1, 2) else OFFSETS[k]
        return 2 * chip_of(place, row, step) + (core if e == 0 else 1 - core)

    fetches = []
    for q in range(2):
        rows = pl.ds(q_refs[q].shape[0] - ROWS, ROWS)
        fetches.append(pltpu.make_async_copy(q_refs[q].at[rows, :], asked.at[q], arrived.at[q]))
        fetches[q].start()

    for n in range(count):
        base = n * CHUNK
        values[base : base + SPAN_ROWS, DIM:] = jnp.ones((SPAN_ROWS, DIM), jnp.bfloat16)
        i = 0
        for ref, units in zip(chunk_refs[n], pieces[n]):
            for u in range(units):
                spot = base + i * TOK
                keys[spot : spot + TOK, :] = ref[u, 0, :TOK, :]
                values[spot : spot + TOK, :DIM] = ref[u, 1, :TOK, :]
                shard = shard_at(rows_of[n], i // 2, i % 2)
                low = first_open - shard * SLOTS
                slot = lax.broadcasted_iota(jnp.int32, (LIVE, DIM), 0)
                live = (slot >= low) & (slot < len_ref[shard])
                spot = base + SPAN_ROWS + i * LIVE
                keys[spot : spot + LIVE, :] = ref[u, 0, TOK:, :]
                piece = ref[u, 1, TOK:, :].astype(jnp.float32)
                values[spot : spot + LIVE, :DIM] = jnp.where(live, piece, 0.0).astype(jnp.bfloat16)
                values[spot : spot + LIVE, DIM:] = jnp.where(live, 1.0, 0.0).astype(jnp.bfloat16)
                i += 1
    spare = count * CHUNK
    keys[spare : spare + BLOCK, :] = jnp.zeros((BLOCK, DIM), jnp.bfloat16)
    values[spare : spare + BLOCK, :] = jnp.zeros((BLOCK, 2 * DIM), jnp.bfloat16)

    for q in range(2):
        mine = 2 * chip + (core if q == 0 else 1 - core)
        queries = asked.at[q]
        fetches[q].wait()

        filled = jnp.int32(0)
        if rows_of[0] == 0:
            todo[0] = q * TOK
            filled = jnp.int32(1)
        for n in range(count):
            seen = []
            for k in range(PER):
                for e in range(2):
                    shard = shard_at(rows_of[n], k, e)
                    wanted = (shard < mine) & (table_ref[mine, shard] == 1)
                    todo[filled] = n * CHUNK + (2 * k + e) * TOK
                    filled = filled + jnp.where(wanted, 1, 0)
                    seen.append(shard * SLOTS + len_ref[shard] > first_open)
            for b in range(CACHE_ROWS // BLOCK):
                wanted = functools.reduce(
                    jnp.logical_or, seen[b * BLOCK // LIVE : ((b + 1) * BLOCK - 1) // LIVE + 1]
                )
                todo[filled] = n * CHUNK + SPAN_ROWS + b * BLOCK
                filled = filled + jnp.where(wanted, 1, 0)
        for b in range(TILE_BLOCKS - 1):
            todo[filled + b] = spare

        def scores_of(first, rows):
            return lax.dot_general(
                queries[first : first + SUB, :], rows, (((1,), (1,)), ((), ())),
                preferred_element_type=jnp.float32,
            )

        def mix(weights, rows):
            return jnp.dot(weights.astype(jnp.bfloat16), rows, preferred_element_type=jnp.float32)

        def tile(blocks, begin, opening=False):
            spots = [pl.multiple_of(todo[begin + b], BLOCK) for b in range(blocks)]
            key_rows = jnp.concatenate([keys[pl.ds(s, BLOCK), :] for s in spots], 0)
            value_rows = jnp.concatenate([values[pl.ds(s, BLOCK), :] for s in spots], 0)

            def finish(first, scores):
                weights = jnp.exp2(scores * TO_LOG2)
                if opening:
                    token = lax.broadcasted_iota(jnp.int32, (TOK, TOK), 0)
                    key = lax.broadcasted_iota(jnp.int32, (TOK, TOK), 1)
                    own = weights[:, :TOK].reshape(SUB // TOK, TOK, TOK)
                    own = jnp.where((key <= token)[None], own, 0.0).reshape(SUB, TOK)
                    weights = jnp.concatenate([own, weights[:, TOK:]], 1)
                    total_ref[q, first : first + SUB, :] = mix(weights, value_rows)
                else:
                    total_ref[q, first : first + SUB, :] += mix(weights, value_rows)

            held = None
            for first in range(0, ROWS, SUB):
                scores = scores_of(first, key_rows)
                if held is not None:
                    finish(*held)
                held = (first, scores)
            finish(*held)

        begin = 0
        if rows_of[0] == 0:
            tile(TILE_BLOCKS, 0, opening=True)
            begin = TILE_BLOCKS
            filled = jnp.maximum(filled - TILE_BLOCKS, 0)
        else:
            total_ref[q] = carry_ref[q]

        whole = (filled + 1) // TILE_BLOCKS
        rest = filled - whole * TILE_BLOCKS

        def whole_tile(step, _):
            tile(TILE_BLOCKS, begin + step * TILE_BLOCKS)
            return 0

        lax.fori_loop(0, whole, whole_tile, 0)

        @pl.when(rest > 2)
        def _():
            tile(4, begin + whole * TILE_BLOCKS)

        left = jnp.where(rest > 2, rest - 4, rest)

        @pl.when(left > 0)
        def _():
            tile(2, begin + filled - left)

    if last:
        held, top = refs[6:]
        strange = jnp.zeros((TOK, DIM), jnp.float32)

        def write_out(q):
            for h in range(GROUP):
                mixed = total_ref[q, h * TOK : (h + 1) * TOK, :DIM]
                total = total_ref[q, h * TOK : (h + 1) * TOK, DIM:]
                out_refs[q][:, h * DIM : (h + 1) * DIM] = (mixed / total).astype(jnp.bfloat16)

        largest = []
        for q in range(2):
            write_out(q)
            most = jnp.zeros((TOK, DIM), jnp.float32)
            for h in range(GROUP):
                mixed = jnp.abs(total_ref[q, h * TOK : (h + 1) * TOK, :DIM])
                total = total_ref[q, h * TOK : (h + 1) * TOK, DIM:]
                good = (total >= LEAST_TOTAL) & (total <= MOST_TOTAL) & (mixed <= MOST_MIXED)
                strange = jnp.where(good, strange, 1.0)
                most = jnp.maximum(most, mixed)
            largest.append(jnp.max(most))
        fine = (jnp.max(strange) == 0.0) & (largest[0] >= LEAST_MIXED) & (largest[1] >= LEAST_MIXED)

        @pl.when(jnp.logical_not(fine))
        def _():
            for q in range(2):
                mine = 2 * chip + (core if q == 0 else 1 - core)
                careful(q, mine, place, sign, first_open, table_ref, len_ref, last, all_refs,
                        asked.at[q], total_ref, held, top)
                write_out(q)


def careful(q, mine, place, sign, first_open, table_ref, len_ref, parts, all_refs, queries, total_ref, held, top):
    core = place[2]
    total_ref[q] = jnp.zeros((ROWS, 2 * DIM), jnp.float32)
    top[...] = jnp.full((ROWS, DIM), -jnp.inf, jnp.float32)

    def add(keys, values, is_open):
        extent = keys.shape[0]

        def head(h, _):
            rows = pl.ds(pl.multiple_of(h * TOK, TOK), TOK)
            scores = lax.dot_general(
                queries[rows, :], keys, (((1,), (1,)), ((), ())), preferred_element_type=jnp.float32
            ) * (1.0 / math.sqrt(DIM))
            before = top[rows, :]
            highest = jnp.max(jnp.where(is_open, scores, -jnp.inf), -1, keepdims=True)
            after = jnp.maximum(before, highest)
            shift = jnp.where(after == -jnp.inf, 0.0, after)
            factor = jnp.exp(before - shift)
            weights = jnp.exp(jnp.minimum(scores - shift[:, :extent], 0.0))
            weights = jnp.where(is_open, weights, 0.0)
            mixed = jnp.dot(weights.astype(jnp.bfloat16), values, preferred_element_type=jnp.float32)
            total_ref[q, rows, :DIM] = total_ref[q, rows, :DIM] * factor + mixed
            total_ref[q, rows, DIM:] = total_ref[q, rows, DIM:] * factor + jnp.sum(weights, -1, keepdims=True)
            top[rows, :] = after
            return 0

        lax.fori_loop(0, GROUP, head, 0)

    for n, row in enumerate(OFFSETS):
        begin = 0
        for ref, units in zip(all_refs[n], parts[n]):

            def unit(u, _, ref=ref, row=row, begin=begin):
                pltpu.sync_copy(ref.at[u], held)
                k, e = (begin + u) >> 1, (begin + u) & 1
                there = chip_of(place, row, jnp.where(k == 3, 2, jnp.where(k < 2, -k, k - 1) * sign))
                shard = 2 * there + jnp.where(e == 0, core, 1 - core)
                token = lax.broadcasted_iota(jnp.int32, (TOK, TOK), 0)
                key = lax.broadcasted_iota(jnp.int32, (TOK, TOK), 1)
                reach = jnp.where(shard < mine, TOK, jnp.where(shard == mine, 0, -2 * TOK))
                reach = jnp.where(table_ref[mine, shard] == 1, reach, -2 * TOK)
                add(held[0, :TOK, :], held[1, :TOK, :], key <= token + reach)
                slot = lax.broadcasted_iota(jnp.int32, (TOK, LIVE), 1)
                live = (slot >= first_open - shard * SLOTS) & (slot < len_ref[shard])
                add(held[0, TOK:, :], held[1, TOK:, :], live)
                return 0

            lax.fori_loop(0, units, unit, 0)
            begin += units


def stage(rows_of, last, scalars, queries, chunks, carry=None, paired=False):
    smem = pl.BlockSpec(memory_space=pltpu.SMEM)
    vmem = pl.BlockSpec(memory_space=pltpu.VMEM)
    anywhere = pl.BlockSpec(memory_space=pl.ANY)
    operands = list(scalars) + list(queries)
    pieces = []
    for row in rows_of:
        operands += chunks[row]
        pieces.append(tuple(part.shape[0] for part in chunks[row]))
    if carry is not None:
        operands.append(carry)
    specs = [smem] * 3 + [pl.BlockSpec(memory_space=pltpu.HBM)] * 2 + [vmem] * (len(operands) - 5)
    every = None
    if last:
        every = []
        for row in OFFSETS:
            operands += chunks[row]
            every.append(tuple(part.shape[0] for part in chunks[row]))
        every = tuple(every)
    specs += [anywhere] * (len(operands) - len(specs))
    count = len(rows_of)
    total = ((2, ROWS, 2 * DIM), jnp.float32)
    scratch = [
        pltpu.VMEM((count * CHUNK + BLOCK, DIM), jnp.bfloat16),
        pltpu.VMEM((count * CHUNK + BLOCK, 2 * DIM), jnp.bfloat16),
        pltpu.SMEM((count * (PER * 2 + CACHE_ROWS // BLOCK) + TILE_BLOCKS + 1,), jnp.int32),
        pltpu.VMEM((2, ROWS, DIM), jnp.bfloat16),
        pltpu.SemaphoreType.DMA((2,)),
    ]
    if last:
        out_shape = (jax.ShapeDtypeStruct((TOK, GROUP * DIM), jnp.bfloat16),) * 2
        out_specs = (vmem, vmem)
        scratch = [pltpu.VMEM(*total)] + scratch + [
            pltpu.VMEM((2, TOK + LIVE, DIM), jnp.bfloat16),
            pltpu.VMEM((ROWS, DIM), jnp.float32),
        ]
    else:
        out_shape = jax.ShapeDtypeStruct(*total)
        out_specs = vmem
    return pl.pallas_call(
        functools.partial(stage_kernel, tuple(rows_of), tuple(pieces), carry is not None, every, paired),
        out_shape=out_shape,
        in_specs=specs,
        out_specs=out_specs,
        scratch_shapes=scratch,
        compiler_params=pltpu.CompilerParams(vmem_limit_bytes=24 * 1024 * 1024),
        cost_estimate=pl.CostEstimate(
            flops=count * 2 * ROWS * CHUNK * DIM * 6,
            bytes_accessed=count * CHUNK * DIM * 4,
            transcendentals=count * 2 * ROWS * CHUNK,
        ),
        name="stage_" + "_".join(str(r % 4) for r in rows_of),
    )(*operands)


def ordered(value, *after):
    return lax.optimization_barrier((value, after))[0]


def pairs_at(span_ref, cache_ref, head, out):
    columns = pl.ds(pl.multiple_of(head * DIM, DIM), DIM)
    for i in range(2):
        begin = i * (TOK + LIVE)
        out[begin : begin + TOK, :] = span_ref[i, :, columns]
        out[begin + TOK : begin + TOK + LIVE, :] = cache_ref[i, :LIVE, columns]


def queries_at(queries_ref, head, out, at):
    for h in range(GROUP):
        columns = pl.ds(pl.multiple_of((head * GROUP + h) * DIM, DIM), DIM)
        out[at + h * TOK : at + (h + 1) * TOK, :] = queries_ref[:, columns]


def near_kernel(span_ref, cache_ref, queries_ref, own, own_q, pack, same, cross):
    core = own_place()[2]
    for head, out in ((core, own), (1 - core, pack), (2 + core, same), (3 - core, cross)):
        pairs_at(span_ref, cache_ref, head, out)
    queries_at(queries_ref, core, own_q, 0)
    queries_at(queries_ref, 1 - core, pack, PAIR)


def late_kernel(queries_ref, stream_ref, same_q, cross_q, late_stream):
    core = own_place()[2]
    queries_at(queries_ref, core, same_q, 0)
    queries_at(queries_ref, 1 - core, cross_q, 0)
    late_stream[...] = stream_ref[...]


def cut(kernel, operands, specs, shapes):
    whole = lambda shape: pl.BlockSpec(shape, lambda i: (0,) * len(shape))
    return pl.pallas_call(
        kernel,
        grid=(1,),
        out_shape=tuple(jax.ShapeDtypeStruct(shape, jnp.bfloat16) for shape in shapes),
        in_specs=specs,
        out_specs=tuple(whole(shape) for shape in shapes),
        cost_estimate=pl.CostEstimate(flops=0, bytes_accessed=8 * 1024 * 1024, transcendentals=0),
        name=kernel.__name__,
    )(*operands)


def unit_of(first, second):
    return jnp.concatenate([first[:PAIR], second[:PAIR]]).reshape(2, 2, TOK + LIVE, DIM)


def shards(stream, queries, span_kv, cache_kv, cache_len, context_start, block_table):
    core = lax.axis_index("seq") % 2
    scalars = (block_table, cache_len, context_start)
    width = GROUP * DIM

    half = 2 * width
    left = pl.BlockSpec((TOK, half), lambda i: (0, 0))
    right = pl.BlockSpec((TOK, half), lambda i: (0, 1))
    mine, q_mine, theirs, late_same, late_cross = cut(
        near_kernel,
        (span_kv[0], cache_kv[0], queries[0]),
        [pl.BlockSpec((2, TOK, 4 * DIM), lambda i: (0, 0, 0))] * 2 + [left],
        [(PAIR, DIM), (ROWS, DIM), (PAIR + ROWS, DIM)] + [(PAIR, DIM)] * 2,
    )
    received = swapped(theirs)
    near_unit = unit_of(mine, received)
    near_q = (q_mine, received)
    late_queries, late_base = ordered((queries[0], stream[0]), near_unit)
    q_same, q_cross, late_stream = cut(
        late_kernel, (late_queries, late_base), [right, right], [(ROWS, DIM)] * 2 + [(TOK, half)]
    )
    near_pieces = [first_ring(near_unit, -k) for k in OFFSETS[1:]]
    late_parts = (up(late_same), up_swapped(late_cross))
    near_pieces, late_parts, (q_same, q_cross) = lax.optimization_barrier(
        (near_pieces, late_parts, (q_same, q_cross))
    )
    near_row = jnp.concatenate([near_unit] + near_pieces)
    near = {0: [near_row], -1: [second_ring(near_row, 1)], 1: [second_ring(near_row, -1)]}

    late_parts, q_same = ordered((late_parts, q_same), near_row)
    late_unit = unit_of(*late_parts)
    q_same = up(q_same)
    late_mate = first_exchange(late_unit)
    near_sum = stage((0,), False, scalars, ordered(near_q, late_unit), near)
    late_pair = jnp.concatenate([late_unit, ordered(late_mate, near_sum)])
    late_others = second_exchange(late_pair)
    q_cross = up_swapped(ordered(q_cross, near_sum))
    late_stream = up(ordered(late_stream, near_sum, q_same))
    late_q = (q_same, q_cross)
    near[-1] = ordered(near[-1], near_sum)
    near[2] = [second_ring(near[-1][0], 1)]
    near_sum = stage((-1, 1), False, scalars, ordered(near_q, late_pair, q_same), near, near_sum)
    late_row = jnp.concatenate([late_pair, ordered(late_others, near_sum, q_cross)])
    late = {0: [late_row], -1: [second_ring(late_row, 1)], 1: [second_ring(late_row, -1)]}
    own, other = stage((2,), True, scalars, ordered(near_q, late_row, q_cross), near, near_sum)

    def added(own, other, base):
        received = swapped(other)
        both = jnp.where(
            core == 0, jnp.concatenate([own, received], 1), jnp.concatenate([received, own], 1)
        )
        return (base.astype(jnp.float32) + both.astype(jnp.float32)).astype(jnp.bfloat16)

    own, late_stream, late[-1] = lax.optimization_barrier((own, late_stream, late[-1]))
    near_done = added(own, other, stream[0, :, : 2 * width])
    near_out = up(near_done)
    late[1] = ordered(late[1], near_done)
    late[2] = [second_ring(late[1][0], -1)]
    late_sum = stage((0, -1, 1), False, ordered(scalars, near_done), late_q, late, paired=True)
    late_sum, near_out = lax.optimization_barrier((late_sum, near_out))
    own, other = stage((2,), True, scalars, late_q, late, late_sum, paired=True)
    late_out = added(own, other, late_stream)
    return jnp.concatenate([near_out, late_out], 1)[None]


def solution(mesh):
    return jax.shard_map(
        shards,
        mesh=mesh,
        in_specs=(
            P("section", "seq", None),
            P("section", "seq", None),
            P("section", None, "seq", None),
            P("section", None, "seq", None),
            P(),
            P(),
            P(),
        ),
        out_specs=P("section", "seq", None),
        check_vma=False,
    )
```

```python
import functools
import math

import jax
import jax.numpy as jnp
from jax import lax
from jax.experimental import pallas as pl
from jax.experimental.pallas import tpu as pltpu
from jax.sharding import PartitionSpec as P

DIM = 128
GROUP = 8
TOK = 128
SLOTS = 128
LIVE = 80
SHARDS = 32
CACHE = SLOTS * SHARDS
ROWS = GROUP * TOK
PER = 4
SPAN_ROWS = PER * 2 * TOK
CACHE_ROWS = PER * 2 * LIVE
PAIR = 2 * (TOK + LIVE)
CHUNK = SPAN_ROWS + CACHE_ROWS
BLOCK = 128
TILE_BLOCKS = 16
OPENING = 8
SUB = 256
OFFSETS = (0, -1, 1, 2)
TO_LOG2 = math.log2(math.e) / math.sqrt(DIM)
LEAST_TOTAL, MOST_TOTAL = 1e-12, 1e30
LEAST_MIXED, MOST_MIXED = 1e-20, 1e37
AXES = ("section", "seq")


def moved(value, rule):
    pairs = []
    for y in range(4):
        for z in range(4):
            for x in range(4):
                for c in range(2):
                    ty, tz, tx, tc = rule(y, z, x, c)
                    source = y * 32 + (z * 4 + x) * 2 + c
                    target = (ty % 4) * 32 + ((tz % 4) * 4 + tx % 4) * 2 + tc
                    pairs.append((source, target))
    return lax.ppermute(value, AXES, pairs)


def swapped(value):
    return moved(value, lambda y, z, x, c: (y, z, x, 1 - c))


def up(value):
    return moved(value, lambda y, z, x, c: (y + 1, z, x, c))


def up_swapped(value):
    return moved(value, lambda y, z, x, c: (y + 1, z, x, 1 - c))


def first_ring(value, k):
    return moved(value, lambda y, z, x, c: (y, z, x + k, c) if c == 0 else (y, z + k, x, c))


def second_ring(value, k):
    return moved(value, lambda y, z, x, c: (y, z + k, x, c) if c == 0 else (y, z, x + k, c))


def own_place():
    seq = lax.axis_index("seq")
    return seq >> 3, (seq >> 1) & 3, seq & 1


def first_exchange(value):
    return moved(value, lambda y, z, x, c: (y, z, x ^ 1, c) if c == 0 else (y, z ^ 1, x, c))


def second_exchange(value):
    return moved(value, lambda y, z, x, c: (y, z, 3 - x, c) if c == 0 else (y, 3 - z, x, c))


def chip_of(place, row, col):
    z, x, c = place
    dz = jnp.where(c == 0, row, col)
    dx = jnp.where(c == 0, col, row)
    return ((z + dz + 4) % 4) * 4 + (x + dx + 4) % 4


def stage_kernel(rows_of, pieces, has_carry, last, paired, *refs):
    refs = list(refs)
    table_ref, len_ref, start_ref = refs[:3]
    q_refs, refs = refs[3:5], refs[5:]
    chunk_refs = []
    for part in pieces:
        chunk_refs.append(refs[: len(part)])
        refs = refs[len(part) :]
    carry_ref = None
    if has_carry:
        carry_ref, refs = refs[0], refs[1:]
    all_refs = []
    if last:
        for part in last:
            all_refs.append(refs[: len(part)])
            refs = refs[len(part) :]
    if last:
        out_refs, refs = refs[:2], refs[2:]
    total_ref, keys, values, todo, asked, arrived = refs[:6]
    count = len(rows_of)
    place = own_place()
    core = place[2]
    chip = place[0] * 4 + place[1]
    first_open = CACHE - start_ref[0]

    sign = 1
    if paired:
        sign = 2 * (jnp.where(core == 0, place[1], place[0]) & 1) - 1

    def shard_at(row, k, e):
        step = OFFSETS[k] * sign if k in (1, 2) else OFFSETS[k]
        return 2 * chip_of(place, row, step) + (core if e == 0 else 1 - core)

    fetches = []
    for q in range(2):
        rows = pl.ds(q_refs[q].shape[0] - ROWS, ROWS)
        fetches.append(pltpu.make_async_copy(q_refs[q].at[rows, :], asked.at[q], arrived.at[q]))
        fetches[q].start()

    for n in range(count):
        base = n * CHUNK
        values[base : base + SPAN_ROWS, DIM:] = jnp.ones((SPAN_ROWS, DIM), jnp.bfloat16)
        i = 0
        for ref, units in zip(chunk_refs[n], pieces[n]):
            for u in range(units):
                spot = base + i * TOK
                keys[spot : spot + TOK, :] = ref[u, 0, :TOK, :]
                values[spot : spot + TOK, :DIM] = ref[u, 1, :TOK, :]
                shard = shard_at(rows_of[n], i // 2, i % 2)
                low = first_open - shard * SLOTS
                slot = lax.broadcasted_iota(jnp.int32, (LIVE, DIM), 0)
                live = (slot >= low) & (slot < len_ref[shard])
                spot = base + SPAN_ROWS + i * LIVE
                keys[spot : spot + LIVE, :] = ref[u, 0, TOK:, :]
                piece = ref[u, 1, TOK:, :].astype(jnp.float32)
                values[spot : spot + LIVE, :DIM] = jnp.where(live, piece, 0.0).astype(jnp.bfloat16)
                values[spot : spot + LIVE, DIM:] = jnp.where(live, 1.0, 0.0).astype(jnp.bfloat16)
                i += 1
    spare = count * CHUNK
    keys[spare : spare + BLOCK, :] = jnp.zeros((BLOCK, DIM), jnp.bfloat16)
    values[spare : spare + BLOCK, :] = jnp.zeros((BLOCK, 2 * DIM), jnp.bfloat16)

    for q in range(2):
        mine = 2 * chip + (core if q == 0 else 1 - core)
        queries = asked.at[q]
        fetches[q].wait()

        filled = jnp.int32(0)
        if rows_of[0] == 0:
            todo[0] = q * TOK
            filled = jnp.int32(1)
        for n in range(count):
            seen = []
            for k in range(PER):
                for e in range(2):
                    shard = shard_at(rows_of[n], k, e)
                    wanted = (shard < mine) & (table_ref[mine, shard] == 1)
                    todo[filled] = n * CHUNK + (2 * k + e) * TOK
                    filled = filled + jnp.where(wanted, 1, 0)
                    seen.append(shard * SLOTS + len_ref[shard] > first_open)
            for b in range(CACHE_ROWS // BLOCK):
                wanted = functools.reduce(
                    jnp.logical_or, seen[b * BLOCK // LIVE : ((b + 1) * BLOCK - 1) // LIVE + 1]
                )
                todo[filled] = n * CHUNK + SPAN_ROWS + b * BLOCK
                filled = filled + jnp.where(wanted, 1, 0)
        for b in range(TILE_BLOCKS - 1):
            todo[filled + b] = spare

        def scores_of(first, rows):
            return lax.dot_general(
                queries[first : first + SUB, :], rows, (((1,), (1,)), ((), ())),
                preferred_element_type=jnp.float32,
            )

        def mix(weights, rows):
            return jnp.dot(weights.astype(jnp.bfloat16), rows, preferred_element_type=jnp.float32)

        def tile(blocks, begin, opening=False):
            spots = [pl.multiple_of(todo[begin + b], BLOCK) for b in range(blocks)]
            key_rows = jnp.concatenate([keys[pl.ds(s, BLOCK), :] for s in spots], 0)
            value_rows = jnp.concatenate([values[pl.ds(s, BLOCK), :] for s in spots], 0)

            def finish(first, scores):
                weights = jnp.exp2(scores * TO_LOG2)
                if opening:
                    token = lax.broadcasted_iota(jnp.int32, (TOK, TOK), 0)
                    key = lax.broadcasted_iota(jnp.int32, (TOK, TOK), 1)
                    own = weights[:, :TOK].reshape(SUB // TOK, TOK, TOK)
                    own = jnp.where((key <= token)[None], own, 0.0).reshape(SUB, TOK)
                    weights = jnp.concatenate([own, weights[:, TOK:]], 1)
                    total_ref[q, first : first + SUB, :] = mix(weights, value_rows)
                else:
                    total_ref[q, first : first + SUB, :] += mix(weights, value_rows)

            held = None
            for first in range(0, ROWS, SUB):
                scores = scores_of(first, key_rows)
                if held is not None:
                    finish(*held)
                held = (first, scores)
            finish(*held)

        begin = 0
        if rows_of[0] == 0:
            tile(OPENING, 0, opening=True)
            begin = OPENING
            filled = jnp.maximum(filled - OPENING, 0)
        else:
            total_ref[q] = carry_ref[q]

        whole = (filled + 1) // TILE_BLOCKS
        rest = filled - whole * TILE_BLOCKS

        def whole_tile(step, _):
            tile(TILE_BLOCKS, begin + step * TILE_BLOCKS)
            return 0

        lax.fori_loop(0, whole, whole_tile, 0)

        done = begin + whole * TILE_BLOCKS

        @pl.when(rest > 6)
        def _():
            tile(8, done)

        done = jnp.where(rest > 6, done + 8, done)
        rest = jnp.where(rest > 6, rest - 8, rest)

        @pl.when(rest > 2)
        def _():
            tile(4, done)

        left = jnp.where(rest > 2, rest - 4, rest)

        @pl.when(left > 0)
        def _():
            tile(2, begin + filled - left)

    if last:
        held, top = refs[6:]
        strange = jnp.zeros((TOK, DIM), jnp.float32)

        def write_out(q):
            for h in range(GROUP):
                mixed = total_ref[q, h * TOK : (h + 1) * TOK, :DIM]
                total = total_ref[q, h * TOK : (h + 1) * TOK, DIM:]
                out_refs[q][:, h * DIM : (h + 1) * DIM] = (mixed / total).astype(jnp.bfloat16)

        largest = []
        for q in range(2):
            write_out(q)
            most = jnp.zeros((TOK, DIM), jnp.float32)
            for h in range(GROUP):
                mixed = jnp.abs(total_ref[q, h * TOK : (h + 1) * TOK, :DIM])
                total = total_ref[q, h * TOK : (h + 1) * TOK, DIM:]
                good = (total >= LEAST_TOTAL) & (total <= MOST_TOTAL) & (mixed <= MOST_MIXED)
                strange = jnp.where(good, strange, 1.0)
                most = jnp.maximum(most, mixed)
            largest.append(jnp.max(most))
        fine = (jnp.max(strange) == 0.0) & (largest[0] >= LEAST_MIXED) & (largest[1] >= LEAST_MIXED)

        @pl.when(jnp.logical_not(fine))
        def _():
            for q in range(2):
                mine = 2 * chip + (core if q == 0 else 1 - core)
                careful(q, mine, place, sign, first_open, table_ref, len_ref, last, all_refs,
                        asked.at[q], total_ref, held, top)
                write_out(q)


def careful(q, mine, place, sign, first_open, table_ref, len_ref, parts, all_refs, queries, total_ref, held, top):
    core = place[2]
    total_ref[q] = jnp.zeros((ROWS, 2 * DIM), jnp.float32)
    top[...] = jnp.full((ROWS, DIM), -jnp.inf, jnp.float32)

    def add(keys, values, is_open):
        extent = keys.shape[0]

        def head(h, _):
            rows = pl.ds(pl.multiple_of(h * TOK, TOK), TOK)
            scores = lax.dot_general(
                queries[rows, :], keys, (((1,), (1,)), ((), ())), preferred_element_type=jnp.float32
            ) * (1.0 / math.sqrt(DIM))
            before = top[rows, :]
            highest = jnp.max(jnp.where(is_open, scores, -jnp.inf), -1, keepdims=True)
            after = jnp.maximum(before, highest)
            shift = jnp.where(after == -jnp.inf, 0.0, after)
            factor = jnp.exp(before - shift)
            weights = jnp.exp(jnp.minimum(scores - shift[:, :extent], 0.0))
            weights = jnp.where(is_open, weights, 0.0)
            mixed = jnp.dot(weights.astype(jnp.bfloat16), values, preferred_element_type=jnp.float32)
            total_ref[q, rows, :DIM] = total_ref[q, rows, :DIM] * factor + mixed
            total_ref[q, rows, DIM:] = total_ref[q, rows, DIM:] * factor + jnp.sum(weights, -1, keepdims=True)
            top[rows, :] = after
            return 0

        lax.fori_loop(0, GROUP, head, 0)

    for n, row in enumerate(OFFSETS):
        begin = 0
        for ref, units in zip(all_refs[n], parts[n]):

            def unit(u, _, ref=ref, row=row, begin=begin):
                pltpu.sync_copy(ref.at[u], held)
                k, e = (begin + u) >> 1, (begin + u) & 1
                there = chip_of(place, row, jnp.where(k == 3, 2, jnp.where(k < 2, -k, k - 1) * sign))
                shard = 2 * there + jnp.where(e == 0, core, 1 - core)
                token = lax.broadcasted_iota(jnp.int32, (TOK, TOK), 0)
                key = lax.broadcasted_iota(jnp.int32, (TOK, TOK), 1)
                reach = jnp.where(shard < mine, TOK, jnp.where(shard == mine, 0, -2 * TOK))
                reach = jnp.where(table_ref[mine, shard] == 1, reach, -2 * TOK)
                add(held[0, :TOK, :], held[1, :TOK, :], key <= token + reach)
                slot = lax.broadcasted_iota(jnp.int32, (TOK, LIVE), 1)
                live = (slot >= first_open - shard * SLOTS) & (slot < len_ref[shard])
                add(held[0, TOK:, :], held[1, TOK:, :], live)
                return 0

            lax.fori_loop(0, units, unit, 0)
            begin += units


def stage(rows_of, last, scalars, queries, chunks, carry=None, paired=False):
    smem = pl.BlockSpec(memory_space=pltpu.SMEM)
    vmem = pl.BlockSpec(memory_space=pltpu.VMEM)
    anywhere = pl.BlockSpec(memory_space=pl.ANY)
    operands = list(scalars) + list(queries)
    pieces = []
    for row in rows_of:
        operands += chunks[row]
        pieces.append(tuple(part.shape[0] for part in chunks[row]))
    if carry is not None:
        operands.append(carry)
    specs = [smem] * 3 + [pl.BlockSpec(memory_space=pltpu.HBM)] * 2 + [vmem] * (len(operands) - 5)
    every = None
    if last:
        every = []
        for row in OFFSETS:
            operands += chunks[row]
            every.append(tuple(part.shape[0] for part in chunks[row]))
        every = tuple(every)
    specs += [anywhere] * (len(operands) - len(specs))
    count = len(rows_of)
    total = ((2, ROWS, 2 * DIM), jnp.float32)
    scratch = [
        pltpu.VMEM((count * CHUNK + BLOCK, DIM), jnp.bfloat16),
        pltpu.VMEM((count * CHUNK + BLOCK, 2 * DIM), jnp.bfloat16),
        pltpu.SMEM((count * (PER * 2 + CACHE_ROWS // BLOCK) + TILE_BLOCKS + 1,), jnp.int32),
        pltpu.VMEM((2, ROWS, DIM), jnp.bfloat16),
        pltpu.SemaphoreType.DMA((2,)),
    ]
    if last:
        out_shape = (jax.ShapeDtypeStruct((TOK, GROUP * DIM), jnp.bfloat16),) * 2
        out_specs = (vmem, vmem)
        scratch = [pltpu.VMEM(*total)] + scratch + [
            pltpu.VMEM((2, TOK + LIVE, DIM), jnp.bfloat16),
            pltpu.VMEM((ROWS, DIM), jnp.float32),
        ]
    else:
        out_shape = jax.ShapeDtypeStruct(*total)
        out_specs = vmem
    return pl.pallas_call(
        functools.partial(stage_kernel, tuple(rows_of), tuple(pieces), carry is not None, every, paired),
        out_shape=out_shape,
        in_specs=specs,
        out_specs=out_specs,
        scratch_shapes=scratch,
        compiler_params=pltpu.CompilerParams(vmem_limit_bytes=24 * 1024 * 1024),
        cost_estimate=pl.CostEstimate(
            flops=count * 2 * ROWS * CHUNK * DIM * 6,
            bytes_accessed=count * CHUNK * DIM * 4,
            transcendentals=count * 2 * ROWS * CHUNK,
        ),
        name="stage_" + "_".join(str(r % 4) for r in rows_of),
    )(*operands)


def ordered(value, *after):
    return lax.optimization_barrier((value, after))[0]


def pairs_at(span_ref, cache_ref, head, out):
    columns = pl.ds(pl.multiple_of(head * DIM, DIM), DIM)
    for i in range(2):
        begin = i * (TOK + LIVE)
        out[begin : begin + TOK, :] = span_ref[i, :, columns]
        out[begin + TOK : begin + TOK + LIVE, :] = cache_ref[i, :LIVE, columns]


def queries_at(queries_ref, head, out, at):
    for h in range(GROUP):
        columns = pl.ds(pl.multiple_of((head * GROUP + h) * DIM, DIM), DIM)
        out[at + h * TOK : at + (h + 1) * TOK, :] = queries_ref[:, columns]


def near_kernel(span_ref, cache_ref, queries_ref, own, own_q, pack, same, cross):
    core = own_place()[2]
    for head, out in ((core, own), (1 - core, pack), (2 + core, same), (3 - core, cross)):
        pairs_at(span_ref, cache_ref, head, out)
    queries_at(queries_ref, core, own_q, 0)
    queries_at(queries_ref, 1 - core, pack, PAIR)


def late_kernel(queries_ref, stream_ref, same_q, cross_q, late_stream):
    core = own_place()[2]
    queries_at(queries_ref, core, same_q, 0)
    queries_at(queries_ref, 1 - core, cross_q, 0)
    late_stream[...] = stream_ref[...]


def cut(kernel, operands, specs, shapes):
    whole = lambda shape: pl.BlockSpec(shape, lambda i: (0,) * len(shape))
    return pl.pallas_call(
        kernel,
        grid=(1,),
        out_shape=tuple(jax.ShapeDtypeStruct(shape, jnp.bfloat16) for shape in shapes),
        in_specs=specs,
        out_specs=tuple(whole(shape) for shape in shapes),
        cost_estimate=pl.CostEstimate(flops=0, bytes_accessed=8 * 1024 * 1024, transcendentals=0),
        name=kernel.__name__,
    )(*operands)


def unit_of(first, second):
    return jnp.concatenate([first[:PAIR], second[:PAIR]]).reshape(2, 2, TOK + LIVE, DIM)


def shards(stream, queries, span_kv, cache_kv, cache_len, context_start, block_table):
    core = lax.axis_index("seq") % 2
    scalars = (block_table, cache_len, context_start)
    width = GROUP * DIM

    half = 2 * width
    left = pl.BlockSpec((TOK, half), lambda i: (0, 0))
    right = pl.BlockSpec((TOK, half), lambda i: (0, 1))
    mine, q_mine, theirs, late_same, late_cross = cut(
        near_kernel,
        (span_kv[0], cache_kv[0], queries[0]),
        [pl.BlockSpec((2, TOK, 4 * DIM), lambda i: (0, 0, 0))] * 2 + [left],
        [(PAIR, DIM), (ROWS, DIM), (PAIR + ROWS, DIM)] + [(PAIR, DIM)] * 2,
    )
    received = swapped(theirs)
    near_unit = unit_of(mine, received)
    near_q = (q_mine, received)
    late_queries, late_base = ordered((queries[0], stream[0]), near_unit)
    q_same, q_cross, late_stream = cut(
        late_kernel, (late_queries, late_base), [right, right], [(ROWS, DIM)] * 2 + [(TOK, half)]
    )
    near_pieces = [first_ring(near_unit, -k) for k in OFFSETS[1:]]
    late_parts = (up(late_same), up_swapped(late_cross))
    near_pieces, late_parts, (q_same, q_cross) = lax.optimization_barrier(
        (near_pieces, late_parts, (q_same, q_cross))
    )
    near_row = jnp.concatenate([near_unit] + near_pieces)
    near = {0: [near_row], -1: [second_ring(near_row, 1)], 1: [second_ring(near_row, -1)]}

    late_parts, q_same = ordered((late_parts, q_same), near_row)
    late_unit = unit_of(*late_parts)
    q_same = up(q_same)
    late_mate = first_exchange(late_unit)
    near_sum = stage((0,), False, scalars, ordered(near_q, late_unit), near)
    late_pair = jnp.concatenate([late_unit, ordered(late_mate, near_sum)])
    late_others = second_exchange(late_pair)
    q_cross = up_swapped(ordered(q_cross, near_sum))
    late_stream = up(ordered(late_stream, near_sum, q_same))
    late_q = (q_same, q_cross)
    near[-1] = ordered(near[-1], near_sum)
    near[2] = [second_ring(near[-1][0], 1)]
    near_sum = stage((-1, 1), False, scalars, ordered(near_q, late_pair, q_same), near, near_sum)
    late_row = jnp.concatenate([late_pair, ordered(late_others, near_sum, q_cross)])
    late = {0: [late_row], -1: [second_ring(late_row, 1)], 1: [second_ring(late_row, -1)]}
    own, other = stage((2,), True, scalars, ordered(near_q, late_row, late_stream, q_cross), near, near_sum)
    late[1] = ordered(late[1], own)
    late[2] = [second_ring(late[1][0], -1)]

    def added(own, other, base):
        received = swapped(other)
        both = jnp.where(
            core == 0, jnp.concatenate([own, received], 1), jnp.concatenate([received, own], 1)
        )
        return (base.astype(jnp.float32) + both.astype(jnp.float32)).astype(jnp.bfloat16)

    near_done = added(own, other, stream[0, :, : 2 * width])
    near_out = up(near_done)
    late_sum = stage((0, -1, 1), False, ordered(scalars, near_done), late_q, late, paired=True)
    late_sum, near_out = lax.optimization_barrier((late_sum, near_out))
    own, other = stage((2,), True, scalars, late_q, late, late_sum, paired=True)
    late_out = added(own, other, late_stream)
    return jnp.concatenate([near_out, late_out], 1)[None]


def solution(mesh):
    return jax.shard_map(
        shards,
        mesh=mesh,
        in_specs=(
            P("section", "seq", None),
            P("section", "seq", None),
            P("section", None, "seq", None),
            P("section", None, "seq", None),
            P(),
            P(),
            P(),
        ),
        out_specs=P("section", "seq", None),
        check_vma=False,
    )
```
